32 devices in a mesh: ctx: 16 (over z, y, x), head: 2 (over core).
Axes of the slice: x: 2, y: 2, z: 4, core: 2. Of those that a mesh axis runs over, the one named last changes fastest.
Arguments:
- queries: bfloat16 [2048, 4096], P('ctx', 'head'), may hold values from -45 to 45
- kv_rows: bfloat16 [2048, 512], P('ctx'), may hold values from -6 to 6
- doc_start: int32 [64], replicated, may hold values from 0 to 2016, as said below
- destination: int32 [64], replicated, may hold values from 0 to 63, as said below
- out_weight: bfloat16 [4096, 2048], P('head'), may hold values from -0.5 to 0.5
Outputs:
- mixed: bfloat16 [2048, 2048], P('head', 'ctx')
The draws below stay inside these ranges and needn't reach their ends.
Inputs may be any that keep to these rules, and one draw needn't show every extreme that they name: Documents are runs of whole blocks: doc_start[b] is a multiple of 32, at most b * 32, never falls from block to block, and equals b * 32 where a document begins; doc_start[0] = 0. `destination`: A permutation of 0 .. 63 that maps every aligned group of 16 consecutive blocks onto itself.
All inputs are finite; a program needn't handle non-finite values.
Results may differ from the reference program's by a relative error of at most 0.011.
Values may be sent and summed in bfloat16 or wider, within the bound.
No kernel may reach another device: no remote copies, remote signals or barrier semaphores. Data moves between devices by JAX's collectives and lax.ppermute only.
A program may use at most 64 MiB of HBM per device.

```python
import jax
import jax.numpy as jnp
import numpy as np
from jax import lax

D = 2048
HEADS = 32
DH = 128
W1 = 512
W2 = 32
QB = 32
HOPS = 3
TOK_DEV = 128
TOKENS = 2048


def joint_draw(key):
    keys_all = jax.random.split(jax.random.fold_in(key, 7), 2)
    kv_values = jnp.clip(jax.random.normal(keys_all[0], (TOKENS, 4 * DH), jnp.float32), -6.0, 6.0)
    query_values = 2.5 * jnp.clip(jax.random.normal(keys_all[1], (TOKENS, HEADS * DH), jnp.float32), -6.0, 6.0)
    return (query_values, kv_values)


def draw_queries(key, part):
    return joint_draw(key)[0].astype(jnp.bfloat16)


def draw_kv_rows(key, part):
    return joint_draw(key)[1].astype(jnp.bfloat16)


def document_draw(key):
    block_total = TOKENS // QB
    begins = jax.random.randint(jax.random.fold_in(key, 11), (block_total,), 0, 16) == 0
    begins = begins.at[0].set(True)
    begins = begins.at[-1].set(True)
    marked = jnp.where(begins, jnp.arange(block_total, dtype=jnp.int32), 0)
    return (lax.cummax(marked, axis=0) * QB).astype(jnp.int32)


def draw_doc_start(key, part):
    return document_draw(key)


def draw_destination(key, part):
    starts = document_draw(key)
    block_total = TOKENS // QB
    per_device = TOK_DEV // QB
    group_devices = HOPS + 1
    group_size = group_devices * per_device
    group_total = block_total // group_size
    block_ids = jnp.arange(block_total, dtype=jnp.int32)
    loads = jnp.minimum(block_ids * QB - starts, W1).astype(jnp.int32)
    local_ids = (block_ids % group_size).astype(jnp.int32)
    scores = (loads * group_size + local_ids).reshape(group_total, group_size)
    order = jnp.argsort(-scores, axis=1, stable=True).astype(jnp.int32)
    ranks = jnp.arange(group_size, dtype=jnp.int32)
    rounds = ranks // group_devices
    within = ranks % group_devices
    device_of = jnp.where(rounds % 2 == 0, within, group_devices - 1 - within)
    slot_of = (device_of * per_device + rounds).astype(jnp.int32)
    local_dest = jnp.zeros((group_total, group_size), jnp.int32)
    row_ids = jnp.arange(group_total, dtype=jnp.int32)[:, None]
    local_dest = local_dest.at[row_ids, order].set(jnp.broadcast_to(slot_of[None, :], (group_total, group_size)))
    offsets = (jnp.arange(group_total, dtype=jnp.int32) * group_size)[:, None]
    return (local_dest + offsets).reshape(-1).astype(jnp.int32)


def spiked(values, key, source, target, blocks, factor):
    def block_of(axis_at):
        return (jnp.arange(values.shape[axis_at]) // (values.shape[axis_at] // blocks)).reshape((-1,) + (1,) * (values.ndim - 1 - axis_at))

    near = jax.random.permutation(key, blocks)[block_of(target)]
    other_side = (block_of(target) + blocks // 2) % blocks
    return jnp.where((block_of(source) == near) | (block_of(source) == other_side), factor * values, values)


def shard_levels(key, dims, pieces, low, high):
    def one(position, parts):
        steps = jax.random.uniform(jax.random.fold_in(jax.random.fold_in(key, 6), position), (parts,), jnp.float32, low / len(pieces), high / len(pieces))
        return jnp.repeat(jnp.exp(steps), dims[position] // parts).reshape((-1,) + (1,) * (len(dims) - position - 1))

    gain = one(*pieces[0])
    for cut in pieces[1:]:
        gain = gain * one(*cut)
    return gain


def noise_with(rng, dims, deviation, limit, shards, heavy, held_as=jnp.bfloat16):
    values = deviation * jax.random.normal(rng, dims, jnp.float32)
    if shards:
        values = values * shard_levels(rng, dims, shards, -0.22, 0.18)
    return jnp.clip(spiked(values, jax.random.fold_in(rng, 3), *heavy), -limit, limit).astype(held_as)


def setup_inputs(seed: int = 0) -> dict:
    key_of = jax.random.split(jax.random.key(seed), 6)
    return {
        "queries": draw_queries(jax.random.fold_in(key_of[5], 71), 0),
        "kv_rows": draw_kv_rows(jax.random.fold_in(key_of[5], 71), 0),
        "doc_start": draw_doc_start(jax.random.fold_in(key_of[5], 71), 0),
        "destination": draw_destination(jax.random.fold_in(key_of[5], 71), 0),
        "out_weight": noise_with(key_of[4], (HEADS * DH, D), (HEADS * DH // 16) ** -0.5, 0.5, ((0, 2),), (0, 1, 2, 2.0)),
    }


def reference(queries, kv_rows, doc_start, destination, out_weight):
    logit_scale = DH ** -0.5
    padded = jnp.concatenate([jnp.zeros((W1, 4 * DH), kv_rows.dtype), kv_rows], axis=0)
    block_total = TOKENS // QB
    index_grid = np.arange(QB)[:, None] + np.arange(W2)[None, :]
    column_ids = jnp.arange(QB * W2, dtype=jnp.int32)

    def one_block(block_id):
        first_row = block_id * QB
        doc_first = doc_start[block_id]
        window_rows = lax.dynamic_slice_in_dim(padded, first_row, W1 + QB, 0)
        near_rows = lax.dynamic_slice_in_dim(padded, first_row + W1 - W2 + 1, QB + W2 - 1, 0)
        keys_first = window_rows[:, :DH]
        values_first = window_rows[:, DH:2 * DH]
        keys_second = near_rows[:, 2 * DH:3 * DH][index_grid]
        values_second = near_rows[:, 3 * DH:][index_grid]
        query_pos = first_row + column_ids // W2
        second_pos = query_pos - W2 + 1 + column_ids % W2
        key_pos = first_row - W1 + jnp.arange(W1 + QB, dtype=jnp.int32)
        allowed = (key_pos[:, None] >= doc_first) & (key_pos[:, None] <= query_pos[None, :])
        allowed = allowed & (key_pos[:, None] > query_pos[None, :] - W1) & (second_pos[None, :] >= doc_first)
        block_queries = lax.dynamic_slice_in_dim(queries, first_row, QB, 0)
        per_head = block_queries.reshape(QB, HEADS, DH).transpose(1, 0, 2)

        def one_head(head_query):
            paired = (head_query[:, None, :].astype(jnp.float32) * keys_second.astype(jnp.float32)).astype(jnp.bfloat16)
            paired = paired.reshape(QB * W2, DH)
            logits = lax.dot_general(keys_first, paired, (((1,), (1,)), ((), ())), preferred_element_type=jnp.float32) * logit_scale
            logits = jnp.where(allowed, logits, jnp.full(logits.shape, -jnp.inf, jnp.float32))
            peak = logits.max(0).reshape(QB, W2).max(1)
            weights = jnp.exp(logits - jnp.repeat(peak, W2)[None, :])
            totals = weights.sum(0).reshape(QB, W2).sum(1)
            rounded = weights.astype(jnp.bfloat16)
            mixed_first = lax.dot_general(rounded, values_first, (((0,), (0,)), ((), ())), preferred_element_type=jnp.float32)
            result = (mixed_first.reshape(QB, W2, DH) * values_second.astype(jnp.float32)).sum(1) / totals[:, None]
            return result.astype(jnp.bfloat16)

        outputs = lax.map(one_head, per_head)
        return outputs.transpose(1, 0, 2).reshape(QB, HEADS * DH)

    attended = lax.map(one_block, jnp.arange(block_total, dtype=jnp.int32)).reshape(TOKENS, HEADS * DH)
    projected = jnp.dot(attended, out_weight, preferred_element_type=jnp.float32).astype(jnp.bfloat16)
    placed = jnp.zeros((block_total, QB, D), projected.dtype).at[destination].set(projected.reshape(block_total, QB, D))
    return placed.reshape(TOKENS, D).T
```

```python
import functools
import jax, jax.numpy as jnp, numpy as np
from jax import lax
from jax.experimental import pallas as pl
from jax.experimental.pallas import tpu as pltpu
from jax.sharding import PartitionSpec as P

DH=128; W1=512; W2=32; QB=32
HG=4
ROWS=W1+QB
VR=DH+16
CH=2
NCH=W2//CH
LOG2E=1.4426950408889634

def att_kernel(inval_ref, q_ref, kv_ref, e_ref, out_ref, k1x, v1t, v2e, k2f, qs, sbuf, acc):
    b=pl.program_id(0); g=pl.program_id(1)
    lanes=HG*QB
    @pl.when(g==0)
    def _():
        inv=inval_ref[b]
        start=pl.multiple_of(b*QB,QB)
        k1=kv_ref[pl.ds(start,ROWS),0:DH].astype(jnp.float32)
        row=lax.broadcasted_iota(jnp.int32,(ROWS,DH),0)
        ok=row>=inv
        k1x[...]=jnp.where(ok,k1,k1[W1:W1+1,:]).astype(jnp.bfloat16)
        v1=kv_ref[pl.ds(start,ROWS),DH:2*DH].astype(jnp.float32)
        v1=jnp.where(ok,v1,0.0)
        v1t[0:DH,:]=v1.T.astype(jnp.bfloat16)
        v1t[DH:,:]=(lax.broadcasted_iota(jnp.int32,(VR-DH,ROWS),1)>=inv).astype(jnp.float32).astype(jnp.bfloat16)
        k2=kv_ref[pl.ds(start+W1-W2,2*QB),2*DH:3*DH].astype(jnp.float32)
        v2=kv_ref[pl.ds(start+W1-W2,2*QB),3*DH:4*DH].astype(jnp.float32)
        row2=lax.broadcasted_iota(jnp.int32,(2*QB,DH),0)
        ok2=(inv<W1)|(row2>=W2)
        k2f[...]=jnp.where(ok2,k2,k2[W2:W2+1,:])
        v2=jnp.where(ok2,v2,0.0)
        v2x=jnp.concatenate([v2.T,(lax.broadcasted_iota(jnp.int32,(VR-DH,2*QB),1)>=jnp.where(inv<W1,0,W2)).astype(jnp.float32)],axis=0).astype(jnp.bfloat16)
        for c in range(NCH):
            v2e[c]=jnp.dot(v2x,e_ref[:,c*CH*lanes:(c+1)*CH*lanes],preferred_element_type=jnp.float32)
    scale=LOG2E/np.sqrt(DH)
    for h in range(HG):
        qs[h*QB:(h+1)*QB,:]=q_ref[:,h*DH:(h+1)*DH].astype(jnp.float32)*scale
    tri=lax.broadcasted_iota(jnp.int32,(QB,CH*lanes),0)<=(lax.broadcasted_iota(jnp.int32,(QB,CH*lanes),1)%QB)

    def qk(c,slot):
        ps=[]
        for u in range(CH):
            k2=k2f[pl.ds(c*CH+u+1,QB),:]
            ps.append((qs[...].reshape(HG,QB,DH)*k2[None]).reshape(lanes,DH).astype(jnp.bfloat16))
        paired=jnp.concatenate(ps,axis=0)
        L=lax.dot_general(k1x[...],paired,(((1,),(1,)),((),())),preferred_element_type=jnp.float32)
        comb=jnp.where(tri,L[W1:],L[:QB])
        sbuf[slot,0:QB]=comb
        sbuf[slot,QB:]=L[QB:W1]
        cm=jnp.maximum(jnp.max(comb,axis=0,keepdims=True),jnp.max(L[QB:W1],axis=0,keepdims=True))
        r=cm[:,0:lanes]
        for u in range(1,CH): r=jnp.maximum(r,cm[:,u*lanes:(u+1)*lanes])
        return r

    def pv(c,slot,m_old,m_new):
        mm=jnp.concatenate([m_new]*CH,axis=1)
        p=jnp.exp2(sbuf[slot]-mm).astype(jnp.bfloat16)
        zero=jnp.zeros((QB,CH*lanes),jnp.bfloat16)
        pf=jnp.concatenate([jnp.where(tri,zero,p[:QB]),p[QB:],jnp.where(tri,p[:QB],zero)],axis=0)
        O=jnp.dot(v1t[...],pf,preferred_element_type=jnp.float32)
        w=O*v2e[c]
        r=w[:,0:lanes]
        for u in range(1,CH): r=r+w[:,u*lanes:(u+1)*lanes]
        acc[...]=acc[...]*jnp.exp2(m_old-m_new)+r

    acc[...]=jnp.zeros_like(acc)
    m0=qk(0,0)
    def step(t,carry):
        m_old,m_new=carry
        c=t*2
        m1=jnp.maximum(m_new,qk(c+1,1))
        pv(c,0,m_old,m_new)
        m2=jnp.maximum(m1,qk(jnp.minimum(c+2,NCH-1),0))
        pv(c+1,1,m_new,m1)
        return m1,m2
    lax.fori_loop(0,NCH//2,step,(m0,m0))
    a=acc[0:DH,:]/acc[DH:DH+1,:]
    lane=lax.broadcasted_iota(jnp.int32,(DH,lanes),1)//QB
    for h in range(HG):
        r=pltpu.roll(a,(b-h+HG)%HG*QB,1)
        i=pl.multiple_of((g*HG+h)*DH,DH)
        prev=out_ref[pl.ds(i,DH),:]
        out_ref[pl.ds(i,DH),:]=jnp.where(lane==b,r.astype(jnp.float32),prev.astype(jnp.float32)).astype(jnp.bfloat16)

def spread():
    lanes=HG*QB
    col=np.arange(W2*lanes); m=col//lanes; i=col%QB
    return (np.arange(2*QB)[:,None]==(i+m+1)[None,:])

def attention(queries, stacked, inval):
    T,HD=queries.shape
    nb=T//QB; ng=HD//(HG*DH)
    lanes=HG*QB
    E=jnp.asarray(spread(),jnp.bfloat16)
    full=lambda s: pl.BlockSpec(s,lambda b,g:(0,)*len(s))
    return pl.pallas_call(
        att_kernel,
        out_shape=jax.ShapeDtypeStruct((HD,T),jnp.bfloat16),
        grid=(nb,ng),
        in_specs=[pl.BlockSpec(memory_space=pltpu.SMEM),
                  pl.BlockSpec((QB,HG*DH),lambda b,g:(b,g)),
                  full(stacked.shape),full(E.shape)],
        out_specs=full((HD,T)),
        scratch_shapes=[pltpu.VMEM((ROWS,DH),jnp.bfloat16),pltpu.VMEM((VR,ROWS),jnp.bfloat16),
            pltpu.VMEM((NCH,VR,CH*lanes),jnp.float32),pltpu.VMEM((2*QB,DH),jnp.float32),
            pltpu.VMEM((lanes,DH),jnp.float32),pltpu.VMEM((2,W1,CH*lanes),jnp.float32),pltpu.VMEM((VR,lanes),jnp.float32)],
        compiler_params=pltpu.CompilerParams(vmem_limit_bytes=48*2**20),
    )(inval,queries,stacked,E)

HOPS = 3


def shifted(block, axis, distance):
    devices = range(lax.axis_size(axis))
    return lax.ppermute(block, axis, [(i - distance, i) for i in devices if i - distance in devices])


def rotated(block, axis, group, distance):
    devices = range(lax.axis_size(axis))
    return lax.ppermute(
        block, axis, [(i, i - i % group + (i % group + distance) % group) for i in devices]
    )


def collect_window(kv_rows, shards_back):
    held = kv_rows
    shard = kv_rows.shape[0]
    count = 1
    while count < shards_back + 1:
        number = min(count, shards_back + 1 - count)
        incoming = shifted(held[-number * shard :], "ctx", count)
        held = jnp.concatenate([incoming, held], axis=0)
        count += number
    return held


def body(queries, kv_rows, doc_start, destination, out_weight):
    position = lax.axis_index("ctx")
    tokens = queries.shape[0]
    blocks = tokens // QB
    group = HOPS + 1
    back = W1 // tokens
    stacked = collect_window(kv_rows, back)
    mine = position * blocks + jnp.arange(blocks, dtype=jnp.int32)
    inval = jnp.clip(doc_start[mine] - (mine * QB - W1), 0, W1).astype(jnp.int32)
    attended = attention(queries, stacked, inval)
    partial = lax.dot_general(
        out_weight, attended, (((0,), (0,)), ((), ())), preferred_element_type=jnp.float32
    )
    summed = lax.psum_scatter(partial, "head", scatter_dimension=0, tiled=True).astype(jnp.bfloat16)
    pieces = [summed] + [rotated(summed, "ctx", group, r) for r in range(1, group)]
    token = jnp.arange(tokens, dtype=jnp.int32)
    slots = mine[token // QB] * QB + token % QB
    picks = []
    for r in range(group):
        owner = position - position % group + (position % group - r + group) % group
        target = destination[owner * blocks + token // QB] * QB + token % QB
        picks.append(target[:, None] == slots[None, :])
    pick = jnp.concatenate(picks, axis=0).astype(jnp.bfloat16)
    return jnp.dot(
        jnp.concatenate(pieces, axis=1), pick, preferred_element_type=jnp.float32
    ).astype(jnp.bfloat16)


def solution(mesh):
    in_specs = (P("ctx", "head"), P("ctx", None), P(), P(), P("head", None))
    return jax.shard_map(
        body, mesh=mesh, in_specs=in_specs, out_specs=P("head", "ctx"), check_vma=False
    )
```

```python
import jax
import jax.numpy as jnp
import numpy as np
from jax import lax
from jax.experimental import pallas as pl
from jax.experimental.pallas import tpu as pltpu
from jax.sharding import PartitionSpec as P

DH = 128
W1 = 512
W2 = 32
QB = 32
LANES = 128
PACK = 16
VR = DH + PACK
UNROLL = 8
LOG2E = 1.4426950408889634


def attention_kernel(inval_ref, q_ref, kv_ref, out_ref, k1n, k1s, v1t, v1n, k2x, v2x, rowid, laneid, q3, sbuf, peak, part, top2, att, rows):
    tokens = q_ref.shape[0]
    heads = q_ref.shape[1] // DH
    cols = W2 * heads
    per_tile = LANES // heads
    tiles = tokens // LANES
    near_tiles = cols // LANES
    size = max(heads, PACK)
    per_pack = size // heads
    scale = LOG2E / np.sqrt(DH)
    f32, bf16 = jnp.float32, jnp.bfloat16

    def iota(shape, dim):
        return lax.broadcasted_iota(jnp.int32, shape, dim)

    for h in range(heads):
        q3[pl.ds(h, tokens, stride=heads), :] = q_ref[:, h * DH : (h + 1) * DH].astype(f32)
    second = kv_ref[W1 - W2 :, 2 * DH : 3 * DH].astype(f32)
    second = jnp.broadcast_to(second[:, None, :], (tokens + W2, heads, DH))
    k2x[...] = second.reshape(k2x.shape).astype(bf16)
    k1n[...] = kv_ref[W1:, :DH]
    rowid[...] = iota(rowid.shape, 0).astype(f32).astype(bf16)
    laneid[...] = iota(laneid.shape, 1).astype(f32).astype(bf16)
    for k in range(tiles):
        own = kv_ref[W1 + k * LANES : W1 + (k + 1) * LANES, DH : 2 * DH]
        v1n[k, :DH] = own.astype(f32).T.astype(bf16)
        v1n[k, DH:] = jnp.ones((VR - DH, LANES), bf16)
    near = LANES + tokens
    v2t = kv_ref[W1 - LANES :, 3 * DH :].astype(f32).T
    v2t = jnp.concatenate([v2t, jnp.ones((VR - DH, near), f32)], axis=0).astype(bf16)
    first = LANES - W2
    for k in range((tokens + W2) // per_tile):
        pick = iota((near, LANES), 0) == first + k * per_tile + iota((near, LANES), 1) // heads
        v2x[k] = jnp.dot(v2t, pick.astype(f32).astype(bf16), preferred_element_type=f32)

    def reset(t, inv):
        kt = kv_ref[pl.ds(pl.multiple_of(W1 + t, PACK), PACK), :].astype(f32)[:1]
        window = kv_ref[:W1, : 2 * DH].astype(f32)
        ok = iota((W1, DH), 0) >= inv
        k1s[...] = jnp.where(ok, window[:, :DH], kt[:, :DH]).astype(bf16)
        values = jnp.where(ok, window[:, DH:], 0.0)
        for k in range(W1 // LANES):
            v1t[k, :DH] = values[k * LANES : (k + 1) * LANES].T.astype(bf16)
            live = k * LANES + iota((VR - DH, LANES), 1) >= inv
            v1t[k, DH:] = live.astype(f32).astype(bf16)
        k1n[...] = jnp.where(iota((tokens, DH), 0) < t, kt[:, :DH], k1n[...].astype(f32)).astype(bf16)
        for k in range(tiles):
            gone = k * LANES + iota((VR, LANES), 1) < t
            v1n[k] = jnp.where(gone, 0.0, v1n[k].astype(f32)).astype(bf16)

        @pl.when(inv == W1)
        def _():
            pack0 = t // per_pack
            fill = jnp.broadcast_to(kt[:, 2 * DH : 3 * DH], (size, DH)).astype(bf16)
            for s in range(W2 // per_pack):
                k2x[pack0 + s] = fill
            for k in range(near_tiles):
                v2x[t // per_tile + k] = jnp.zeros((VR, LANES), f32)

    def score(t, slot):
        mark = t.astype(f32).astype(bf16)
        keys = [
            jnp.where(rowid[...] + (k * LANES) <= mark, k1n[k * LANES : (k + 1) * LANES], k1s[k * LANES : (k + 1) * LANES])
            for k in range(tiles)
        ]
        keys = jnp.concatenate(keys + [k1s[tokens:]], axis=0)
        query = q3[pl.ds(t * heads, heads), :]
        if heads < PACK:
            query = jnp.concatenate([query] * per_pack, axis=0)
        query = query.astype(bf16)
        here = t % W2
        base = (t - here) // per_pack
        wide = min(2 * LANES, cols)
        best = None
        for n in range(0, cols, wide):
            paired = []
            for s in range(n // size, (n + wide) // size):
                if heads >= PACK:
                    near_keys = k2x[base + s + jnp.where(s <= here, W2, 0)]
                else:
                    token = s * per_pack + iota((size, DH), 0) // heads
                    after = k2x[base + s + W2 // per_pack].astype(f32)
                    near_keys = jnp.where(token <= here, after, k2x[base + s].astype(f32)).astype(bf16)
                paired.append(near_keys * query)
            paired = jnp.concatenate(paired, axis=0)
            logits = lax.dot_general(
                keys, paired, (((1,), (1,)), ((), ())), preferred_element_type=f32
            )
            sbuf[slot, :, n : n + wide] = logits
            top = jnp.max(logits, axis=0, keepdims=True)
            for u in range(0, wide, LANES):
                some = top[:, u : u + LANES]
                best = some if best is None else jnp.maximum(best, some)
        peak[slot] = jnp.broadcast_to(best * scale, (8, LANES))

    def mix(t, slot):
        mark = t.astype(f32).astype(bf16)
        values = [
            jnp.where(laneid[...] + (k * LANES) <= mark, v1n[k], v1t[k]) for k in range(tiles)
        ] + [v1t[k] for k in range(tiles, W1 // LANES)]
        here = t % W2
        base = (t - here) // per_tile
        place = iota((VR, LANES), 1) // heads
        top = peak[slot][:1]
        wide = min(2 * LANES, cols)
        total = jnp.zeros((VR, LANES), f32)
        for n in range(0, cols, wide):
            product = jnp.zeros((VR, wide), f32)
            for k in range(0, W1, 2 * LANES):
                some = sbuf[slot, k : k + 2 * LANES, n : n + wide]
                weights = jnp.exp2(some * scale - jnp.concatenate([top] * (wide // LANES), axis=1))
                two = jnp.concatenate(values[k // LANES : k // LANES + 2], axis=1)
                product = product + jnp.dot(two, weights.astype(bf16), preferred_element_type=f32)
            for u in range(0, wide, LANES):
                k = (n + u) // LANES
                second = jnp.where(
                    place + k * per_tile <= here, v2x[base + near_tiles + k], v2x[base + k]
                )
                total = total + product[:, u : u + LANES] * second
        part[slot] = total
        top2[slot] = peak[slot]

    def finish(t, slot):
        lane = iota((DH, LANES), 1)
        top = top2[slot]
        best = top
        shift = LANES // 2
        while shift >= heads:
            best = jnp.maximum(best, pltpu.roll(best, shift, 1))
            shift //= 2
        total = part[slot] * jnp.exp2(top - best)[:1]
        shift = LANES // 2
        while shift >= heads:
            total = total + pltpu.roll(total, shift, 1)
            shift //= 2
        value = total[:DH] * (1.0 / total[DH : DH + 1])
        tile = t // per_tile
        att[tile] = jnp.where(lane // heads == t % per_tile, value, att[tile])

    def block(b, _):
        inv = inval_ref[b]
        t0 = b * QB

        @pl.when((b == 0) | (inv == W1))
        def _():
            reset(t0, inv)
            score(t0, 0)

        def several(s, _):
            t = t0 + UNROLL * s
            for u in range(UNROLL):
                score(jnp.minimum(t + u + 1, tokens - 1), (u + 1) % 2)
                mix(t + u, u % 2)
                finish(jnp.maximum(t + u - 1, 0), (u + 1) % 2)
            return 0

        return lax.fori_loop(0, QB // UNROLL, several, 0)

    lax.fori_loop(0, tokens // QB, block, 0)
    finish(tokens - 1, (tokens - 1) % 2)
    for k in range(tokens // per_tile):
        rows[k * LANES : (k + 1) * LANES, :] = att[k].T
    for h in range(heads):
        out_ref[:, h * DH : (h + 1) * DH] = rows[pl.ds(h, tokens, stride=heads), :].astype(bf16)


def attention(queries, stacked, inval):
    tokens, width = queries.shape
    heads = width // DH
    cols = W2 * heads
    f32, bf16 = jnp.float32, jnp.bfloat16
    return pl.pallas_call(
        attention_kernel,
        out_shape=jax.ShapeDtypeStruct((tokens, width), bf16),
        in_specs=[
            pl.BlockSpec(memory_space=pltpu.SMEM),
            pl.BlockSpec(memory_space=pltpu.VMEM),
            pl.BlockSpec(memory_space=pltpu.VMEM),
        ],
        out_specs=pl.BlockSpec(memory_space=pltpu.VMEM),
        scratch_shapes=[
            pltpu.VMEM((tokens, DH), bf16),
            pltpu.VMEM((W1, DH), bf16),
            pltpu.VMEM((W1 // LANES, VR, LANES), bf16),
            pltpu.VMEM((tokens // LANES, VR, LANES), bf16),
            pltpu.VMEM(((tokens + W2) * heads // max(heads, PACK), max(heads, PACK), DH), bf16),
            pltpu.VMEM(((tokens + W2) * heads // LANES, VR, LANES), f32),
            pltpu.VMEM((LANES, DH), bf16),
            pltpu.VMEM((VR, LANES), bf16),
            pltpu.VMEM((tokens * heads, DH), f32),
            pltpu.VMEM((2, W1, cols), f32),
            pltpu.VMEM((2, 8, LANES), f32),
            pltpu.VMEM((2, VR, LANES), f32),
            pltpu.VMEM((2, 8, LANES), f32),
            pltpu.VMEM((tokens * heads // LANES, DH, LANES), f32),
            pltpu.VMEM((tokens * heads, DH), f32),
        ],
        compiler_params=pltpu.CompilerParams(vmem_limit_bytes=24 * 2**20),
    )(inval, queries, stacked)

HOPS = 3


def shifted(block, axis, distance):
    devices = range(lax.axis_size(axis))
    return lax.ppermute(block, axis, [(i - distance, i) for i in devices if i - distance in devices])


def swapped(block, axis, bits):
    return lax.ppermute(block, axis, [(i, i ^ bits) for i in range(lax.axis_size(axis))])


def summed_over_heads(partial):
    count = lax.axis_size("head")
    width = partial.shape[1] // count
    if count != 2:
        return lax.psum_scatter(partial, "head", scatter_dimension=1, tiled=True)
    here = lax.axis_index("head")
    theirs = lax.dynamic_slice_in_dim(partial, (1 - here) * width, width, 1)
    mine = lax.dynamic_slice_in_dim(partial, here * width, width, 1)
    return mine + swapped(theirs, "head", 1)


def body(queries, kv_rows, doc_start, destination, out_weight):
    position = lax.axis_index("ctx")
    tokens = queries.shape[0]
    blocks = tokens // QB
    group = HOPS + 1
    back = W1 // tokens
    stacked = jnp.concatenate(
        [shifted(kv_rows, "ctx", back - k) for k in range(back)] + [kv_rows], axis=0
    )
    first = position * blocks
    starts = lax.dynamic_slice_in_dim(doc_start, first, blocks, 0)
    own_rows = (first + jnp.arange(blocks, dtype=jnp.int32)) * QB
    inval = jnp.clip(starts - (own_rows - W1), 0, W1).astype(jnp.int32)
    place = position % group
    slots = group * blocks
    targets = lax.dynamic_slice_in_dim(destination, first - place * blocks, slots, 0)
    row = jnp.arange(group * tokens, dtype=jnp.int32)
    source = (place ^ (row // tokens)) * blocks + row % tokens // QB
    known = source[:, None] == jnp.arange(slots, dtype=jnp.int32)[None, :]
    target = jnp.sum(jnp.where(known, targets[None, :], 0), axis=1) * QB + row % QB
    pick = target[:, None] == (first * QB + jnp.arange(tokens, dtype=jnp.int32))[None, :]
    pick = pick.astype(jnp.bfloat16)
    attended = attention(queries, stacked, inval)
    partial = jnp.dot(attended, out_weight, preferred_element_type=jnp.float32)
    projected = summed_over_heads(partial).astype(jnp.bfloat16)
    pieces = jnp.concatenate(
        [projected] + [swapped(projected, "ctx", r) for r in range(1, group)], axis=0
    )
    return lax.dot_general(
        pieces, pick, (((0,), (0,)), ((), ())), preferred_element_type=jnp.float32
    ).astype(jnp.bfloat16)


def solution(mesh):
    in_specs = (P("ctx", "head"), P("ctx", None), P(), P(), P("head", None))
    return jax.shard_map(
        body, mesh=mesh, in_specs=in_specs, out_specs=P("head", "ctx"), check_vma=False
    )
```

```python
import functools

import jax
import jax.numpy as jnp
import numpy as np
from jax import lax
from jax.experimental import pallas as pl
from jax.experimental.pallas import tpu as pltpu
from jax.sharding import PartitionSpec as P

DH = 128
W1 = 512
W2 = 32
QB = 32
LANES = 128
PACK = 16
VR = DH + PACK
SAMPLE = 32
AHEAD = 3
LIMIT = 1e30
LOG2E = 1.4426950408889634


def attention_kernel(pairs, outputs, meta_ref, q_ref, w_ref, *refs):
    shards, refs = refs[:pairs], refs[pairs:]
    out_refs, refs = refs[:outputs], refs[outputs:]
    kv_ref, wbuf, wsem, k1n, k1s, v1t, v1n, k2x, v2x, rowid, laneid, q3, part, top2, bad, rows = refs
    tokens = q_ref.shape[0]
    heads = q_ref.shape[1] // DH
    cols = W2 * heads
    group = LANES // heads
    tiles = tokens // LANES
    near_tiles = cols // LANES
    size = max(heads, PACK)
    pack = size // heads
    wide = min(2 * LANES, cols)
    scale = LOG2E / np.sqrt(DH)
    f32, bf16 = jnp.float32, jnp.bfloat16

    def iota(shape, dim):
        return lax.broadcasted_iota(jnp.int32, shape, dim)

    def either(cond, a, b):
        if isinstance(cond, bool):
            return a if cond else b
        return jnp.where(cond, a, b)

    weight_copy = pltpu.make_async_copy(w_ref, wbuf, wsem)
    weight_copy.start()
    blocks = tokens // QB
    here = meta_ref[blocks]

    def lay(order):
        at = 0
        for ref in order:
            kv_ref[at : at + ref.shape[0], :] = ref[...]
            at += ref.shape[0]

    if outputs == 2:

        @pl.when(here == 0)
        def _():
            lay((shards[1], shards[0], shards[2]))

        @pl.when(here != 0)
        def _():
            lay(shards)

    else:
        lay(shards)

    def prepare():
        for h in range(heads):
            q3[pl.ds(h, tokens, stride=heads), :] = q_ref[:, h * DH : (h + 1) * DH].astype(f32)
        second = kv_ref[W1 - W2 :, 2 * DH : 3 * DH].astype(f32)
        second = jnp.broadcast_to(second[:, None, :], (tokens + W2, heads, DH))
        k2x[...] = second.reshape(k2x.shape).astype(bf16)
        k1n[...] = kv_ref[W1:, :DH]
        rowid[...] = iota(rowid.shape, 0).astype(f32).astype(bf16)
        laneid[...] = iota(laneid.shape, 1).astype(f32).astype(bf16)
        bad[...] = jnp.zeros_like(bad)
        for k in range(tiles):
            own = kv_ref[W1 + k * LANES : W1 + (k + 1) * LANES, DH : 2 * DH]
            v1n[k, :DH] = own.astype(f32).T.astype(bf16)
            v1n[k, DH:] = jnp.ones((VR - DH, LANES), bf16)
        near = LANES + tokens
        v2t = kv_ref[W1 - LANES :, 3 * DH :].astype(f32).T
        v2t = jnp.concatenate([v2t, jnp.ones((VR - DH, near), f32)], axis=0).astype(bf16)
        first = LANES - W2
        for k in range((tokens + W2) // group):
            pick = iota((near, LANES), 0) == first + k * group + iota((near, LANES), 1) // heads
            v2x[k] = jnp.dot(v2t, pick.astype(f32).astype(bf16), preferred_element_type=f32)

    def reset(t, inv):
        kt = kv_ref[pl.ds(pl.multiple_of(W1 + t, PACK), PACK), :].astype(f32)[:1]
        window = kv_ref[:W1, : 2 * DH].astype(f32)
        ok = iota((W1, DH), 0) >= inv
        k1s[...] = jnp.where(ok, window[:, :DH], kt[:, :DH]).astype(bf16)
        values = jnp.where(ok, window[:, DH:], 0.0)
        for k in range(W1 // LANES):
            v1t[k, :DH] = values[k * LANES : (k + 1) * LANES].T.astype(bf16)
            live = k * LANES + iota((VR - DH, LANES), 1) >= inv
            v1t[k, DH:] = live.astype(f32).astype(bf16)
        k1n[...] = jnp.where(iota((tokens, DH), 0) < t, kt[:, :DH], k1n[...].astype(f32)).astype(bf16)
        for k in range(tiles):
            gone = k * LANES + iota((VR, LANES), 1) < t
            v1n[k] = jnp.where(gone, 0.0, v1n[k].astype(f32)).astype(bf16)

        @pl.when(inv == W1)
        def _():
            fill = jnp.broadcast_to(kt[:, 2 * DH : 3 * DH], (size, DH)).astype(bf16)
            for s in range(W2 // pack):
                k2x[t // pack + s] = fill
            for k in range(near_tiles):
                v2x[t // group + k] = jnp.zeros((VR, LANES), f32)

    def scores(g, u):
        t = g * group + u
        mark = t.astype(f32).astype(bf16)
        keys = [
            jnp.where(rowid[...] + (k * LANES) <= mark, k1n[k * LANES : (k + 1) * LANES], k1s[k * LANES : (k + 1) * LANES])
            for k in range(tiles)
        ]
        keys = jnp.concatenate(keys + [k1s[tokens:]], axis=0)
        query = q3[pl.ds(t * heads, heads), :]
        if heads < PACK:
            query = jnp.concatenate([query] * pack, axis=0)
        query = query.astype(bf16)
        base = g * (group // pack)
        for n in range(0, cols, wide):
            paired = []
            for s in range(n // size, (n + wide) // size):
                if s * pack >= group:
                    near_keys = k2x[base + s]
                elif pack == 1:
                    near_keys = k2x[base + either(s <= u, s + W2, s)]
                else:
                    token = s * pack + iota((size, DH), 0) // heads
                    after = k2x[base + s + W2 // pack].astype(f32)
                    near_keys = jnp.where(token <= u, after, k2x[base + s].astype(f32)).astype(bf16)
                paired.append(near_keys * query)
            yield lax.dot_general(
                keys,
                jnp.concatenate(paired, axis=0),
                (((1,), (1,)), ((), ())),
                preferred_element_type=f32,
            )

    def highest(logits, best=None):
        top = jnp.max(logits, axis=0, keepdims=True)
        for k in range(0, wide, LANES):
            some = top[:, k : k + LANES]
            best = some if best is None else jnp.maximum(best, some)
        return best

    def mix(g, u, n, logits, top):
        mark = (g * group + u).astype(f32).astype(bf16)
        values = [
            jnp.where(laneid[...] + (k * LANES) <= mark, v1n[k], v1t[k]) for k in range(tiles)
        ] + [v1t[k] for k in range(tiles, W1 // LANES)]
        tops = jnp.concatenate([top] * (wide // LANES), axis=1)
        product = None
        for k in range(0, W1, 2 * LANES):
            weights = jnp.exp2(logits[k : k + 2 * LANES] * scale - tops).astype(bf16)
            two = jnp.concatenate(values[k // LANES : k // LANES + 2], axis=1)
            some = jnp.dot(two, weights, preferred_element_type=f32)
            product = some if product is None else product + some
        total = None
        for c in range(0, wide, LANES):
            k = (n + c) // LANES
            near = v2x[g + k]
            if k == 0:
                near = jnp.where(iota((VR, LANES), 1) // heads <= u, v2x[g + near_tiles], near)
            some = product[:, c : c + LANES] * near
            total = some if total is None else total + some
        return total

    def keep(g, u, total, top):
        part[g * group + u] = total
        top2[g * group + u] = jnp.broadcast_to(top, (8, LANES))
        bad[...] = jnp.where(total[DH : DH + 8] < LIMIT, bad[...], 1.0)

    def finish(g):
        lane = iota((VR, LANES), 1)
        sums = []
        for u in range(group):
            top = top2[g * group + u]
            best = top
            shift = LANES // 2
            while shift >= heads:
                best = jnp.maximum(best, pltpu.roll(best, shift, 1))
                shift //= 2
            sums.append(part[g * group + u] * jnp.exp2(top - best)[:1])
        shift = heads
        while shift < LANES:
            low = lane % (2 * shift) < shift
            sums = [
                jnp.where(low, a, b) + pltpu.roll(jnp.where(low, b, a), shift, 1)
                for a, b in zip(sums[::2], sums[1::2])
            ]
            shift *= 2
        value = sums[0][:DH] * (1.0 / sums[0][DH : DH + 1])
        rows[pl.ds(pl.multiple_of(g * LANES, LANES), LANES), :] = value.T

    def run(exact):
        prepare()

        def block(b, _):
            inv = meta_ref[b]
            g0 = b * (QB // group)

            @pl.when((b == 0) | (inv == W1))
            def _():
                reset(b * QB, inv)

            def fast(s, _):
                g = g0 + s
                work = []
                for u in range(group):
                    work += [(u, n) for n in range(0, cols, wide)]
                source = {u: scores(g, u) for u in range(group)}
                top = total = None
                ahead = [next(source[u]) for u, n in work[:AHEAD]]
                for i, (u, n) in enumerate(work):
                    if i + AHEAD < len(work):
                        ahead.append(next(source[work[i + AHEAD][0]]))
                    logits = ahead.pop(0)
                    if n == 0:
                        top = highest(logits[:SAMPLE]) * scale
                        total = None
                    some = mix(g, u, n, logits, top)
                    total = some if total is None else total + some
                    if n + wide == cols:
                        keep(g, u, total, top)
                    if i == 0:
                        finish(jnp.maximum(g - 1, 0))
                return 0

            def slow(s, _):
                g, u = g0 + s // group, s % group
                best = None
                for logits in scores(g, u):
                    best = highest(logits, best)
                total = None
                for n, logits in zip(range(0, cols, wide), scores(g, u)):
                    some = mix(g, u, n, logits, best * scale)
                    total = some if total is None else total + some
                keep(g, u, total, best * scale)
                return 0

            if exact:
                return lax.fori_loop(0, QB, slow, 0)
            return lax.fori_loop(0, QB // group, fast, 0)

        lax.fori_loop(0, tokens // QB, block, 0)
        if exact:
            lax.fori_loop(0, tokens // group - 1, lambda g, _: finish(g) or 0, 0)
        finish(jnp.int32(tokens // group - 1))

    run(False)

    @pl.when(jnp.max(bad[...]) > 0)
    def _():
        run(True)

    attended = jnp.concatenate(
        [rows[pl.ds(h, tokens, stride=heads), :].astype(bf16) for h in range(heads)], axis=1
    )
    weight_copy.wait()
    width = out_refs[0].shape[1]
    step = 2 * LANES
    for k, out_ref in enumerate(out_refs):
        begin = 0 if outputs == 1 else jnp.where(here == k, width, 0)
        for n in range(0, width, step):
            some = wbuf[:, pl.ds(pl.multiple_of(begin + n, step), step)]
            out_ref[:, n : n + step] = jnp.dot(attended, some, preferred_element_type=f32)


def attended_and_projected(queries, shards, meta, weight, outputs):
    tokens, width = queries.shape
    heads = width // DH
    cols = W2 * heads
    size = max(heads, PACK)
    f32, bf16 = jnp.float32, jnp.bfloat16
    vmem = pl.BlockSpec(memory_space=pltpu.VMEM)
    return pl.pallas_call(
        functools.partial(attention_kernel, len(shards), outputs),
        out_shape=[jax.ShapeDtypeStruct((tokens, weight.shape[1] // outputs), f32)] * outputs,
        in_specs=[
            pl.BlockSpec(memory_space=pltpu.SMEM),
            vmem,
            pl.BlockSpec(memory_space=pl.ANY),
        ]
        + [vmem] * len(shards),
        out_specs=[vmem] * outputs,
        scratch_shapes=[
            pltpu.VMEM((W1 + tokens, 4 * DH), bf16),
            pltpu.VMEM(weight.shape, bf16),
            pltpu.SemaphoreType.DMA,
            pltpu.VMEM((tokens, DH), bf16),
            pltpu.VMEM((W1, DH), bf16),
            pltpu.VMEM((W1 // LANES, VR, LANES), bf16),
            pltpu.VMEM((tokens // LANES, VR, LANES), bf16),
            pltpu.VMEM(((tokens + W2) * heads // size, size, DH), bf16),
            pltpu.VMEM(((tokens + W2) * heads // LANES, VR, LANES), f32),
            pltpu.VMEM((LANES, DH), bf16),
            pltpu.VMEM((VR, LANES), bf16),
            pltpu.VMEM((tokens * heads, DH), f32),
            pltpu.VMEM((tokens, VR, LANES), f32),
            pltpu.VMEM((tokens, 8, LANES), f32),
            pltpu.VMEM((8, LANES), f32),
            pltpu.VMEM((tokens * heads, DH), f32),
        ],
        compiler_params=pltpu.CompilerParams(vmem_limit_bytes=40 * 2**20),
    )(meta, queries, weight, *shards)

HOPS = 3


def shifted(block, axis, distance):
    devices = range(lax.axis_size(axis))
    return lax.ppermute(block, axis, [(i - distance, i) for i in devices if i - distance in devices])


def swapped(block, axis, bits):
    return lax.ppermute(block, axis, [(i, i ^ bits) for i in range(lax.axis_size(axis))])


def collect_window(kv_rows, back):
    if lax.axis_size("head") != 2 or back != 4:
        return [shifted(kv_rows, "ctx", back - k) for k in range(back)] + [kv_rows]

    def taken(distances):
        devices = range(lax.axis_size("ctx"))
        route = [
            ((i - d) * 2 + h, i * 2 + h) for i in devices for h, d in enumerate(distances) if i >= d
        ]
        return lax.ppermute(kv_rows, ("ctx", "head"), route)

    held = jnp.concatenate([taken((2, 4)), taken((1, 3))], axis=0)
    return [held, swapped(held, "head", 1), kv_rows]


def body(queries, kv_rows, doc_start, destination, out_weight):
    position = lax.axis_index("ctx")
    tokens = queries.shape[0]
    blocks = tokens // QB
    group = HOPS + 1
    back = W1 // tokens
    shards = collect_window(kv_rows, back)
    first = position * blocks
    starts = lax.dynamic_slice_in_dim(doc_start, first, blocks, 0)
    own_rows = (first + jnp.arange(blocks, dtype=jnp.int32)) * QB
    inval = jnp.clip(starts - (own_rows - W1), 0, W1).astype(jnp.int32)
    place = position % group
    slots = group * blocks
    targets = lax.dynamic_slice_in_dim(destination, first - place * blocks, slots, 0)
    row = jnp.arange(group * tokens, dtype=jnp.int32)
    source = (place ^ (row // tokens)) * blocks + row % tokens // QB
    known = source[:, None] == jnp.arange(slots, dtype=jnp.int32)[None, :]
    target = jnp.sum(jnp.where(known, targets[None, :], 0), axis=1) * QB + row % QB
    pick = target[:, None] == (first * QB + jnp.arange(tokens, dtype=jnp.int32))[None, :]
    pick = pick.astype(jnp.bfloat16)
    here = lax.axis_index("head").astype(jnp.int32)
    meta = jnp.concatenate([inval, here[None]])
    outputs = 2 if len(shards) == 3 else 1
    partials = attended_and_projected(queries, shards, meta, out_weight, outputs)
    if outputs == 2:
        summed = partials[1] + swapped(partials[0], "head", 1)
    else:
        summed = lax.psum_scatter(partials[0], "head", scatter_dimension=1, tiled=True)
    projected = summed.astype(jnp.bfloat16)
    pieces = jnp.concatenate(
        [projected] + [swapped(projected, "ctx", r) for r in range(1, group)], axis=0
    )
    return lax.dot_general(
        pieces, pick, (((0,), (0,)), ((), ())), preferred_element_type=jnp.float32
    ).astype(jnp.bfloat16)


def solution(mesh):
    in_specs = (P("ctx", "head"), P("ctx", None), P(), P(), P("head", None))
    return jax.shard_map(
        body, mesh=mesh, in_specs=in_specs, out_specs=P("head", "ctx"), check_vma=False
    )
```

```python
import functools

import jax
import jax.numpy as jnp
import numpy as np
from jax import lax
from jax.experimental import pallas as pl
from jax.experimental.pallas import tpu as pltpu
from jax.sharding import PartitionSpec as P

DH = 128
W1 = 512
W2 = 32
QB = 32
LANES = 128
PACK = 16
VR = DH + PACK
SAMPLE = 32
AHEAD = 3
LIMIT = 1e30
LOG2E = 1.4426950408889634


def iota(shape, dim):
    return lax.broadcasted_iota(jnp.int32, shape, dim)


def spread(columns, first, heads):
    pick = iota((columns.shape[1], LANES), 0) == first + iota((columns.shape[1], LANES), 1) // heads
    pick = pick.astype(jnp.float32).astype(jnp.bfloat16)
    return jnp.dot(columns, pick, preferred_element_type=jnp.float32)


def with_ones(values):
    return jnp.concatenate(
        [values.astype(jnp.float32).T, jnp.ones((VR - DH, LANES), jnp.float32)], axis=0
    ).astype(jnp.bfloat16)


def own_kernel(q_ref, kv_ref, q3, k1o, v1o, k2o, v2o):
    f32, bf16 = jnp.float32, jnp.bfloat16
    tokens = q_ref.shape[0]
    heads = q_ref.shape[1] // DH
    group = LANES // heads
    k1o[...] = kv_ref[:, :DH]
    second = kv_ref[:, 2 * DH : 3 * DH].astype(f32)
    second = jnp.broadcast_to(second[:, None, :], (tokens, heads, DH))
    k2o[...] = second.reshape(k2o.shape).astype(bf16)
    for k in range(tokens // LANES):
        v1o[k] = with_ones(kv_ref[k * LANES : (k + 1) * LANES, DH : 2 * DH])
        columns = with_ones(kv_ref[k * LANES : (k + 1) * LANES, 3 * DH :])
        for c in range(heads):
            v2o[k * heads + c] = spread(columns, c * group, heads)
    for h in range(heads):
        q3[pl.ds(h, tokens, stride=heads), :] = q_ref[:, h * DH : (h + 1) * DH].astype(f32)


def attention_kernel(pairs, outputs, meta_ref, q3, k1o, v1o, k2o, v2o, w_ref, *refs):
    shards, refs = refs[:pairs], refs[pairs:]
    out_refs, refs = refs[:outputs], refs[outputs:]
    kv_ref, wbuf, wsem, k1n, k1s, v1t, v1n, k2x, v2x, rowid, laneid, part, top2, bad, rows = refs
    tokens = k1o.shape[0]
    heads = q3.shape[0] // tokens
    cols = W2 * heads
    group = LANES // heads
    tiles = tokens // LANES
    near_tiles = cols // LANES
    size = max(heads, PACK)
    pack = size // heads
    wide = min(2 * LANES, cols)
    scale = LOG2E / np.sqrt(DH)
    f32, bf16 = jnp.float32, jnp.bfloat16

    def either(cond, a, b):
        if isinstance(cond, bool):
            return a if cond else b
        return jnp.where(cond, a, b)

    weight_copy = pltpu.make_async_copy(w_ref, wbuf, wsem)
    weight_copy.start()
    blocks = tokens // QB
    here = meta_ref[blocks]

    def lay(order):
        at = 0
        for ref in order:
            kv_ref[at : at + ref.shape[0], :] = ref[...]
            at += ref.shape[0]

    if outputs == 2:

        @pl.when(here == 0)
        def _():
            lay(shards[::-1])

        @pl.when(here != 0)
        def _():
            lay(shards)

    else:
        lay(shards)

    def prepare():
        rowid[...] = iota(rowid.shape, 0).astype(f32).astype(bf16)
        laneid[...] = iota(laneid.shape, 1).astype(f32).astype(bf16)
        bad[...] = jnp.zeros_like(bad)
        k1n[...] = k1o[...]
        v1n[...] = v1o[...]
        second = kv_ref[W1 - W2 :, 2 * DH : 3 * DH].astype(f32)
        second = jnp.broadcast_to(second[:, None, :], (W2, heads, DH))
        k2x[: W2 // pack] = second.reshape(W2 // pack, size, DH).astype(bf16)
        k2x[W2 // pack :] = k2o[...]
        columns = with_ones(kv_ref[W1 - LANES :, 3 * DH :])
        for k in range(near_tiles):
            v2x[k] = spread(columns, LANES - W2 + k * group, heads)
        v2x[near_tiles:] = v2o[...]

    def reset(t, inv):
        kt = k1o[pl.ds(pl.multiple_of(t, PACK), PACK), :].astype(f32)[:1]
        window = kv_ref[:, : 2 * DH].astype(f32)
        ok = iota((W1, DH), 0) >= inv
        k1s[...] = jnp.where(ok, window[:, :DH], kt).astype(bf16)
        values = jnp.where(ok, window[:, DH:], 0.0)
        for k in range(W1 // LANES):
            v1t[k, :DH] = values[k * LANES : (k + 1) * LANES].T.astype(bf16)
            live = k * LANES + iota((VR - DH, LANES), 1) >= inv
            v1t[k, DH:] = live.astype(f32).astype(bf16)
        k1n[...] = jnp.where(iota((tokens, DH), 0) < t, kt, k1n[...].astype(f32)).astype(bf16)
        for k in range(tiles):
            gone = k * LANES + iota((VR, LANES), 1) < t
            v1n[k] = jnp.where(gone, 0.0, v1n[k].astype(f32)).astype(bf16)

        @pl.when(inv == W1)
        def _():
            fill = jnp.broadcast_to(k2x[(t + W2) // pack].astype(f32)[:1], (size, DH)).astype(bf16)
            for s in range(W2 // pack):
                k2x[t // pack + s] = fill
            for k in range(near_tiles):
                v2x[t // group + k] = jnp.zeros((VR, LANES), f32)

    def scores(g, u):
        t = g * group + u
        mark = t.astype(f32).astype(bf16)
        keys = [
            jnp.where(rowid[...] + (k * LANES) <= mark, k1n[k * LANES : (k + 1) * LANES], k1s[k * LANES : (k + 1) * LANES])
            for k in range(tiles)
        ]
        keys = jnp.concatenate(keys + [k1s[tokens:]], axis=0)
        query = q3[pl.ds(t * heads, heads), :]
        if heads < PACK:
            query = jnp.concatenate([query] * pack, axis=0)
        query = query.astype(bf16)
        base = g * (group // pack)
        for n in range(0, cols, wide):
            paired = []
            for s in range(n // size, (n + wide) // size):
                if s * pack >= group:
                    near_keys = k2x[base + s]
                elif pack == 1:
                    near_keys = k2x[base + either(s <= u, s + W2, s)]
                else:
                    token = s * pack + iota((size, DH), 0) // heads
                    after = k2x[base + s + W2 // pack].astype(f32)
                    near_keys = jnp.where(token <= u, after, k2x[base + s].astype(f32)).astype(bf16)
                paired.append(near_keys * query)
            yield lax.dot_general(
                keys,
                jnp.concatenate(paired, axis=0),
                (((1,), (1,)), ((), ())),
                preferred_element_type=f32,
            )

    def highest(logits, best=None):
        top = jnp.max(logits, axis=0, keepdims=True)
        for k in range(0, wide, LANES):
            some = top[:, k : k + LANES]
            best = some if best is None else jnp.maximum(best, some)
        return best

    def mix(g, u, n, logits, top):
        mark = (g * group + u).astype(f32).astype(bf16)
        values = [
            jnp.where(laneid[...] + (k * LANES) <= mark, v1n[k], v1t[k]) for k in range(tiles)
        ] + [v1t[k] for k in range(tiles, W1 // LANES)]
        tops = jnp.concatenate([top] * (wide // LANES), axis=1)
        product = None
        for k in range(0, W1, 2 * LANES):
            weights = jnp.exp2(logits[k : k + 2 * LANES] * scale - tops).astype(bf16)
            two = jnp.concatenate(values[k // LANES : k // LANES + 2], axis=1)
            some = jnp.dot(two, weights, preferred_element_type=f32)
            product = some if product is None else product + some
        total = None
        for c in range(0, wide, LANES):
            k = (n + c) // LANES
            near = v2x[g + k]
            if k == 0:
                near = jnp.where(iota((VR, LANES), 1) // heads <= u, v2x[g + near_tiles], near)
            some = product[:, c : c + LANES] * near
            total = some if total is None else total + some
        return total

    def keep(g, u, total, top):
        part[g * group + u] = total
        top2[g * group + u] = jnp.broadcast_to(top, (8, LANES))
        bad[...] = jnp.where(total[DH : DH + 8] < LIMIT, bad[...], 1.0)

    def finish(g):
        lane = iota((VR, LANES), 1)
        sums = []
        for u in range(group):
            top = top2[g * group + u]
            best = top
            shift = LANES // 2
            while shift >= heads:
                best = jnp.maximum(best, pltpu.roll(best, shift, 1))
                shift //= 2
            sums.append(part[g * group + u] * jnp.exp2(top - best)[:1])
        shift = heads
        while shift < LANES:
            low = lane % (2 * shift) < shift
            sums = [
                jnp.where(low, a, b) + pltpu.roll(jnp.where(low, b, a), shift, 1)
                for a, b in zip(sums[::2], sums[1::2])
            ]
            shift *= 2
        value = sums[0][:DH] * (1.0 / sums[0][DH : DH + 1])
        rows[pl.ds(pl.multiple_of(g * LANES, LANES), LANES), :] = value.T

    def run(exact):
        prepare()

        def block(b, _):
            inv = meta_ref[b]
            g0 = b * (QB // group)

            @pl.when((b == 0) | (inv == W1))
            def _():
                reset(b * QB, inv)

            def fast(s, _):
                g = g0 + s
                work = []
                for u in range(group):
                    work += [(u, n) for n in range(0, cols, wide)]
                source = {u: scores(g, u) for u in range(group)}
                top = total = None
                ahead = [next(source[u]) for u, n in work[:AHEAD]]
                for i, (u, n) in enumerate(work):
                    if i + AHEAD < len(work):
                        ahead.append(next(source[work[i + AHEAD][0]]))
                    logits = ahead.pop(0)
                    if n == 0:
                        top = highest(logits[:SAMPLE]) * scale
                        total = None
                    some = mix(g, u, n, logits, top)
                    total = some if total is None else total + some
                    if n + wide == cols:
                        keep(g, u, total, top)
                    if i == 0:
                        finish(jnp.maximum(g - 1, 0))
                return 0

            def slow(s, _):
                g, u = g0 + s // group, s % group
                best = None
                for logits in scores(g, u):
                    best = highest(logits, best)
                total = None
                for n, logits in zip(range(0, cols, wide), scores(g, u)):
                    some = mix(g, u, n, logits, best * scale)
                    total = some if total is None else total + some
                keep(g, u, total, best * scale)
                return 0

            if exact:
                return lax.fori_loop(0, QB, slow, 0)
            return lax.fori_loop(0, QB // group, fast, 0)

        lax.fori_loop(0, tokens // QB, block, 0)
        if exact:
            lax.fori_loop(0, tokens // group - 1, lambda g, _: finish(g) or 0, 0)
        finish(jnp.int32(tokens // group - 1))

    run(False)

    @pl.when(jnp.max(bad[...]) > 0)
    def _():
        run(True)

    attended = jnp.concatenate(
        [rows[pl.ds(h, tokens, stride=heads), :].astype(bf16) for h in range(heads)], axis=1
    )
    weight_copy.wait()
    width = out_refs[0].shape[1]
    step = 2 * LANES
    for k, out_ref in enumerate(out_refs):
        begin = 0 if outputs == 1 else jnp.where(here == k, width, 0)
        for n in range(0, width, step):
            some = wbuf[:, pl.ds(pl.multiple_of(begin + n, step), step)]
            out_ref[:, n : n + step] = jnp.dot(attended, some, preferred_element_type=f32)


VMEM = pl.BlockSpec(memory_space=pltpu.VMEM)
HBM = pl.BlockSpec(memory_space=pltpu.HBM)


def own_layouts(queries, kv_rows):
    tokens, width = queries.shape
    heads = width // DH
    size = max(heads, PACK)
    f32, bf16 = jnp.float32, jnp.bfloat16
    return pl.pallas_call(
        own_kernel,
        out_shape=[
            jax.ShapeDtypeStruct((tokens * heads, DH), f32),
            jax.ShapeDtypeStruct((tokens, DH), bf16),
            jax.ShapeDtypeStruct((tokens // LANES, VR, LANES), bf16),
            jax.ShapeDtypeStruct((tokens * heads // size, size, DH), bf16),
            jax.ShapeDtypeStruct((tokens * heads // LANES, VR, LANES), f32),
        ],
        in_specs=[VMEM] * 2,
        out_specs=[VMEM] * 5,
        compiler_params=pltpu.CompilerParams(vmem_limit_bytes=16 * 2**20),
        cost_estimate=pl.CostEstimate(flops=10**9, bytes_accessed=4 * 2**20, transcendentals=0),
    )(queries, kv_rows)


def attended_and_projected(own, shards, meta, weight, outputs):
    heads = own[0].shape[0] // own[1].shape[0]
    tokens = own[1].shape[0]
    size = max(heads, PACK)
    f32, bf16 = jnp.float32, jnp.bfloat16
    return pl.pallas_call(
        functools.partial(attention_kernel, len(shards), outputs),
        out_shape=[jax.ShapeDtypeStruct((tokens, weight.shape[1] // outputs), f32)] * outputs,
        in_specs=[pl.BlockSpec(memory_space=pltpu.SMEM)] + [VMEM] * 5 + [HBM] + [VMEM] * len(shards),
        out_specs=[VMEM] * outputs,
        scratch_shapes=[
            pltpu.VMEM((W1, 4 * DH), bf16),
            pltpu.VMEM(weight.shape, bf16),
            pltpu.SemaphoreType.DMA,
            pltpu.VMEM((tokens, DH), bf16),
            pltpu.VMEM((W1, DH), bf16),
            pltpu.VMEM((W1 // LANES, VR, LANES), bf16),
            pltpu.VMEM((tokens // LANES, VR, LANES), bf16),
            pltpu.VMEM(((tokens + W2) * heads // size, size, DH), bf16),
            pltpu.VMEM(((tokens + W2) * heads // LANES, VR, LANES), f32),
            pltpu.VMEM((LANES, DH), bf16),
            pltpu.VMEM((VR, LANES), bf16),
            pltpu.VMEM((tokens, VR, LANES), f32),
            pltpu.VMEM((tokens, 8, LANES), f32),
            pltpu.VMEM((8, LANES), f32),
            pltpu.VMEM((tokens * heads, DH), f32),
        ],
        compiler_params=pltpu.CompilerParams(vmem_limit_bytes=46 * 2**20),
    )(meta, *own, weight, *shards)

HOPS = 3


def shifted(block, axis, distance):
    devices = range(lax.axis_size(axis))
    return lax.ppermute(block, axis, [(i - distance, i) for i in devices if i - distance in devices])


def swapped(block, axis, bits):
    return lax.ppermute(block, axis, [(i, i ^ bits) for i in range(lax.axis_size(axis))])


def collect_window(kv_rows, back, own):
    if lax.axis_size("head") != 2 or back != 4:
        return [shifted(kv_rows, "ctx", back - k) for k in range(back)], own

    def taken(distances):
        devices = range(lax.axis_size("ctx"))
        route = [
            ((i - d) * 2 + h, i * 2 + h) for i in devices for h, d in enumerate(distances) if i >= d
        ]
        return lax.ppermute(kv_rows, ("ctx", "head"), route)

    parts, own = lax.optimization_barrier(([taken((2, 4)), taken((1, 3))], own))
    held = jnp.concatenate(parts, axis=0)
    return [held, swapped(held, "head", 1)], own


def body(queries, kv_rows, doc_start, destination, out_weight):
    position = lax.axis_index("ctx")
    tokens = queries.shape[0]
    blocks = tokens // QB
    group = HOPS + 1
    back = W1 // tokens
    shards, own = collect_window(kv_rows, back, own_layouts(queries, kv_rows))
    first = position * blocks
    starts = lax.dynamic_slice_in_dim(doc_start, first, blocks, 0)
    own_rows = (first + jnp.arange(blocks, dtype=jnp.int32)) * QB
    inval = jnp.clip(starts - (own_rows - W1), 0, W1).astype(jnp.int32)
    place = position % group
    slots = group * blocks
    targets = lax.dynamic_slice_in_dim(destination, first - place * blocks, slots, 0)
    row = jnp.arange(group * tokens, dtype=jnp.int32)
    source = (place ^ (row // tokens)) * blocks + row % tokens // QB
    known = source[:, None] == jnp.arange(slots, dtype=jnp.int32)[None, :]
    target = jnp.sum(jnp.where(known, targets[None, :], 0), axis=1) * QB + row % QB
    pick = target[:, None] == (first * QB + jnp.arange(tokens, dtype=jnp.int32))[None, :]
    pick = pick.astype(jnp.bfloat16)
    here = lax.axis_index("head").astype(jnp.int32)
    meta = jnp.concatenate([inval, here[None]])
    outputs = 2 if len(shards) == 2 else 1
    partials = attended_and_projected(own, shards, meta, out_weight, outputs)
    if outputs == 2:
        summed = partials[1] + swapped(partials[0], "head", 1)
    else:
        summed = lax.psum_scatter(partials[0], "head", scatter_dimension=1, tiled=True)
    projected = summed.astype(jnp.bfloat16)
    pieces = jnp.concatenate(
        [projected] + [swapped(projected, "ctx", r) for r in range(1, group)], axis=0
    )
    return lax.dot_general(
        pieces, pick, (((0,), (0,)), ((), ())), preferred_element_type=jnp.float32
    ).astype(jnp.bfloat16)


def solution(mesh):
    in_specs = (P("ctx", "head"), P("ctx", None), P(), P(), P("head", None))
    return jax.shard_map(
        body, mesh=mesh, in_specs=in_specs, out_specs=P("head", "ctx"), check_vma=False
    )
```

```python
import functools

import jax
import jax.numpy as jnp
import numpy as np
from jax import lax
from jax.experimental import pallas as pl
from jax.experimental.pallas import tpu as pltpu
from jax.sharding import PartitionSpec as P

DH = 128
W1 = 512
W2 = 32
QB = 32
LANES = 128
PACK = 16
VR = DH + PACK
SAMPLE = 32
AHEAD = 3
LIMIT = 1e30
LOG2E = 1.4426950408889634


def iota(shape, dim):
    return lax.broadcasted_iota(jnp.int32, shape, dim)


def spread(columns, first, heads):
    pick = iota((columns.shape[1], LANES), 0) == first + iota((columns.shape[1], LANES), 1) // heads
    pick = pick.astype(jnp.float32).astype(jnp.bfloat16)
    return jnp.dot(columns, pick, preferred_element_type=jnp.float32)


def with_ones(values):
    return jnp.concatenate(
        [values.astype(jnp.float32).T, jnp.ones((VR - DH, LANES), jnp.float32)], axis=0
    ).astype(jnp.bfloat16)


def own_kernel(q_ref, kv_ref, q3, k1o, v1o, k2o, v2o):
    f32, bf16 = jnp.float32, jnp.bfloat16
    tokens = q_ref.shape[0]
    heads = q_ref.shape[1] // DH
    group = LANES // heads
    k1o[...] = kv_ref[:, :DH]
    second = kv_ref[:, 2 * DH : 3 * DH].astype(f32)
    second = jnp.broadcast_to(second[:, None, :], (tokens, heads, DH))
    k2o[...] = second.reshape(k2o.shape).astype(bf16)
    for k in range(tokens // LANES):
        v1o[k] = with_ones(kv_ref[k * LANES : (k + 1) * LANES, DH : 2 * DH])
        columns = with_ones(kv_ref[k * LANES : (k + 1) * LANES, 3 * DH :])
        for c in range(heads):
            v2o[k * heads + c] = spread(columns, c * group, heads)
    for h in range(heads):
        q3[pl.ds(h, tokens, stride=heads), :] = q_ref[:, h * DH : (h + 1) * DH].astype(f32)


def attention_kernel(pairs, outputs, meta_ref, q3, k1o, v1o, k2o, v2o, w_ref, *refs):
    shards, refs = refs[:pairs], refs[pairs:]
    out_refs, refs = refs[:outputs], refs[outputs:]
    kv_ref, wbuf, wsem, k1n, k1s, v1t, v1n, k2x, v2x, rowid, laneid, part, top2, bad, rows = refs
    tokens = k1o.shape[0]
    heads = q3.shape[0] // tokens
    cols = W2 * heads
    group = LANES // heads
    tiles = tokens // LANES
    near_tiles = cols // LANES
    size = max(heads, PACK)
    pack = size // heads
    wide = min(2 * LANES, cols)
    scale = LOG2E / np.sqrt(DH)
    f32, bf16 = jnp.float32, jnp.bfloat16

    def either(cond, a, b):
        if isinstance(cond, bool):
            return a if cond else b
        return jnp.where(cond, a, b)

    weight_copy = pltpu.make_async_copy(w_ref, wbuf, wsem)
    weight_copy.start()
    blocks = tokens // QB
    here = meta_ref[blocks]

    def lay(order):
        at = 0
        for ref in order:
            kv_ref[at : at + ref.shape[0], :] = ref[...]
            at += ref.shape[0]

    if outputs == 2:

        @pl.when(here == 0)
        def _():
            lay(shards[::-1])

        @pl.when(here != 0)
        def _():
            lay(shards)

    else:
        lay(shards)

    def prepare():
        rowid[...] = iota(rowid.shape, 0).astype(f32).astype(bf16)
        laneid[...] = iota(laneid.shape, 1).astype(f32).astype(bf16)
        bad[...] = jnp.zeros_like(bad)
        k1n[...] = k1o[...]
        v1n[...] = v1o[...]
        second = kv_ref[W1 - W2 :, 2 * DH : 3 * DH].astype(f32)
        second = jnp.broadcast_to(second[:, None, :], (W2, heads, DH))
        k2x[: W2 // pack] = second.reshape(W2 // pack, size, DH).astype(bf16)
        k2x[W2 // pack :] = k2o[...]
        columns = with_ones(kv_ref[W1 - LANES :, 3 * DH :])
        for k in range(near_tiles):
            v2x[k] = spread(columns, LANES - W2 + k * group, heads)
        v2x[near_tiles:] = v2o[...]

    def reset(t, inv):
        kt = k1o[pl.ds(pl.multiple_of(t, PACK), PACK), :].astype(f32)[:1]
        window = kv_ref[:, : 2 * DH].astype(f32)
        ok = iota((W1, DH), 0) >= inv
        k1s[...] = jnp.where(ok, window[:, :DH], kt).astype(bf16)
        values = jnp.where(ok, window[:, DH:], 0.0)
        for k in range(W1 // LANES):
            v1t[k, :DH] = values[k * LANES : (k + 1) * LANES].T.astype(bf16)
            live = k * LANES + iota((VR - DH, LANES), 1) >= inv
            v1t[k, DH:] = live.astype(f32).astype(bf16)
        k1n[...] = jnp.where(iota((tokens, DH), 0) < t, kt, k1n[...].astype(f32)).astype(bf16)
        for k in range(tiles):
            gone = k * LANES + iota((VR, LANES), 1) < t
            v1n[k] = jnp.where(gone, 0.0, v1n[k].astype(f32)).astype(bf16)

        @pl.when(inv == W1)
        def _():
            fill = jnp.broadcast_to(k2x[(t + W2) // pack].astype(f32)[:1], (size, DH)).astype(bf16)
            for s in range(W2 // pack):
                k2x[t // pack + s] = fill
            for k in range(near_tiles):
                v2x[t // group + k] = jnp.zeros((VR, LANES), f32)

    def scores(g, u):
        t = g * group + u
        mark = t.astype(f32).astype(bf16)
        keys = [
            jnp.where(rowid[...] + (k * LANES) <= mark, k1n[k * LANES : (k + 1) * LANES], k1s[k * LANES : (k + 1) * LANES])
            for k in range(tiles)
        ]
        keys = jnp.concatenate(keys + [k1s[tokens:]], axis=0)
        query = q3[pl.ds(t * heads, heads), :]
        if heads < PACK:
            query = jnp.concatenate([query] * pack, axis=0)
        query = query.astype(bf16)
        base = g * (group // pack)
        for n in range(0, cols, wide):
            paired = []
            for s in range(n // size, (n + wide) // size):
                if s * pack >= group:
                    near_keys = k2x[base + s]
                elif pack == 1:
                    near_keys = k2x[base + either(s <= u, s + W2, s)]
                else:
                    token = s * pack + iota((size, DH), 0) // heads
                    after = k2x[base + s + W2 // pack].astype(f32)
                    near_keys = jnp.where(token <= u, after, k2x[base + s].astype(f32)).astype(bf16)
                paired.append(near_keys * query)
            yield lax.dot_general(
                keys,
                jnp.concatenate(paired, axis=0),
                (((1,), (1,)), ((), ())),
                preferred_element_type=f32,
            )

    def highest(logits, best=None):
        top = jnp.max(logits, axis=0, keepdims=True)
        for k in range(0, wide, LANES):
            some = top[:, k : k + LANES]
            best = some if best is None else jnp.maximum(best, some)
        return best

    def mix(g, u, n, logits, top):
        mark = (g * group + u).astype(f32).astype(bf16)
        values = [
            jnp.where(laneid[...] + (k * LANES) <= mark, v1n[k], v1t[k]) for k in range(tiles)
        ] + [v1t[k] for k in range(tiles, W1 // LANES)]
        tops = jnp.concatenate([top] * (wide // LANES), axis=1)
        product = None
        for k in range(0, W1, 2 * LANES):
            weights = jnp.exp2(logits[k : k + 2 * LANES] * scale - tops).astype(bf16)
            two = jnp.concatenate(values[k // LANES : k // LANES + 2], axis=1)
            some = jnp.dot(two, weights, preferred_element_type=f32)
            product = some if product is None else product + some
        total = None
        for c in range(0, wide, LANES):
            k = (n + c) // LANES
            near = v2x[g + k]
            if k == 0:
                near = jnp.where(iota((VR, LANES), 1) // heads <= u, v2x[g + near_tiles], near)
            some = product[:, c : c + LANES] * near
            total = some if total is None else total + some
        return total

    def keep(g, u, total, top):
        part[g * group + u] = total
        top2[g * group + u] = jnp.broadcast_to(top, (8, LANES))
        bad[...] = jnp.where(total[DH : DH + 8] < LIMIT, bad[...], 1.0)

    def finish(g):
        lane = iota((VR, LANES), 1)
        sums = []
        for u in range(group):
            top = top2[g * group + u]
            best = top
            shift = LANES // 2
            while shift >= heads:
                best = jnp.maximum(best, pltpu.roll(best, shift, 1))
                shift //= 2
            sums.append(part[g * group + u] * jnp.exp2(top - best)[:1])
        shift = heads
        while shift < LANES:
            low = lane % (2 * shift) < shift
            sums = [
                jnp.where(low, a, b) + pltpu.roll(jnp.where(low, b, a), shift, 1)
                for a, b in zip(sums[::2], sums[1::2])
            ]
            shift *= 2
        value = sums[0][:DH] * (1.0 / sums[0][DH : DH + 1])
        rows[pl.ds(pl.multiple_of(g * LANES, LANES), LANES), :] = value.T

    def run(exact):
        prepare()

        def block(b, _):
            inv = meta_ref[b]
            g0 = b * (QB // group)

            @pl.when((b == 0) | (inv == W1))
            def _():
                reset(b * QB, inv)

            def fast(s, _):
                g = g0 + s
                work = []
                for u in range(group):
                    work += [(u, n) for n in range(0, cols, wide)]
                source = {u: scores(g, u) for u in range(group)}
                top = total = None
                ahead = [next(source[u]) for u, n in work[:AHEAD]]
                for i, (u, n) in enumerate(work):
                    if i + AHEAD < len(work):
                        ahead.append(next(source[work[i + AHEAD][0]]))
                    logits = ahead.pop(0)
                    if n == 0:
                        top = highest(logits[:SAMPLE]) * scale
                        total = None
                    some = mix(g, u, n, logits, top)
                    total = some if total is None else total + some
                    if n + wide == cols:
                        keep(g, u, total, top)
                    if i == 0:
                        finish(jnp.maximum(g - 1, 0))
                return 0

            def slow(s, _):
                g, u = g0 + s // group, s % group
                best = None
                for logits in scores(g, u):
                    best = highest(logits, best)
                total = None
                for n, logits in zip(range(0, cols, wide), scores(g, u)):
                    some = mix(g, u, n, logits, best * scale)
                    total = some if total is None else total + some
                keep(g, u, total, best * scale)
                return 0

            if exact:
                return lax.fori_loop(0, QB, slow, 0)
            return lax.fori_loop(0, QB // group, fast, 0)

        lax.fori_loop(0, tokens // QB, block, 0)
        if exact:
            lax.fori_loop(0, tokens // group - 1, lambda g, _: finish(g) or 0, 0)
        finish(jnp.int32(tokens // group - 1))

    run(False)

    @pl.when(jnp.max(bad[...]) > 0)
    def _():
        run(True)

    attended = jnp.concatenate(
        [rows[pl.ds(h, tokens, stride=heads), :].astype(bf16) for h in range(heads)], axis=1
    )
    weight_copy.wait()
    width = out_refs[0].shape[1]
    step = 2 * LANES
    for k, out_ref in enumerate(out_refs):
        begin = 0 if outputs == 1 else jnp.where(here == k, width, 0)
        for n in range(0, width, step):
            some = wbuf[:, pl.ds(pl.multiple_of(begin + n, step), step)]
            out_ref[:, n : n + step] = jnp.dot(attended, some, preferred_element_type=f32)


VMEM = pl.BlockSpec(memory_space=pltpu.VMEM)
HBM = pl.BlockSpec(memory_space=pltpu.HBM)


def own_layouts(queries, kv_rows):
    tokens, width = queries.shape
    heads = width // DH
    size = max(heads, PACK)
    f32, bf16 = jnp.float32, jnp.bfloat16
    return pl.pallas_call(
        own_kernel,
        out_shape=[
            jax.ShapeDtypeStruct((tokens * heads, DH), f32),
            jax.ShapeDtypeStruct((tokens, DH), bf16),
            jax.ShapeDtypeStruct((tokens // LANES, VR, LANES), bf16),
            jax.ShapeDtypeStruct((tokens * heads // size, size, DH), bf16),
            jax.ShapeDtypeStruct((tokens * heads // LANES, VR, LANES), f32),
        ],
        in_specs=[VMEM] * 2,
        out_specs=[VMEM] * 5,
        compiler_params=pltpu.CompilerParams(vmem_limit_bytes=16 * 2**20),
        cost_estimate=pl.CostEstimate(flops=10**9, bytes_accessed=4 * 2**20, transcendentals=0),
    )(queries, kv_rows)


def attended_and_projected(own, shards, meta, weight, outputs):
    heads = own[0].shape[0] // own[1].shape[0]
    tokens = own[1].shape[0]
    size = max(heads, PACK)
    f32, bf16 = jnp.float32, jnp.bfloat16
    return pl.pallas_call(
        functools.partial(attention_kernel, len(shards), outputs),
        out_shape=[jax.ShapeDtypeStruct((tokens, weight.shape[1] // outputs), f32)] * outputs,
        in_specs=[pl.BlockSpec(memory_space=pltpu.SMEM)] + [VMEM] * 5 + [HBM] + [VMEM] * len(shards),
        out_specs=[VMEM] * outputs,
        scratch_shapes=[
            pltpu.VMEM((W1, 4 * DH), bf16),
            pltpu.VMEM(weight.shape, bf16),
            pltpu.SemaphoreType.DMA,
            pltpu.VMEM((tokens, DH), bf16),
            pltpu.VMEM((W1, DH), bf16),
            pltpu.VMEM((W1 // LANES, VR, LANES), bf16),
            pltpu.VMEM((tokens // LANES, VR, LANES), bf16),
            pltpu.VMEM(((tokens + W2) * heads // size, size, DH), bf16),
            pltpu.VMEM(((tokens + W2) * heads // LANES, VR, LANES), f32),
            pltpu.VMEM((LANES, DH), bf16),
            pltpu.VMEM((VR, LANES), bf16),
            pltpu.VMEM((tokens, VR, LANES), f32),
            pltpu.VMEM((tokens, 8, LANES), f32),
            pltpu.VMEM((8, LANES), f32),
            pltpu.VMEM((tokens * heads, DH), f32),
        ],
        compiler_params=pltpu.CompilerParams(vmem_limit_bytes=43 * 2**20),
    )(meta, *own, weight, *shards)

HOPS = 3


def shifted(block, axis, distance):
    devices = range(lax.axis_size(axis))
    return lax.ppermute(block, axis, [(i - distance, i) for i in devices if i - distance in devices])


def swapped(block, axis, bits):
    return lax.ppermute(block, axis, [(i, i ^ bits) for i in range(lax.axis_size(axis))])


def collect_window(kv_rows, back, own):
    if lax.axis_size("head") != 2 or back != 4:
        return [shifted(kv_rows, "ctx", back - k) for k in range(back)], own

    def taken(distances):
        devices = range(lax.axis_size("ctx"))
        route = [
            ((i - d) * 2 + h, i * 2 + h) for i in devices for h, d in enumerate(distances) if i >= d
        ]
        return lax.ppermute(kv_rows, ("ctx", "head"), route)

    parts, own = lax.optimization_barrier(([taken((2, 4)), taken((1, 3))], own))
    held = jnp.concatenate(parts, axis=0)
    return [held, swapped(held, "head", 1)], own


def earlier_alike(devices):
    blocks = devices.shape[-1]
    same = devices[..., :, None] == devices[..., None, :]
    before = np.tril(np.ones((blocks, blocks), bool), -1)
    return jnp.sum(jnp.where(before, same, False).astype(jnp.int32), axis=-1)


def split_kernel(room, index_ref, *refs):
    count = 1 + index_ref.shape[0] // room
    terms, outs = refs[:-count], refs[-count:]

    def rows(where):
        some = terms[0][where, :]
        for term in terms[1:]:
            some = some + term[where, :]
        return some.astype(jnp.bfloat16)

    outs[0][...] = rows(slice(None))
    for r, out in enumerate(outs[1:]):
        for c in range(room):
            block = index_ref[r * room + c]
            out[c * QB : (c + 1) * QB, :] = rows(pl.ds(pl.multiple_of(block * QB, QB), QB))


def split(terms, index, room):
    tokens, width = terms[0].shape
    others = HOPS
    vmem = pl.BlockSpec(memory_space=pltpu.VMEM)
    return pl.pallas_call(
        functools.partial(split_kernel, room),
        out_shape=[jax.ShapeDtypeStruct((tokens, width), jnp.bfloat16)]
        + [jax.ShapeDtypeStruct((room * QB, width), jnp.bfloat16)] * others,
        in_specs=[pl.BlockSpec(memory_space=pltpu.SMEM)] + [vmem] * len(terms),
        out_specs=[vmem] * (others + 1),
        compiler_params=pltpu.CompilerParams(vmem_limit_bytes=16 * 2**20),
    )(index, *terms)


def exchanged(terms, destination, position, blocks):
    group = HOPS + 1
    room = blocks // 2
    tokens = blocks * QB
    place = position % group
    slots = group * blocks
    targets = lax.dynamic_slice_in_dim(destination, (position - place) * blocks, slots, 0)
    order = place ^ np.arange(group, dtype=np.int32)
    known = order[:, None] == np.arange(group, dtype=np.int32)[None, :]
    slot = jnp.sum(
        jnp.where(known[:, :, None], targets.reshape(1, group, blocks), 0), axis=1
    )
    device = slot // blocks % group
    rank = earlier_alike(device)
    places = np.arange(room, dtype=np.int32)
    mine = (device[1:, None, :] == place) & (rank[1:, None, :] == places[None, :, None])
    got = jnp.sum(jnp.where(mine, slot[1:, None, :] + 1, 0), axis=2) - 1
    sent = (device[0][None, None, :] == order[1:, None, None]) & (
        rank[0][None, None, :] == places[None, :, None]
    )
    numbers = np.arange(blocks, dtype=np.int32)
    index = jnp.sum(jnp.where(sent, numbers[None, None, :], 0), axis=2).reshape(-1)
    everywhere = (destination // blocks % group).reshape(-1, blocks)
    few = jnp.max(earlier_alike(everywhere)) < room
    tokens_here = position * tokens + jnp.arange(tokens, dtype=jnp.int32)

    def placed(pieces, block_slots):
        rows = (block_slots[:, None] * QB + np.arange(QB, dtype=np.int32)[None, :]).reshape(-1)
        pick = (rows[:, None] == tokens_here[None, :]).astype(jnp.bfloat16)
        return lax.dot_general(
            jnp.concatenate(pieces, axis=0),
            pick,
            (((0,), (0,)), ((), ())),
            preferred_element_type=jnp.float32,
        ).astype(jnp.bfloat16)

    def some(*terms):
        own, *outgoing = split(terms, index, room)
        pieces = [own] + [swapped(block, "ctx", r + 1) for r, block in enumerate(outgoing)]
        return placed(pieces, jnp.concatenate([slot[0], got.reshape(-1)]))

    def whole(*terms):
        own = sum(terms[1:], terms[0]).astype(jnp.bfloat16)
        pieces = [own] + [swapped(own, "ctx", r) for r in range(1, group)]
        return placed(pieces, slot.reshape(-1))

    return lax.cond(few, some, whole, *terms)


def body(queries, kv_rows, doc_start, destination, out_weight):
    position = lax.axis_index("ctx")
    tokens = queries.shape[0]
    blocks = tokens // QB
    group = HOPS + 1
    back = W1 // tokens
    shards, own = collect_window(kv_rows, back, own_layouts(queries, kv_rows))
    first = position * blocks
    starts = lax.dynamic_slice_in_dim(doc_start, first, blocks, 0)
    own_rows = (first + jnp.arange(blocks, dtype=jnp.int32)) * QB
    inval = jnp.clip(starts - (own_rows - W1), 0, W1).astype(jnp.int32)
    here = lax.axis_index("head").astype(jnp.int32)
    meta = jnp.concatenate([inval, here[None]])
    outputs = 2 if len(shards) == 2 else 1
    partials = attended_and_projected(own, shards, meta, out_weight, outputs)
    if outputs == 2:
        terms = [partials[1], swapped(partials[0], "head", 1)]
    else:
        terms = [lax.psum_scatter(partials[0], "head", scatter_dimension=1, tiled=True)]
    return exchanged(terms, destination, position, blocks)


def solution(mesh):
    in_specs = (P("ctx", "head"), P("ctx", None), P(), P(), P("head", None))
    return jax.shard_map(
        body, mesh=mesh, in_specs=in_specs, out_specs=P("head", "ctx"), check_vma=False
    )
```

```python
import functools

import jax
import jax.numpy as jnp
import numpy as np
from jax import lax
from jax.experimental import pallas as pl
from jax.experimental.pallas import tpu as pltpu
from jax.sharding import PartitionSpec as P

DH = 128
W1 = 512
W2 = 32
QB = 32
LANES = 128
PACK = 16
VR = DH + PACK
SAMPLE = 32
AHEAD = 3
SPAN = 4
LIMIT = 1e30
LOG2E = 1.4426950408889634


def iota(shape, dim):
    return lax.broadcasted_iota(jnp.int32, shape, dim)


def spread(columns, first, heads):
    pick = iota((columns.shape[1], LANES), 0) == first + iota((columns.shape[1], LANES), 1) // heads
    pick = pick.astype(jnp.float32).astype(jnp.bfloat16)
    return jnp.dot(columns, pick, preferred_element_type=jnp.float32)


def with_ones(values):
    return jnp.concatenate(
        [values.astype(jnp.float32).T, jnp.ones((VR - DH, LANES), jnp.float32)], axis=0
    ).astype(jnp.bfloat16)


def own_kernel(q_ref, kv_ref, q3, k1o, v1o, k2o, v2o):
    f32, bf16 = jnp.float32, jnp.bfloat16
    tokens = q_ref.shape[0]
    heads = q_ref.shape[1] // DH
    group = LANES // heads
    k1o[...] = kv_ref[:, :DH]
    second = kv_ref[:, 2 * DH : 3 * DH].astype(f32)
    second = jnp.broadcast_to(second[:, None, :], (tokens, heads, DH))
    k2o[...] = second.reshape(k2o.shape).astype(bf16)
    for k in range(tokens // LANES):
        v1o[k] = with_ones(kv_ref[k * LANES : (k + 1) * LANES, DH : 2 * DH])
        columns = with_ones(kv_ref[k * LANES : (k + 1) * LANES, 3 * DH :])
        for c in range(heads):
            v2o[k * heads + c] = spread(columns, c * group, heads)
    for h in range(heads):
        q3[pl.ds(h, tokens, stride=heads), :] = q_ref[:, h * DH : (h + 1) * DH].astype(f32)


def attention_kernel(pairs, outputs, meta_ref, q3, k1o, v1o, k2o, v2o, w_ref, *refs):
    shards, refs = refs[:pairs], refs[pairs:]
    out_refs, refs = refs[:outputs], refs[outputs:]
    kv_ref, wbuf, wsem, k1n, k1s, v1t, v1n, k2x, v2x, rowid, laneid, part, top2, bad, rows = refs
    tokens = k1o.shape[0]
    heads = q3.shape[0] // tokens
    cols = W2 * heads
    group = LANES // heads
    tiles = tokens // LANES
    near_tiles = cols // LANES
    size = max(heads, PACK)
    pack = size // heads
    wide = min(2 * LANES, cols)
    span = min(SPAN, QB // group)
    scale = LOG2E / np.sqrt(DH)
    f32, bf16 = jnp.float32, jnp.bfloat16

    def either(cond, a, b):
        if isinstance(cond, bool):
            return a if cond else b
        return jnp.where(cond, a, b)

    weight_copy = pltpu.make_async_copy(w_ref, wbuf, wsem)
    weight_copy.start()
    blocks = tokens // QB
    here = meta_ref[blocks]

    def lay(order):
        at = 0
        for ref in order:
            kv_ref[at : at + ref.shape[0], :] = ref[...]
            at += ref.shape[0]

    if outputs == 2:

        @pl.when(here == 0)
        def _():
            lay(shards[::-1])

        @pl.when(here != 0)
        def _():
            lay(shards)

    else:
        lay(shards)

    def prepare():
        rowid[...] = iota(rowid.shape, 0).astype(f32).astype(bf16)
        laneid[...] = iota(laneid.shape, 1).astype(f32).astype(bf16)
        bad[...] = jnp.zeros_like(bad)
        k1n[...] = k1o[...]
        v1n[...] = v1o[...]
        second = kv_ref[W1 - W2 :, 2 * DH : 3 * DH].astype(f32)
        second = jnp.broadcast_to(second[:, None, :], (W2, heads, DH))
        k2x[: W2 // pack] = second.reshape(W2 // pack, size, DH).astype(bf16)
        k2x[W2 // pack :] = k2o[...]
        columns = with_ones(kv_ref[W1 - LANES :, 3 * DH :])
        for k in range(near_tiles):
            v2x[k] = spread(columns, LANES - W2 + k * group, heads)
        v2x[near_tiles:] = v2o[...]

    def reset(t, inv):
        kt = k1o[pl.ds(pl.multiple_of(t, PACK), PACK), :].astype(f32)[:1]
        window = kv_ref[:, : 2 * DH].astype(f32)
        ok = iota((W1, DH), 0) >= inv
        k1s[...] = jnp.where(ok, window[:, :DH], kt).astype(bf16)
        values = jnp.where(ok, window[:, DH:], 0.0)
        for k in range(W1 // LANES):
            v1t[k, :DH] = values[k * LANES : (k + 1) * LANES].T.astype(bf16)
            live = k * LANES + iota((VR - DH, LANES), 1) >= inv
            v1t[k, DH:] = live.astype(f32).astype(bf16)
        k1n[...] = jnp.where(iota((tokens, DH), 0) < t, kt, k1n[...].astype(f32)).astype(bf16)
        for k in range(tiles):
            gone = k * LANES + iota((VR, LANES), 1) < t
            v1n[k] = jnp.where(gone, 0.0, v1n[k].astype(f32)).astype(bf16)

        @pl.when(inv == W1)
        def _():
            fill = jnp.broadcast_to(k2x[(t + W2) // pack].astype(f32)[:1], (size, DH)).astype(bf16)
            for s in range(W2 // pack):
                k2x[t // pack + s] = fill
            for k in range(near_tiles):
                v2x[t // group + k] = jnp.zeros((VR, LANES), f32)

    def scores(g, u):
        t = g * group + u
        mark = t.astype(f32).astype(bf16)
        keys = [
            jnp.where(rowid[...] + (k * LANES) <= mark, k1n[k * LANES : (k + 1) * LANES], k1s[k * LANES : (k + 1) * LANES])
            for k in range(tiles)
        ]
        keys = jnp.concatenate(keys + [k1s[tokens:]], axis=0)
        query = q3[pl.ds(t * heads, heads), :]
        if heads < PACK:
            query = jnp.concatenate([query] * pack, axis=0)
        query = query.astype(bf16)
        base = g * (group // pack)
        for n in range(0, cols, wide):
            paired = []
            for s in range(n // size, (n + wide) // size):
                if s * pack >= group:
                    near_keys = k2x[base + s]
                elif pack == 1:
                    near_keys = k2x[base + either(s <= u, s + W2, s)]
                else:
                    token = s * pack + iota((size, DH), 0) // heads
                    after = k2x[base + s + W2 // pack].astype(f32)
                    near_keys = jnp.where(token <= u, after, k2x[base + s].astype(f32)).astype(bf16)
                paired.append(near_keys * query)
            yield lax.dot_general(
                keys,
                jnp.concatenate(paired, axis=0),
                (((1,), (1,)), ((), ())),
                preferred_element_type=f32,
            )

    def highest(logits, best=None):
        top = jnp.max(logits, axis=0, keepdims=True)
        for k in range(0, wide, LANES):
            some = top[:, k : k + LANES]
            best = some if best is None else jnp.maximum(best, some)
        return best

    def mix(g, u, n, logits, top):
        mark = (g * group + u).astype(f32).astype(bf16)
        values = [
            jnp.where(laneid[...] + (k * LANES) <= mark, v1n[k], v1t[k]) for k in range(tiles)
        ] + [v1t[k] for k in range(tiles, W1 // LANES)]
        tops = jnp.concatenate([top] * (wide // LANES), axis=1)
        product = None
        for k in range(0, W1, 2 * LANES):
            weights = jnp.exp2(logits[k : k + 2 * LANES] * scale - tops).astype(bf16)
            two = jnp.concatenate(values[k // LANES : k // LANES + 2], axis=1)
            some = jnp.dot(two, weights, preferred_element_type=f32)
            product = some if product is None else product + some
        total = None
        for c in range(0, wide, LANES):
            k = (n + c) // LANES
            near = v2x[g + k]
            if k == 0:
                near = jnp.where(iota((VR, LANES), 1) // heads <= u, v2x[g + near_tiles], near)
            some = product[:, c : c + LANES] * near
            total = some if total is None else total + some
        return total

    def keep(g, u, total, top):
        part[g * group + u] = total
        top2[g * group + u] = jnp.broadcast_to(top, (8, LANES))
        bad[...] = jnp.where(total[DH : DH + 8] < LIMIT, bad[...], 1.0)

    def finish(g):
        lane = iota((VR, LANES), 1)
        sums = []
        for u in range(group):
            top = top2[g * group + u]
            best = top
            shift = LANES // 2
            while shift >= heads:
                best = jnp.maximum(best, pltpu.roll(best, shift, 1))
                shift //= 2
            sums.append(part[g * group + u] * jnp.exp2(top - best)[:1])
        shift = heads
        while shift < LANES:
            low = lane % (2 * shift) < shift
            sums = [
                jnp.where(low, a, b) + pltpu.roll(jnp.where(low, b, a), shift, 1)
                for a, b in zip(sums[::2], sums[1::2])
            ]
            shift *= 2
        value = sums[0][:DH] * (1.0 / sums[0][DH : DH + 1])
        rows[pl.ds(pl.multiple_of(g * LANES, LANES), LANES), :] = value.T

    def run(exact):
        prepare()

        def block(b, _):
            inv = meta_ref[b]
            g0 = b * (QB // group)

            @pl.when((b == 0) | (inv == W1))
            def _():
                reset(b * QB, inv)

            def fast(s, _):
                work = []
                for u in range(span * group):
                    work += [(u, n) for n in range(0, cols, wide)]
                at = [divmod(u, group) for u in range(span * group)]
                first = g0 + s * span
                source = [scores(first + k, u) for k, u in at]
                top = total = None
                ahead = [next(source[u]) for u, n in work[:AHEAD]]
                for i, (u, n) in enumerate(work):
                    if i + AHEAD < len(work):
                        ahead.append(next(source[work[i + AHEAD][0]]))
                    logits = ahead.pop(0)
                    g, v = first + at[u][0], at[u][1]
                    if n == 0:
                        top = highest(logits[:SAMPLE]) * scale
                        total = None
                    some = mix(g, v, n, logits, top)
                    total = some if total is None else total + some
                    if n + wide == cols:
                        keep(g, v, total, top)
                        if v == group // 2:
                            finish(jnp.maximum(g - 1, 0))
                return 0

            def slow(s, _):
                g, u = g0 + s // group, s % group
                best = None
                for logits in scores(g, u):
                    best = highest(logits, best)
                total = None
                for n, logits in zip(range(0, cols, wide), scores(g, u)):
                    some = mix(g, u, n, logits, best * scale)
                    total = some if total is None else total + some
                keep(g, u, total, best * scale)
                return 0

            if exact:
                return lax.fori_loop(0, QB, slow, 0)
            return lax.fori_loop(0, QB // group // span, fast, 0)

        lax.fori_loop(0, tokens // QB, block, 0)
        if exact:
            lax.fori_loop(0, tokens // group - 1, lambda g, _: finish(g) or 0, 0)
        finish(jnp.int32(tokens // group - 1))

    run(False)

    @pl.when(jnp.max(bad[...]) > 0)
    def _():
        run(True)

    attended = jnp.concatenate(
        [rows[pl.ds(h, tokens, stride=heads), :].astype(bf16) for h in range(heads)], axis=1
    )
    weight_copy.wait()
    width = out_refs[0].shape[1]
    step = 2 * LANES
    for k, out_ref in enumerate(out_refs):
        begin = 0 if outputs == 1 else jnp.where(here == k, width, 0)
        for n in range(0, width, step):
            some = wbuf[:, pl.ds(pl.multiple_of(begin + n, step), step)]
            out_ref[:, n : n + step] = jnp.dot(attended, some, preferred_element_type=f32)


VMEM = pl.BlockSpec(memory_space=pltpu.VMEM)
HBM = pl.BlockSpec(memory_space=pltpu.HBM)


def own_layouts(queries, kv_rows):
    tokens, width = queries.shape
    heads = width // DH
    size = max(heads, PACK)
    f32, bf16 = jnp.float32, jnp.bfloat16
    return pl.pallas_call(
        own_kernel,
        out_shape=[
            jax.ShapeDtypeStruct((tokens * heads, DH), f32),
            jax.ShapeDtypeStruct((tokens, DH), bf16),
            jax.ShapeDtypeStruct((tokens // LANES, VR, LANES), bf16),
            jax.ShapeDtypeStruct((tokens * heads // size, size, DH), bf16),
            jax.ShapeDtypeStruct((tokens * heads // LANES, VR, LANES), f32),
        ],
        in_specs=[VMEM] * 2,
        out_specs=[VMEM] * 5,
        compiler_params=pltpu.CompilerParams(vmem_limit_bytes=16 * 2**20),
        cost_estimate=pl.CostEstimate(flops=10**9, bytes_accessed=4 * 2**20, transcendentals=0),
    )(queries, kv_rows)


def attended_and_projected(own, shards, meta, weight, outputs):
    heads = own[0].shape[0] // own[1].shape[0]
    tokens = own[1].shape[0]
    size = max(heads, PACK)
    f32, bf16 = jnp.float32, jnp.bfloat16
    return pl.pallas_call(
        functools.partial(attention_kernel, len(shards), outputs),
        out_shape=[jax.ShapeDtypeStruct((tokens, weight.shape[1] // outputs), f32)] * outputs,
        in_specs=[pl.BlockSpec(memory_space=pltpu.SMEM)] + [VMEM] * 5 + [HBM] + [VMEM] * len(shards),
        out_specs=[VMEM] * outputs,
        scratch_shapes=[
            pltpu.VMEM((W1, 4 * DH), bf16),
            pltpu.VMEM(weight.shape, bf16),
            pltpu.SemaphoreType.DMA,
            pltpu.VMEM((tokens, DH), bf16),
            pltpu.VMEM((W1, DH), bf16),
            pltpu.VMEM((W1 // LANES, VR, LANES), bf16),
            pltpu.VMEM((tokens // LANES, VR, LANES), bf16),
            pltpu.VMEM(((tokens + W2) * heads // size, size, DH), bf16),
            pltpu.VMEM(((tokens + W2) * heads // LANES, VR, LANES), f32),
            pltpu.VMEM((LANES, DH), bf16),
            pltpu.VMEM((VR, LANES), bf16),
            pltpu.VMEM((tokens, VR, LANES), f32),
            pltpu.VMEM((tokens, 8, LANES), f32),
            pltpu.VMEM((8, LANES), f32),
            pltpu.VMEM((tokens * heads, DH), f32),
        ],
        compiler_params=pltpu.CompilerParams(vmem_limit_bytes=43 * 2**20),
    )(meta, *own, weight, *shards)

HOPS = 3


def shifted(block, axis, distance):
    devices = range(lax.axis_size(axis))
    return lax.ppermute(block, axis, [(i - distance, i) for i in devices if i - distance in devices])


def swapped(block, axis, bits):
    return lax.ppermute(block, axis, [(i, i ^ bits) for i in range(lax.axis_size(axis))])


def collect_window(kv_rows, back, own):
    if lax.axis_size("head") != 2 or back != 4:
        return [shifted(kv_rows, "ctx", back - k) for k in range(back)], own

    def taken(distances):
        devices = range(lax.axis_size("ctx"))
        route = [
            ((i - d) % len(devices) * 2 + h, i * 2 + h) for i in devices for h, d in enumerate(distances)
        ]
        return lax.ppermute(kv_rows, ("ctx", "head"), route)

    parts, own = lax.optimization_barrier(([taken((2, 4)), taken((1, 3))], own))
    held = jnp.concatenate(parts, axis=0)
    return [held, swapped(held, "head", 1)], own


def earlier_alike(devices):
    blocks = devices.shape[-1]
    same = devices[..., :, None] == devices[..., None, :]
    before = np.tril(np.ones((blocks, blocks), bool), -1)
    return jnp.sum(jnp.where(before, same, False).astype(jnp.int32), axis=-1)


def split_kernel(room, index_ref, *refs):
    count = 1 + index_ref.shape[0] // room
    terms, outs = refs[:-count], refs[-count:]

    def rows(where):
        some = terms[0][where, :]
        for term in terms[1:]:
            some = some + term[where, :]
        return some.astype(jnp.bfloat16)

    outs[0][...] = rows(slice(None))
    for r, out in enumerate(outs[1:]):
        for c in range(room):
            block = index_ref[r * room + c]
            out[c * QB : (c + 1) * QB, :] = rows(pl.ds(pl.multiple_of(block * QB, QB), QB))


def split(terms, index, room):
    tokens, width = terms[0].shape
    others = HOPS
    vmem = pl.BlockSpec(memory_space=pltpu.VMEM)
    return pl.pallas_call(
        functools.partial(split_kernel, room),
        out_shape=[jax.ShapeDtypeStruct((tokens, width), jnp.bfloat16)]
        + [jax.ShapeDtypeStruct((room * QB, width), jnp.bfloat16)] * others,
        in_specs=[pl.BlockSpec(memory_space=pltpu.SMEM)] + [vmem] * len(terms),
        out_specs=[vmem] * (others + 1),
        compiler_params=pltpu.CompilerParams(vmem_limit_bytes=16 * 2**20),
    )(index, *terms)


def exchanged(terms, destination, position, blocks):
    group = HOPS + 1
    room = blocks // 2
    tokens = blocks * QB
    place = position % group
    slots = group * blocks
    targets = lax.dynamic_slice_in_dim(destination, (position - place) * blocks, slots, 0)
    order = place ^ np.arange(group, dtype=np.int32)
    known = order[:, None] == np.arange(group, dtype=np.int32)[None, :]
    slot = jnp.sum(
        jnp.where(known[:, :, None], targets.reshape(1, group, blocks), 0), axis=1
    )
    device = slot // blocks % group
    rank = earlier_alike(device)
    places = np.arange(room, dtype=np.int32)
    mine = (device[1:, None, :] == place) & (rank[1:, None, :] == places[None, :, None])
    got = jnp.sum(jnp.where(mine, slot[1:, None, :] + 1, 0), axis=2) - 1
    sent = (device[0][None, None, :] == order[1:, None, None]) & (
        rank[0][None, None, :] == places[None, :, None]
    )
    numbers = np.arange(blocks, dtype=np.int32)
    index = jnp.sum(jnp.where(sent, numbers[None, None, :], 0), axis=2).reshape(-1)
    everywhere = (destination // blocks % group).reshape(-1, blocks)
    few = jnp.max(earlier_alike(everywhere)) < room
    tokens_here = position * tokens + jnp.arange(tokens, dtype=jnp.int32)

    def placed(pieces, block_slots):
        rows = (block_slots[:, None] * QB + np.arange(QB, dtype=np.int32)[None, :]).reshape(-1)
        pick = (rows[:, None] == tokens_here[None, :]).astype(jnp.bfloat16)
        return lax.dot_general(
            jnp.concatenate(pieces, axis=0),
            pick,
            (((0,), (0,)), ((), ())),
            preferred_element_type=jnp.float32,
        ).astype(jnp.bfloat16)

    def some(*terms):
        own, *outgoing = split(terms, index, room)
        pieces = [own] + [swapped(block, "ctx", r + 1) for r, block in enumerate(outgoing)]
        return placed(pieces, jnp.concatenate([slot[0], got.reshape(-1)]))

    def whole(*terms):
        own = sum(terms[1:], terms[0]).astype(jnp.bfloat16)
        pieces = [own] + [swapped(own, "ctx", r) for r in range(1, group)]
        return placed(pieces, slot.reshape(-1))

    return lax.cond(few, some, whole, *terms)


def body(queries, kv_rows, doc_start, destination, out_weight):
    position = lax.axis_index("ctx")
    tokens = queries.shape[0]
    blocks = tokens // QB
    group = HOPS + 1
    back = W1 // tokens
    shards, own = collect_window(kv_rows, back, own_layouts(queries, kv_rows))
    first = position * blocks
    starts = lax.dynamic_slice_in_dim(doc_start, first, blocks, 0)
    own_rows = (first + jnp.arange(blocks, dtype=jnp.int32)) * QB
    inval = jnp.clip(starts - (own_rows - W1), 0, W1).astype(jnp.int32)
    here = lax.axis_index("head").astype(jnp.int32)
    meta = jnp.concatenate([inval, here[None]])
    outputs = 2 if len(shards) == 2 else 1
    partials = attended_and_projected(own, shards, meta, out_weight, outputs)
    if outputs == 2:
        terms = [partials[1], swapped(partials[0], "head", 1)]
    else:
        terms = [lax.psum_scatter(partials[0], "head", scatter_dimension=1, tiled=True)]
    return exchanged(terms, destination, position, blocks)


def solution(mesh):
    in_specs = (P("ctx", "head"), P("ctx", None), P(), P(), P("head", None))
    return jax.shard_map(
        body, mesh=mesh, in_specs=in_specs, out_specs=P("head", "ctx"), check_vma=False
    )
```

```python
import functools

import jax
import jax.numpy as jnp
import numpy as np
from jax import lax
from jax.experimental import pallas as pl
from jax.experimental.pallas import tpu as pltpu
from jax.sharding import PartitionSpec as P

DH = 128
W1 = 512
W2 = 32
QB = 32
LANES = 128
PACK = 16
VR = DH + PACK
SAMPLE = 32
AHEAD = 3
SPAN = 4
LIMIT = 1e30
LOG2E = 1.4426950408889634


def iota(shape, dim):
    return lax.broadcasted_iota(jnp.int32, shape, dim)


def spread(columns, first, heads):
    pick = iota((columns.shape[1], LANES), 0) == first + iota((columns.shape[1], LANES), 1) // heads
    pick = pick.astype(jnp.float32).astype(jnp.bfloat16)
    return jnp.dot(columns, pick, preferred_element_type=jnp.float32)


def with_ones(values):
    return jnp.concatenate(
        [values.astype(jnp.float32).T, jnp.ones((VR - DH, LANES), jnp.float32)], axis=0
    ).astype(jnp.bfloat16)


def own_kernel(q_ref, kv_ref, q3, k1o, v1o, k2o, v2o):
    f32, bf16 = jnp.float32, jnp.bfloat16
    tokens = q_ref.shape[0]
    heads = q_ref.shape[1] // DH
    group = LANES // heads
    k1o[...] = kv_ref[:, :DH]
    second = kv_ref[:, 2 * DH : 3 * DH].astype(f32)
    second = jnp.broadcast_to(second[:, None, :], (tokens, heads, DH))
    k2o[...] = second.reshape(k2o.shape).astype(bf16)
    for k in range(tokens // LANES):
        v1o[k] = with_ones(kv_ref[k * LANES : (k + 1) * LANES, DH : 2 * DH])
        columns = with_ones(kv_ref[k * LANES : (k + 1) * LANES, 3 * DH :])
        for c in range(heads):
            v2o[k * heads + c] = spread(columns, c * group, heads)
    for h in range(heads):
        q3[pl.ds(h, tokens, stride=heads), :] = q_ref[:, h * DH : (h + 1) * DH].astype(f32)


def attention_kernel(pairs, outputs, meta_ref, q3, k1o, v1o, k2o, v2o, w_ref, *refs):
    shards, refs = refs[:pairs], refs[pairs:]
    out_refs, refs = refs[:outputs], refs[outputs:]
    kv_ref, wbuf, wsem, k1n, k1s, v1t, v1n, k2x, v2x, rowid, laneid, part, top2, bad, rows = refs
    tokens = k1o.shape[0]
    heads = q3.shape[0] // tokens
    cols = W2 * heads
    group = LANES // heads
    tiles = tokens // LANES
    near_tiles = cols // LANES
    size = max(heads, PACK)
    pack = size // heads
    wide = min(2 * LANES, cols)
    span = min(SPAN, QB // group)
    scale = LOG2E / np.sqrt(DH)
    f32, bf16 = jnp.float32, jnp.bfloat16

    def either(cond, a, b):
        if isinstance(cond, bool):
            return a if cond else b
        return jnp.where(cond, a, b)

    weight_copy = pltpu.make_async_copy(w_ref, wbuf, wsem)
    weight_copy.start()
    blocks = tokens // QB
    here = meta_ref[blocks]

    def lay(order):
        at = 0
        for ref in order:
            kv_ref[at : at + ref.shape[0], :] = ref[...]
            at += ref.shape[0]

    if outputs == 2:

        @pl.when(here == 0)
        def _():
            lay(shards[::-1])

        @pl.when(here != 0)
        def _():
            lay(shards)

    else:
        lay(shards)

    def prepare():
        rowid[...] = iota(rowid.shape, 0).astype(f32).astype(bf16)
        laneid[...] = iota(laneid.shape, 1).astype(f32).astype(bf16)
        bad[...] = jnp.zeros_like(bad)
        k1n[...] = k1o[...]
        v1n[...] = v1o[...]
        second = kv_ref[W1 - W2 :, 2 * DH : 3 * DH].astype(f32)
        second = jnp.broadcast_to(second[:, None, :], (W2, heads, DH))
        k2x[: W2 // pack] = second.reshape(W2 // pack, size, DH).astype(bf16)
        k2x[W2 // pack :] = k2o[...]
        columns = with_ones(kv_ref[W1 - LANES :, 3 * DH :])
        for k in range(near_tiles):
            v2x[k] = spread(columns, LANES - W2 + k * group, heads)
        v2x[near_tiles:] = v2o[...]

    def reset(t, inv):
        kt = k1o[pl.ds(pl.multiple_of(t, PACK), PACK), :].astype(f32)[:1]
        window = kv_ref[:, : 2 * DH].astype(f32)
        ok = iota((W1, DH), 0) >= inv
        k1s[...] = jnp.where(ok, window[:, :DH], kt).astype(bf16)
        values = jnp.where(ok, window[:, DH:], 0.0)
        for k in range(W1 // LANES):
            v1t[k, :DH] = values[k * LANES : (k + 1) * LANES].T.astype(bf16)
            live = k * LANES + iota((VR - DH, LANES), 1) >= inv
            v1t[k, DH:] = live.astype(f32).astype(bf16)
        k1n[...] = jnp.where(iota((tokens, DH), 0) < t, kt, k1n[...].astype(f32)).astype(bf16)
        for k in range(tiles):
            gone = k * LANES + iota((VR, LANES), 1) < t
            v1n[k] = jnp.where(gone, 0.0, v1n[k].astype(f32)).astype(bf16)

        @pl.when(inv == W1)
        def _():
            fill = jnp.broadcast_to(k2x[(t + W2) // pack].astype(f32)[:1], (size, DH)).astype(bf16)
            for s in range(W2 // pack):
                k2x[t // pack + s] = fill
            for k in range(near_tiles):
                v2x[t // group + k] = jnp.zeros((VR, LANES), f32)

    def scores(g, u):
        t = g * group + u
        mark = t.astype(f32).astype(bf16)
        keys = [
            jnp.where(rowid[...] + (k * LANES) <= mark, k1n[k * LANES : (k + 1) * LANES], k1s[k * LANES : (k + 1) * LANES])
            for k in range(tiles)
        ]
        keys = jnp.concatenate(keys + [k1s[tokens:]], axis=0)
        query = q3[pl.ds(t * heads, heads), :]
        if heads < PACK:
            query = jnp.concatenate([query] * pack, axis=0)
        query = query.astype(bf16)
        base = g * (group // pack)
        for n in range(0, cols, wide):
            paired = []
            for s in range(n // size, (n + wide) // size):
                if s * pack >= group:
                    near_keys = k2x[base + s]
                elif pack == 1:
                    near_keys = k2x[base + either(s <= u, s + W2, s)]
                else:
                    token = s * pack + iota((size, DH), 0) // heads
                    after = k2x[base + s + W2 // pack].astype(f32)
                    near_keys = jnp.where(token <= u, after, k2x[base + s].astype(f32)).astype(bf16)
                paired.append(near_keys * query)
            yield lax.dot_general(
                keys,
                jnp.concatenate(paired, axis=0),
                (((1,), (1,)), ((), ())),
                preferred_element_type=f32,
            )

    def highest(logits, best=None):
        top = jnp.max(logits, axis=0, keepdims=True)
        for k in range(0, wide, LANES):
            some = top[:, k : k + LANES]
            best = some if best is None else jnp.maximum(best, some)
        return best

    def mix(g, u, n, logits, top):
        mark = (g * group + u).astype(f32).astype(bf16)
        values = [
            jnp.where(laneid[...] + (k * LANES) <= mark, v1n[k], v1t[k]) for k in range(tiles)
        ] + [v1t[k] for k in range(tiles, W1 // LANES)]
        tops = jnp.concatenate([top] * (wide // LANES), axis=1)
        product = None
        for k in range(0, W1, 2 * LANES):
            weights = jnp.exp2(logits[k : k + 2 * LANES] * scale - tops).astype(bf16)
            two = jnp.concatenate(values[k // LANES : k // LANES + 2], axis=1)
            some = jnp.dot(two, weights, preferred_element_type=f32)
            product = some if product is None else product + some
        total = None
        for c in range(0, wide, LANES):
            k = (n + c) // LANES
            near = v2x[g + k]
            if k == 0:
                near = jnp.where(iota((VR, LANES), 1) // heads <= u, v2x[g + near_tiles], near)
            some = product[:, c : c + LANES] * near
            total = some if total is None else total + some
        return total

    def keep(g, u, total, top):
        part[g * group + u] = total
        top2[g * group + u] = jnp.broadcast_to(top, (8, LANES))
        bad[...] = jnp.where(total[DH : DH + 8] < LIMIT, bad[...], 1.0)

    def finish(g):
        lane = iota((VR, LANES), 1)
        sums = []
        for u in range(group):
            top = top2[g * group + u]
            best = top
            shift = LANES // 2
            while shift >= heads:
                best = jnp.maximum(best, pltpu.roll(best, shift, 1))
                shift //= 2
            sums.append(part[g * group + u] * jnp.exp2(top - best)[:1])
        shift = heads
        while shift < LANES:
            low = lane % (2 * shift) < shift
            sums = [
                jnp.where(low, a, b) + pltpu.roll(jnp.where(low, b, a), shift, 1)
                for a, b in zip(sums[::2], sums[1::2])
            ]
            shift *= 2
        value = sums[0][:DH] * (1.0 / sums[0][DH : DH + 1])
        spot = (meta_ref[blocks + 1 + g * group // QB] * QB + g * group % QB) * heads
        rows[pl.ds(pl.multiple_of(spot, LANES), LANES), :] = value.T

    def run(exact):
        prepare()

        def block(b, _):
            inv = meta_ref[b]
            g0 = b * (QB // group)

            @pl.when((b == 0) | (inv == W1))
            def _():
                reset(b * QB, inv)

            def fast(s, _):
                work = []
                for u in range(span * group):
                    work += [(u, n) for n in range(0, cols, wide)]
                at = [divmod(u, group) for u in range(span * group)]
                first = g0 + s * span
                source = [scores(first + k, u) for k, u in at]
                top = total = None
                ahead = [next(source[u]) for u, n in work[:AHEAD]]
                for i, (u, n) in enumerate(work):
                    if i + AHEAD < len(work):
                        ahead.append(next(source[work[i + AHEAD][0]]))
                    logits = ahead.pop(0)
                    g, v = first + at[u][0], at[u][1]
                    if n == 0:
                        top = highest(logits[:SAMPLE]) * scale
                        total = None
                    some = mix(g, v, n, logits, top)
                    total = some if total is None else total + some
                    if n + wide == cols:
                        keep(g, v, total, top)
                        if v == group // 2:
                            finish(jnp.maximum(g - 1, 0))
                return 0

            def slow(s, _):
                g, u = g0 + s // group, s % group
                best = None
                for logits in scores(g, u):
                    best = highest(logits, best)
                total = None
                for n, logits in zip(range(0, cols, wide), scores(g, u)):
                    some = mix(g, u, n, logits, best * scale)
                    total = some if total is None else total + some
                keep(g, u, total, best * scale)
                return 0

            if exact:
                return lax.fori_loop(0, QB, slow, 0)
            return lax.fori_loop(0, QB // group // span, fast, 0)

        lax.fori_loop(0, tokens // QB, block, 0)
        if exact:
            lax.fori_loop(0, tokens // group - 1, lambda g, _: finish(g) or 0, 0)
        finish(jnp.int32(tokens // group - 1))

    run(False)

    @pl.when(jnp.max(bad[...]) > 0)
    def _():
        run(True)

    attended = jnp.concatenate(
        [rows[pl.ds(h, tokens, stride=heads), :].astype(bf16) for h in range(heads)], axis=1
    )
    weight_copy.wait()
    width = out_refs[0].shape[1]
    step = 2 * LANES
    for k, out_ref in enumerate(out_refs):
        begin = 0 if outputs == 1 else jnp.where(here == k, width, 0)
        for n in range(0, width, step):
            some = wbuf[:, pl.ds(pl.multiple_of(begin + n, step), step)]
            some = jnp.dot(attended, some, preferred_element_type=f32)
            out_ref[:, n : n + step] = some.astype(out_ref.dtype)


VMEM = pl.BlockSpec(memory_space=pltpu.VMEM)
HBM = pl.BlockSpec(memory_space=pltpu.HBM)


def own_layouts(queries, kv_rows):
    tokens, width = queries.shape
    heads = width // DH
    size = max(heads, PACK)
    f32, bf16 = jnp.float32, jnp.bfloat16
    return pl.pallas_call(
        own_kernel,
        out_shape=[
            jax.ShapeDtypeStruct((tokens * heads, DH), f32),
            jax.ShapeDtypeStruct((tokens, DH), bf16),
            jax.ShapeDtypeStruct((tokens // LANES, VR, LANES), bf16),
            jax.ShapeDtypeStruct((tokens * heads // size, size, DH), bf16),
            jax.ShapeDtypeStruct((tokens * heads // LANES, VR, LANES), f32),
        ],
        in_specs=[VMEM] * 2,
        out_specs=[VMEM] * 5,
        compiler_params=pltpu.CompilerParams(vmem_limit_bytes=16 * 2**20),
        cost_estimate=pl.CostEstimate(flops=10**9, bytes_accessed=4 * 2**20, transcendentals=0),
    )(queries, kv_rows)


def attended_and_projected(own, shards, meta, weight, outputs):
    heads = own[0].shape[0] // own[1].shape[0]
    tokens = own[1].shape[0]
    size = max(heads, PACK)
    f32, bf16 = jnp.float32, jnp.bfloat16
    return pl.pallas_call(
        functools.partial(attention_kernel, len(shards), outputs),
        out_shape=[
            jax.ShapeDtypeStruct((tokens, weight.shape[1] // outputs), kind)
            for kind in (bf16, f32)[2 - outputs :]
        ],
        in_specs=[pl.BlockSpec(memory_space=pltpu.SMEM)] + [VMEM] * 5 + [HBM] + [VMEM] * len(shards),
        out_specs=[VMEM] * outputs,
        scratch_shapes=[
            pltpu.VMEM((W1, 4 * DH), bf16),
            pltpu.VMEM(weight.shape, bf16),
            pltpu.SemaphoreType.DMA,
            pltpu.VMEM((tokens, DH), bf16),
            pltpu.VMEM((W1, DH), bf16),
            pltpu.VMEM((W1 // LANES, VR, LANES), bf16),
            pltpu.VMEM((tokens // LANES, VR, LANES), bf16),
            pltpu.VMEM(((tokens + W2) * heads // size, size, DH), bf16),
            pltpu.VMEM(((tokens + W2) * heads // LANES, VR, LANES), f32),
            pltpu.VMEM((LANES, DH), bf16),
            pltpu.VMEM((VR, LANES), bf16),
            pltpu.VMEM((tokens, VR, LANES), f32),
            pltpu.VMEM((tokens, 8, LANES), f32),
            pltpu.VMEM((8, LANES), f32),
            pltpu.VMEM((tokens * heads, DH), f32),
        ],
        compiler_params=pltpu.CompilerParams(vmem_limit_bytes=43 * 2**20),
    )(meta, *own, weight, *shards)

HOPS = 3


def shifted(block, axis, distance):
    devices = range(lax.axis_size(axis))
    return lax.ppermute(block, axis, [(i - distance, i) for i in devices if i - distance in devices])


def swapped(block, axis, bits):
    return lax.ppermute(block, axis, [(i, i ^ bits) for i in range(lax.axis_size(axis))])


def collect_window(kv_rows, back, own):
    if lax.axis_size("head") != 2 or back != 4:
        return [shifted(kv_rows, "ctx", back - k) for k in range(back)], own

    def taken(distances):
        devices = range(lax.axis_size("ctx"))
        route = [
            ((i - d) % len(devices) * 2 + h, i * 2 + h) for i in devices for h, d in enumerate(distances)
        ]
        return lax.ppermute(kv_rows, ("ctx", "head"), route)

    parts, own = lax.optimization_barrier(([taken((2, 4)), taken((1, 3))], own))
    held = jnp.concatenate(parts, axis=0)
    return [held, swapped(held, "head", 1)], own


def sorted_places(keys):
    blocks = keys.shape[-1]
    before = np.tril(np.ones((blocks, blocks), bool), -1)
    mine, other = keys[..., :, None], keys[..., None, :]
    return jnp.sum(((other < mine) | ((other == mine) & before)).astype(jnp.int32), axis=-1)


class Exchange:
    def __init__(self, destination, position, blocks):
        group = HOPS + 1
        self.blocks, self.room = blocks, blocks // 2
        self.position = position
        place = position % group
        near = lax.dynamic_slice_in_dim(destination, (position - place) * blocks, group * blocks, 0)
        order = place ^ np.arange(group, dtype=np.int32)
        known = order[:, None] == np.arange(group, dtype=np.int32)[None, :]
        slot = jnp.sum(jnp.where(known[:, :, None], near.reshape(1, group, blocks), 0), axis=1)
        distance = (slot // blocks % group) ^ order[:, None]
        places = sorted_places(distance)
        self.places = places[0]
        numbers = np.arange(blocks, dtype=np.int32)
        here = places[:, None, :] == numbers[None, :, None]
        slots = jnp.sum(jnp.where(here, slot[:, None, :], 0), axis=2)

        def starts(distances, limits):
            nearer = jnp.sum((distances < limits[:, None]).astype(jnp.int32), axis=1)
            return jnp.minimum(nearer, blocks - self.room)

        swaps = np.arange(1, group, dtype=np.int32)
        start = starts(distance[:1], swaps)
        first = starts(distance[1:], swaps)[:, None, None]
        window = first + np.arange(self.room, dtype=np.int32)[None, :, None] == numbers[None, None, :]
        got = jnp.sum(jnp.where(window, slots[1:, None, :], 0), axis=2)
        to = (destination // blocks % group).reshape(-1, blocks)
        counts = jnp.sum((to[:, :, None] == to[:, None, :]).astype(jnp.int32), axis=2)
        few = jnp.max(counts) <= self.room

        def rows(slots):
            return (slots[:, None] * QB + np.arange(QB, dtype=np.int32)[None, :]).reshape(-1)

        self.plan = (
            [start[r] for r in range(HOPS)],
            rows(jnp.concatenate([slots[0], got.reshape(-1)])),
            rows(slots.reshape(-1)),
            few,
        )

    def placed(self, pieces, rows):
        tokens = self.blocks * QB
        stored = self.position * tokens + jnp.arange(tokens, dtype=jnp.int32)
        pick = (rows[:, None] == stored[None, :]).astype(jnp.bfloat16)
        return lax.dot_general(
            jnp.concatenate(pieces, axis=0),
            pick,
            (((0,), (0,)), ((), ())),
            preferred_element_type=jnp.float32,
        ).astype(jnp.bfloat16)

    def __call__(self, terms, plan):
        start, some_rows, whole_rows, few = plan

        def added(terms):
            return sum((term.astype(jnp.float32) for term in terms[1:]), terms[0]).astype(jnp.bfloat16)

        def some(*terms):
            own = added(terms)
            pieces = [own]
            for r in range(HOPS):
                rows = lax.dynamic_slice_in_dim(own, start[r] * QB, self.room * QB, 0)
                pieces.append(swapped(rows, "ctx", r + 1))
            return self.placed(pieces, some_rows)

        def whole(*terms):
            own = added(terms)
            pieces = [own] + [swapped(own, "ctx", r) for r in range(1, HOPS + 1)]
            return self.placed(pieces, whole_rows)

        return lax.cond(few, some, whole, *terms)


def body(queries, kv_rows, doc_start, destination, out_weight):
    position = lax.axis_index("ctx")
    tokens = queries.shape[0]
    blocks = tokens // QB
    group = HOPS + 1
    back = W1 // tokens
    shards, own = collect_window(kv_rows, back, own_layouts(queries, kv_rows))
    first = position * blocks
    starts = lax.dynamic_slice_in_dim(doc_start, first, blocks, 0)
    own_rows = (first + jnp.arange(blocks, dtype=jnp.int32)) * QB
    inval = jnp.clip(starts - (own_rows - W1), 0, W1).astype(jnp.int32)
    here = lax.axis_index("head").astype(jnp.int32)
    exchange = Exchange(destination, position, blocks)
    meta = jnp.concatenate([inval, here[None], exchange.places])
    outputs = 2 if len(shards) == 2 else 1
    partials = attended_and_projected(own, shards, meta, out_weight, outputs)
    partials, plan = lax.optimization_barrier((partials, exchange.plan))
    if outputs == 2:
        terms = [partials[1], swapped(partials[0], "head", 1)]
    else:
        terms = [lax.psum_scatter(partials[0], "head", scatter_dimension=1, tiled=True)]
    return exchange(terms, plan)


def solution(mesh):
    in_specs = (P("ctx", "head"), P("ctx", None), P(), P(), P("head", None))
    return jax.shard_map(
        body, mesh=mesh, in_specs=in_specs, out_specs=P("head", "ctx"), check_vma=False
    )
```

```python
import functools

import jax
import jax.numpy as jnp
import numpy as np
from jax import lax
from jax.experimental import pallas as pl
from jax.experimental.pallas import tpu as pltpu
from jax.sharding import PartitionSpec as P

DH = 128
W1 = 512
W2 = 32
QB = 32
LANES = 128
PACK = 16
VR = DH + PACK
SAMPLE = 32
AHEAD = 3
SPAN = 4
LIMIT = 1e30
LOG2E = 1.4426950408889634


def iota(shape, dim):
    return lax.broadcasted_iota(jnp.int32, shape, dim)


def spread(columns, first, heads):
    pick = iota((columns.shape[1], LANES), 0) == first + iota((columns.shape[1], LANES), 1) // heads
    pick = pick.astype(jnp.float32).astype(jnp.bfloat16)
    return jnp.dot(columns, pick, preferred_element_type=jnp.float32)


def with_ones(values):
    return jnp.concatenate(
        [values.astype(jnp.float32).T, jnp.ones((VR - DH, LANES), jnp.float32)], axis=0
    ).astype(jnp.bfloat16)


GROUP = 4


def plan_places(blocks):
    room = blocks // 2
    sizes = (blocks, 1, blocks, GROUP - 1, 1, blocks + (GROUP - 1) * room, GROUP * blocks)
    return [sum(sizes[:k]) for k in range(len(sizes) + 1)]


def make_plan(table_ref, plan_ref, blocks):
    room = blocks // 2
    position, here = table_ref[0], table_ref[1]
    total = (table_ref.shape[0] - 2) // 2
    target = 2 + total
    place = lax.rem(position, GROUP)
    masked, head, order, sent, small, some, whole, _ = plan_places(blocks)
    one, zero = jnp.int32(1), jnp.int32(0)
    for k in range(blocks):
        block = position * blocks + k
        outside = table_ref[2 + block] - (block * QB - W1)
        plan_ref[masked + k] = jnp.clip(outside, 0, W1)
    plan_ref[head] = here
    for r in range(GROUP):
        source = lax.bitwise_xor(place, jnp.int32(r))
        slots = [table_ref[target + (position - place + source) * blocks + k] for k in range(blocks)]
        far = [lax.bitwise_xor(lax.rem(lax.div(s, blocks), GROUP), source) for s in slots]
        for k in range(blocks):
            at = zero
            for j in range(blocks):
                if j != k:
                    ahead = far[j] <= far[k] if j < k else far[j] < far[k]
                    at = at + jnp.where(ahead, one, zero)
            plan_ref[whole + r * blocks + at] = slots[k]
            if r == 0:
                plan_ref[order + k] = at
        for distance in range(1, GROUP) if r == 0 else (r,):
            nearer = zero
            for k in range(blocks):
                nearer = nearer + jnp.where(far[k] < distance, one, zero)
            nearer = jnp.minimum(nearer, blocks - room)
            if r == 0:
                plan_ref[sent + distance - 1] = nearer
            else:
                for c in range(room):
                    into = some + blocks + (r - 1) * room + c
                    plan_ref[into] = plan_ref[whole + r * blocks + nearer + c]
    for k in range(blocks):
        plan_ref[some + k] = plan_ref[whole + k]

    def most(device, so_far):
        to = [lax.rem(lax.div(table_ref[target + device * blocks + k], blocks), GROUP) for k in range(blocks)]
        for k in range(blocks):
            alike = one
            for j in range(blocks):
                if j != k:
                    alike = alike + jnp.where(to[j] == to[k], one, zero)
            so_far = jnp.maximum(so_far, alike)
        return so_far

    alike = lax.fori_loop(0, total // blocks, most, zero)
    plan_ref[small] = jnp.where(alike <= room, one, zero)


def own_kernel(table_ref, q_ref, kv_ref, q3, k1o, v1o, k2o, v2o, plan_ref):
    make_plan(table_ref, plan_ref, q_ref.shape[0] // QB)
    f32, bf16 = jnp.float32, jnp.bfloat16
    tokens = q_ref.shape[0]
    heads = q_ref.shape[1] // DH
    group = LANES // heads
    k1o[...] = kv_ref[:, :DH]
    second = kv_ref[:, 2 * DH : 3 * DH].astype(f32)
    second = jnp.broadcast_to(second[:, None, :], (tokens, heads, DH))
    k2o[...] = second.reshape(k2o.shape).astype(bf16)
    for k in range(tokens // LANES):
        v1o[k] = with_ones(kv_ref[k * LANES : (k + 1) * LANES, DH : 2 * DH])
        columns = with_ones(kv_ref[k * LANES : (k + 1) * LANES, 3 * DH :])
        for c in range(heads):
            v2o[k * heads + c] = spread(columns, c * group, heads)
    for h in range(heads):
        q3[pl.ds(h, tokens, stride=heads), :] = q_ref[:, h * DH : (h + 1) * DH].astype(f32)


def attention_kernel(pairs, outputs, plan_ref, q3, k1o, v1o, k2o, v2o, w_ref, *refs):
    shards, refs = refs[:pairs], refs[pairs:]
    out_refs, refs = refs[:outputs], refs[outputs:]
    kv_ref, wbuf, wsem, k1n, k1s, v1t, v1n, k2x, v2x, rowid, laneid, part, top2, bad, rows = refs
    tokens = k1o.shape[0]
    heads = q3.shape[0] // tokens
    cols = W2 * heads
    group = LANES // heads
    tiles = tokens // LANES
    near_tiles = cols // LANES
    size = max(heads, PACK)
    pack = size // heads
    wide = min(2 * LANES, cols)
    span = min(SPAN, QB // group)
    scale = LOG2E / np.sqrt(DH)
    f32, bf16 = jnp.float32, jnp.bfloat16

    def either(cond, a, b):
        if isinstance(cond, bool):
            return a if cond else b
        return jnp.where(cond, a, b)

    weight_copy = pltpu.make_async_copy(w_ref, wbuf, wsem)
    weight_copy.start()
    blocks = tokens // QB
    masked, head, order = plan_places(blocks)[:3]
    here = plan_ref[head]

    def lay(order):
        at = 0
        for ref in order:
            kv_ref[at : at + ref.shape[0], :] = ref[...]
            at += ref.shape[0]

    if outputs == 2:

        @pl.when(here == 0)
        def _():
            lay(shards[::-1])

        @pl.when(here != 0)
        def _():
            lay(shards)

    else:
        lay(shards)

    def prepare():
        rowid[...] = iota(rowid.shape, 0).astype(f32).astype(bf16)
        laneid[...] = iota(laneid.shape, 1).astype(f32).astype(bf16)
        bad[...] = jnp.zeros_like(bad)
        k1n[...] = k1o[...]
        v1n[...] = v1o[...]
        second = kv_ref[W1 - W2 :, 2 * DH : 3 * DH].astype(f32)
        second = jnp.broadcast_to(second[:, None, :], (W2, heads, DH))
        k2x[: W2 // pack] = second.reshape(W2 // pack, size, DH).astype(bf16)
        k2x[W2 // pack :] = k2o[...]
        columns = with_ones(kv_ref[W1 - LANES :, 3 * DH :])
        for k in range(near_tiles):
            v2x[k] = spread(columns, LANES - W2 + k * group, heads)
        v2x[near_tiles:] = v2o[...]

    def reset(t, inv):
        kt = k1o[pl.ds(pl.multiple_of(t, PACK), PACK), :].astype(f32)[:1]
        window = kv_ref[:, : 2 * DH].astype(f32)
        ok = iota((W1, DH), 0) >= inv
        k1s[...] = jnp.where(ok, window[:, :DH], kt).astype(bf16)
        values = jnp.where(ok, window[:, DH:], 0.0)
        for k in range(W1 // LANES):
            v1t[k, :DH] = values[k * LANES : (k + 1) * LANES].T.astype(bf16)
            live = k * LANES + iota((VR - DH, LANES), 1) >= inv
            v1t[k, DH:] = live.astype(f32).astype(bf16)
        k1n[...] = jnp.where(iota((tokens, DH), 0) < t, kt, k1n[...].astype(f32)).astype(bf16)
        for k in range(tiles):
            gone = k * LANES + iota((VR, LANES), 1) < t
            v1n[k] = jnp.where(gone, 0.0, v1n[k].astype(f32)).astype(bf16)

        @pl.when(inv == W1)
        def _():
            fill = jnp.broadcast_to(k2x[(t + W2) // pack].astype(f32)[:1], (size, DH)).astype(bf16)
            for s in range(W2 // pack):
                k2x[t // pack + s] = fill
            for k in range(near_tiles):
                v2x[t // group + k] = jnp.zeros((VR, LANES), f32)

    def scores(g, u):
        t = g * group + u
        mark = t.astype(f32).astype(bf16)
        keys = [
            jnp.where(rowid[...] + (k * LANES) <= mark, k1n[k * LANES : (k + 1) * LANES], k1s[k * LANES : (k + 1) * LANES])
            for k in range(tiles)
        ]
        keys = jnp.concatenate(keys + [k1s[tokens:]], axis=0)
        query = q3[pl.ds(t * heads, heads), :]
        if heads < PACK:
            query = jnp.concatenate([query] * pack, axis=0)
        query = query.astype(bf16)
        base = g * (group // pack)
        for n in range(0, cols, wide):
            paired = []
            for s in range(n // size, (n + wide) // size):
                if s * pack >= group:
                    near_keys = k2x[base + s]
                elif pack == 1:
                    near_keys = k2x[base + either(s <= u, s + W2, s)]
                else:
                    token = s * pack + iota((size, DH), 0) // heads
                    after = k2x[base + s + W2 // pack].astype(f32)
                    near_keys = jnp.where(token <= u, after, k2x[base + s].astype(f32)).astype(bf16)
                paired.append(near_keys * query)
            yield lax.dot_general(
                keys,
                jnp.concatenate(paired, axis=0),
                (((1,), (1,)), ((), ())),
                preferred_element_type=f32,
            )

    def highest(logits, best=None):
        top = jnp.max(logits, axis=0, keepdims=True)
        for k in range(0, wide, LANES):
            some = top[:, k : k + LANES]
            best = some if best is None else jnp.maximum(best, some)
        return best

    def mix(g, u, n, logits, top):
        mark = (g * group + u).astype(f32).astype(bf16)
        values = [
            jnp.where(laneid[...] + (k * LANES) <= mark, v1n[k], v1t[k]) for k in range(tiles)
        ] + [v1t[k] for k in range(tiles, W1 // LANES)]
        tops = jnp.concatenate([top] * (wide // LANES), axis=1)
        product = None
        for k in range(0, W1, 2 * LANES):
            weights = jnp.exp2(logits[k : k + 2 * LANES] * scale - tops).astype(bf16)
            two = jnp.concatenate(values[k // LANES : k // LANES + 2], axis=1)
            some = jnp.dot(two, weights, preferred_element_type=f32)
            product = some if product is None else product + some
        total = None
        for c in range(0, wide, LANES):
            k = (n + c) // LANES
            near = v2x[g + k]
            if k == 0:
                near = jnp.where(iota((VR, LANES), 1) // heads <= u, v2x[g + near_tiles], near)
            some = product[:, c : c + LANES] * near
            total = some if total is None else total + some
        return total

    def keep(g, u, total, top):
        part[g * group + u] = total
        top2[g * group + u] = jnp.broadcast_to(top, (8, LANES))
        bad[...] = jnp.where(total[DH : DH + 8] < LIMIT, bad[...], 1.0)

    def finish(g):
        lane = iota((VR, LANES), 1)
        sums = []
        for u in range(group):
            top = top2[g * group + u]
            best = top
            shift = LANES // 2
            while shift >= heads:
                best = jnp.maximum(best, pltpu.roll(best, shift, 1))
                shift //= 2
            sums.append(part[g * group + u] * jnp.exp2(top - best)[:1])
        shift = heads
        while shift < LANES:
            low = lane % (2 * shift) < shift
            sums = [
                jnp.where(low, a, b) + pltpu.roll(jnp.where(low, b, a), shift, 1)
                for a, b in zip(sums[::2], sums[1::2])
            ]
            shift *= 2
        value = sums[0][:DH] * (1.0 / sums[0][DH : DH + 1])
        spot = (plan_ref[order + g * group // QB] * QB + g * group % QB) * heads
        rows[pl.ds(pl.multiple_of(spot, LANES), LANES), :] = value.T

    def run(exact):
        prepare()

        def block(b, _):
            inv = plan_ref[masked + b]
            g0 = b * (QB // group)

            @pl.when((b == 0) | (inv == W1))
            def _():
                reset(b * QB, inv)

            def fast(s, _):
                work = []
                for u in range(span * group):
                    work += [(u, n) for n in range(0, cols, wide)]
                at = [divmod(u, group) for u in range(span * group)]
                first = g0 + s * span
                source = [scores(first + k, u) for k, u in at]
                top = total = None
                ahead = [next(source[u]) for u, n in work[:AHEAD]]
                for i, (u, n) in enumerate(work):
                    if i + AHEAD < len(work):
                        ahead.append(next(source[work[i + AHEAD][0]]))
                    logits = ahead.pop(0)
                    g, v = first + at[u][0], at[u][1]
                    if n == 0:
                        top = highest(logits[:SAMPLE]) * scale
                        total = None
                    some = mix(g, v, n, logits, top)
                    total = some if total is None else total + some
                    if n + wide == cols:
                        keep(g, v, total, top)
                        if v == group // 2:
                            finish(jnp.maximum(g - 1, 0))
                return 0

            def slow(s, _):
                g, u = g0 + s // group, s % group
                best = None
                for logits in scores(g, u):
                    best = highest(logits, best)
                total = None
                for n, logits in zip(range(0, cols, wide), scores(g, u)):
                    some = mix(g, u, n, logits, best * scale)
                    total = some if total is None else total + some
                keep(g, u, total, best * scale)
                return 0

            if exact:
                return lax.fori_loop(0, QB, slow, 0)
            return lax.fori_loop(0, QB // group // span, fast, 0)

        lax.fori_loop(0, tokens // QB, block, 0)
        if exact:
            lax.fori_loop(0, tokens // group - 1, lambda g, _: finish(g) or 0, 0)
        finish(jnp.int32(tokens // group - 1))

    run(False)

    @pl.when(jnp.max(bad[...]) > 0)
    def _():
        run(True)

    attended = jnp.concatenate(
        [rows[pl.ds(h, tokens, stride=heads), :].astype(bf16) for h in range(heads)], axis=1
    )
    weight_copy.wait()
    width = out_refs[0].shape[1]
    step = 2 * LANES
    for k, out_ref in enumerate(out_refs):
        begin = 0 if outputs == 1 else jnp.where(here == k, width, 0)
        for n in range(0, width, step):
            some = wbuf[:, pl.ds(pl.multiple_of(begin + n, step), step)]
            out_ref[:, n : n + step] = jnp.dot(attended, some, preferred_element_type=f32)


VMEM = pl.BlockSpec(memory_space=pltpu.VMEM)
HBM = pl.BlockSpec(memory_space=pltpu.HBM)
SMEM = pl.BlockSpec(memory_space=pltpu.SMEM)


def own_layouts(table, queries, kv_rows):
    tokens, width = queries.shape
    heads = width // DH
    size = max(heads, PACK)
    f32, bf16 = jnp.float32, jnp.bfloat16
    return pl.pallas_call(
        own_kernel,
        out_shape=[
            jax.ShapeDtypeStruct((tokens * heads, DH), f32),
            jax.ShapeDtypeStruct((tokens, DH), bf16),
            jax.ShapeDtypeStruct((tokens // LANES, VR, LANES), bf16),
            jax.ShapeDtypeStruct((tokens * heads // size, size, DH), bf16),
            jax.ShapeDtypeStruct((tokens * heads // LANES, VR, LANES), f32),
            jax.ShapeDtypeStruct((plan_places(tokens // QB)[-1],), jnp.int32),
        ],
        in_specs=[SMEM] + [VMEM] * 2,
        out_specs=[VMEM] * 5 + [SMEM],
        compiler_params=pltpu.CompilerParams(vmem_limit_bytes=16 * 2**20),
        cost_estimate=pl.CostEstimate(flops=10**9, bytes_accessed=4 * 2**20, transcendentals=0),
    )(table, queries, kv_rows)


def attended_and_projected(own, shards, plan, weight, outputs):
    heads = own[0].shape[0] // own[1].shape[0]
    tokens = own[1].shape[0]
    size = max(heads, PACK)
    f32, bf16 = jnp.float32, jnp.bfloat16
    return pl.pallas_call(
        functools.partial(attention_kernel, len(shards), outputs),
        out_shape=[jax.ShapeDtypeStruct((tokens, weight.shape[1] // outputs), f32)] * outputs,
        in_specs=[SMEM] + [VMEM] * 5 + [HBM] + [VMEM] * len(shards),
        out_specs=[VMEM] * outputs,
        scratch_shapes=[
            pltpu.VMEM((W1, 4 * DH), bf16),
            pltpu.VMEM(weight.shape, bf16),
            pltpu.SemaphoreType.DMA,
            pltpu.VMEM((tokens, DH), bf16),
            pltpu.VMEM((W1, DH), bf16),
            pltpu.VMEM((W1 // LANES, VR, LANES), bf16),
            pltpu.VMEM((tokens // LANES, VR, LANES), bf16),
            pltpu.VMEM(((tokens + W2) * heads // size, size, DH), bf16),
            pltpu.VMEM(((tokens + W2) * heads // LANES, VR, LANES), f32),
            pltpu.VMEM((LANES, DH), bf16),
            pltpu.VMEM((VR, LANES), bf16),
            pltpu.VMEM((tokens, VR, LANES), f32),
            pltpu.VMEM((tokens, 8, LANES), f32),
            pltpu.VMEM((8, LANES), f32),
            pltpu.VMEM((tokens * heads, DH), f32),
        ],
        compiler_params=pltpu.CompilerParams(vmem_limit_bytes=43 * 2**20),
    )(plan, *own, weight, *shards)

def shifted(block, axis, distance):
    devices = range(lax.axis_size(axis))
    return lax.ppermute(block, axis, [(i - distance, i) for i in devices if i - distance in devices])


def swapped(block, axis, bits):
    return lax.ppermute(block, axis, [(i, i ^ bits) for i in range(lax.axis_size(axis))])


def collect_window(kv_rows, back, own):
    if lax.axis_size("head") != 2 or back != 4:
        return [shifted(kv_rows, "ctx", back - k) for k in range(back)], own

    def taken(distances):
        devices = range(lax.axis_size("ctx"))
        route = [
            ((i - d) % len(devices) * 2 + h, i * 2 + h) for i in devices for h, d in enumerate(distances)
        ]
        return lax.ppermute(kv_rows, ("ctx", "head"), route)

    parts, own = lax.optimization_barrier(([taken((2, 4)), taken((1, 3))], own))
    held = jnp.concatenate(parts, axis=0)
    return [held, swapped(held, "head", 1)], own


def exchanged(terms, plan, position, blocks):
    room = blocks // 2
    start, some_slots, whole_slots, few = plan

    def added(terms):
        return sum(terms[1:], terms[0]).astype(jnp.bfloat16)

    def placed(pieces, slots):
        tokens = blocks * QB
        rows = (slots[:, None] * QB + np.arange(QB, dtype=np.int32)[None, :]).reshape(-1)
        stored = position * tokens + jnp.arange(tokens, dtype=jnp.int32)
        pick = (rows[:, None] == stored[None, :]).astype(jnp.bfloat16)
        return lax.dot_general(
            jnp.concatenate(pieces, axis=0),
            pick,
            (((0,), (0,)), ((), ())),
            preferred_element_type=jnp.float32,
        ).astype(jnp.bfloat16)

    def some(*terms):
        own = added(terms)
        pieces = [own]
        for r in range(1, GROUP):
            rows = lax.dynamic_slice_in_dim(own, start[r - 1] * QB, room * QB, 0)
            pieces.append(swapped(rows, "ctx", r))
        return placed(pieces, some_slots)

    def whole(*terms):
        own = added(terms)
        pieces = [own] + [swapped(own, "ctx", r) for r in range(1, GROUP)]
        return placed(pieces, whole_slots)

    return lax.cond(few, some, whole, *terms)


def body(queries, kv_rows, doc_start, destination, out_weight):
    position = lax.axis_index("ctx").astype(jnp.int32)
    tokens = queries.shape[0]
    blocks = tokens // QB
    here = lax.axis_index("head").astype(jnp.int32)
    table = jnp.concatenate([jnp.stack([position, here]), doc_start, destination])
    own = own_layouts(table, queries, kv_rows)
    shards, (*own, plan) = collect_window(kv_rows, W1 // tokens, own)
    outputs = 2 if len(shards) == 2 else 1
    partials = attended_and_projected(own, shards, plan, out_weight, outputs)
    _, _, _, sent, small, some, whole, end = plan_places(blocks)
    parts = ([plan[sent + r] for r in range(GROUP - 1)], plan[some:whole], plan[whole:end], plan[small] > 0)
    partials, parts = lax.optimization_barrier((partials, parts))
    if outputs == 2:
        terms = [partials[1], swapped(partials[0], "head", 1)]
    else:
        terms = [lax.psum_scatter(partials[0], "head", scatter_dimension=1, tiled=True)]
    return exchanged(terms, parts, position, blocks)


def solution(mesh):
    in_specs = (P("ctx", "head"), P("ctx", None), P(), P(), P("head", None))
    return jax.shard_map(
        body, mesh=mesh, in_specs=in_specs, out_specs=P("head", "ctx"), check_vma=False
    )
```

```python
import functools

import jax
import jax.numpy as jnp
import numpy as np
from jax import lax
from jax.experimental import pallas as pl
from jax.experimental.pallas import tpu as pltpu
from jax.sharding import PartitionSpec as P

DH = 128
W1 = 512
W2 = 32
QB = 32
LANES = 128
PACK = 16
VR = DH + PACK
SAMPLE = 32
AHEAD = 3
SPAN = 4
LIMIT = 1e30
LOG2E = 1.4426950408889634


def iota(shape, dim):
    return lax.broadcasted_iota(jnp.int32, shape, dim)


def spread(columns, first, heads):
    pick = iota((columns.shape[1], LANES), 0) == first + iota((columns.shape[1], LANES), 1) // heads
    pick = pick.astype(jnp.float32).astype(jnp.bfloat16)
    return jnp.dot(columns, pick, preferred_element_type=jnp.float32)


def with_ones(values):
    return jnp.concatenate(
        [values.astype(jnp.float32).T, jnp.ones((VR - DH, LANES), jnp.float32)], axis=0
    ).astype(jnp.bfloat16)


GROUP = 4


def plan_places(blocks):
    room = blocks // 2
    sizes = (blocks, 1, blocks, GROUP - 1, blocks + (GROUP - 1) * room, GROUP * blocks)
    return [sum(sizes[:k]) for k in range(len(sizes) + 1)]


def make_plan(table_ref, plan_ref, blocks):
    room = blocks // 2
    position, here = table_ref[0], table_ref[1]
    total = (table_ref.shape[0] - 2) // 2
    target = 2 + total
    place = lax.rem(position, GROUP)
    masked, head, order, sent, some, whole, _ = plan_places(blocks)
    one, zero = jnp.int32(1), jnp.int32(0)
    for k in range(blocks):
        block = position * blocks + k
        outside = table_ref[2 + block] - (block * QB - W1)
        plan_ref[masked + k] = jnp.clip(outside, 0, W1)
    plan_ref[head] = here
    for r in range(GROUP):
        source = lax.bitwise_xor(place, jnp.int32(r))
        slots = [table_ref[target + (position - place + source) * blocks + k] for k in range(blocks)]
        far = [lax.bitwise_xor(lax.rem(lax.div(s, blocks), GROUP), source) for s in slots]
        for k in range(blocks):
            at = zero
            for j in range(blocks):
                if j != k:
                    ahead = far[j] <= far[k] if j < k else far[j] < far[k]
                    at = at + jnp.where(ahead, one, zero)
            plan_ref[whole + r * blocks + at] = slots[k]
            if r == 0:
                plan_ref[order + k] = at
        for distance in range(1, GROUP) if r == 0 else (r,):
            nearer = zero
            for k in range(blocks):
                nearer = nearer + jnp.where(far[k] < distance, one, zero)
            nearer = jnp.minimum(nearer, blocks - room)
            if r == 0:
                plan_ref[sent + distance - 1] = nearer
            else:
                for c in range(room):
                    into = some + blocks + (r - 1) * room + c
                    plan_ref[into] = plan_ref[whole + r * blocks + nearer + c]
    for k in range(blocks):
        plan_ref[some + k] = plan_ref[whole + k]


def own_kernel(table_ref, q_ref, kv_ref, q3, k1o, v1o, k2o, v2o, plan_ref):
    make_plan(table_ref, plan_ref, q_ref.shape[0] // QB)
    f32, bf16 = jnp.float32, jnp.bfloat16
    tokens = q_ref.shape[0]
    heads = q_ref.shape[1] // DH
    group = LANES // heads
    k1o[...] = kv_ref[:, :DH]
    second = kv_ref[:, 2 * DH : 3 * DH].astype(f32)
    second = jnp.broadcast_to(second[:, None, :], (tokens, heads, DH))
    k2o[...] = second.reshape(k2o.shape).astype(bf16)
    for k in range(tokens // LANES):
        v1o[k] = with_ones(kv_ref[k * LANES : (k + 1) * LANES, DH : 2 * DH])
        columns = with_ones(kv_ref[k * LANES : (k + 1) * LANES, 3 * DH :])
        for c in range(heads):
            v2o[k * heads + c] = spread(columns, c * group, heads)
    for h in range(heads):
        q3[pl.ds(h, tokens, stride=heads), :] = q_ref[:, h * DH : (h + 1) * DH].astype(f32)


def attention_kernel(pairs, outputs, plan_ref, table_ref, q3, k1o, v1o, k2o, v2o, w_ref, *refs):
    shards, refs = refs[:pairs], refs[pairs:]
    out_refs, few_ref, pick_ref, refs = refs[:outputs], refs[outputs], refs[outputs + 1], refs[outputs + 2 :]
    kv_ref, wbuf, wsem, k1n, k1s, v1t, v1n, k2x, v2x, rowid, laneid, part, top2, bad, rows = refs
    tokens = k1o.shape[0]
    heads = q3.shape[0] // tokens
    cols = W2 * heads
    group = LANES // heads
    tiles = tokens // LANES
    blocks = tokens // QB
    near_tiles = cols // LANES
    size = max(heads, PACK)
    pack = size // heads
    wide = min(2 * LANES, cols)
    span = min(SPAN, QB // group)
    scale = LOG2E / np.sqrt(DH)
    f32, bf16 = jnp.float32, jnp.bfloat16

    room = blocks // 2
    total = (table_ref.shape[0] - 2) // 2
    senders = total // blocks

    def most_alike(device):
        to = [lax.rem(lax.div(table_ref[2 + total + device * blocks + k], blocks), GROUP) for k in range(blocks)]
        most = jnp.int32(1)
        for k in range(blocks - room):
            alike = jnp.int32(1)
            for j in range(k + 1, blocks):
                alike = alike + jnp.where(to[j] == to[k], 1, 0).astype(jnp.int32)
            most = jnp.maximum(most, alike)
        return most

    def either(cond, a, b):
        if isinstance(cond, bool):
            return a if cond else b
        return jnp.where(cond, a, b)

    weight_copy = pltpu.make_async_copy(w_ref, wbuf, wsem)
    weight_copy.start()
    masked, head, order, sent = plan_places(blocks)[:4]
    here = plan_ref[head]

    def lay(order):
        at = 0
        for ref in order:
            kv_ref[at : at + ref.shape[0], :] = ref[...]
            at += ref.shape[0]

    if outputs == 2:

        @pl.when(here == 0)
        def _():
            lay(shards[::-1])

        @pl.when(here != 0)
        def _():
            lay(shards)

    else:
        lay(shards)

    def prepare():
        rowid[...] = iota(rowid.shape, 0).astype(f32).astype(bf16)
        laneid[...] = iota(laneid.shape, 1).astype(f32).astype(bf16)
        bad[...] = jnp.zeros_like(bad)
        k1n[...] = k1o[...]
        v1n[...] = v1o[...]
        second = kv_ref[W1 - W2 :, 2 * DH : 3 * DH].astype(f32)
        second = jnp.broadcast_to(second[:, None, :], (W2, heads, DH))
        k2x[: W2 // pack] = second.reshape(W2 // pack, size, DH).astype(bf16)
        k2x[W2 // pack :] = k2o[...]
        columns = with_ones(kv_ref[W1 - LANES :, 3 * DH :])
        for k in range(near_tiles):
            v2x[k] = spread(columns, LANES - W2 + k * group, heads)
        v2x[near_tiles:] = v2o[...]

    def reset(t, inv):
        kt = k1o[pl.ds(pl.multiple_of(t, PACK), PACK), :].astype(f32)[:1]
        window = kv_ref[:, : 2 * DH].astype(f32)
        ok = iota((W1, DH), 0) >= inv
        k1s[...] = jnp.where(ok, window[:, :DH], kt).astype(bf16)
        values = jnp.where(ok, window[:, DH:], 0.0)
        for k in range(W1 // LANES):
            v1t[k, :DH] = values[k * LANES : (k + 1) * LANES].T.astype(bf16)
            live = k * LANES + iota((VR - DH, LANES), 1) >= inv
            v1t[k, DH:] = live.astype(f32).astype(bf16)
        k1n[...] = jnp.where(iota((tokens, DH), 0) < t, kt, k1n[...].astype(f32)).astype(bf16)
        for k in range(tiles):
            gone = k * LANES + iota((VR, LANES), 1) < t
            v1n[k] = jnp.where(gone, 0.0, v1n[k].astype(f32)).astype(bf16)

        @pl.when(inv == W1)
        def _():
            fill = jnp.broadcast_to(k2x[(t + W2) // pack].astype(f32)[:1], (size, DH)).astype(bf16)
            for s in range(W2 // pack):
                k2x[t // pack + s] = fill
            for k in range(near_tiles):
                v2x[t // group + k] = jnp.zeros((VR, LANES), f32)

    def scores(g, u):
        t = g * group + u
        mark = t.astype(f32).astype(bf16)
        keys = [
            jnp.where(rowid[...] + (k * LANES) <= mark, k1n[k * LANES : (k + 1) * LANES], k1s[k * LANES : (k + 1) * LANES])
            for k in range(tiles)
        ]
        keys = jnp.concatenate(keys + [k1s[tokens:]], axis=0)
        query = q3[pl.ds(t * heads, heads), :]
        if heads < PACK:
            query = jnp.concatenate([query] * pack, axis=0)
        query = query.astype(bf16)
        base = g * (group // pack)
        for n in range(0, cols, wide):
            paired = []
            for s in range(n // size, (n + wide) // size):
                if s * pack >= group:
                    near_keys = k2x[base + s]
                elif pack == 1:
                    near_keys = k2x[base + either(s <= u, s + W2, s)]
                else:
                    token = s * pack + iota((size, DH), 0) // heads
                    after = k2x[base + s + W2 // pack].astype(f32)
                    near_keys = jnp.where(token <= u, after, k2x[base + s].astype(f32)).astype(bf16)
                paired.append(near_keys * query)
            yield lax.dot_general(
                keys,
                jnp.concatenate(paired, axis=0),
                (((1,), (1,)), ((), ())),
                preferred_element_type=f32,
            )

    def highest(logits, best=None):
        top = jnp.max(logits, axis=0, keepdims=True)
        for k in range(0, wide, LANES):
            some = top[:, k : k + LANES]
            best = some if best is None else jnp.maximum(best, some)
        return best

    def mix(g, u, n, logits, top):
        mark = (g * group + u).astype(f32).astype(bf16)
        values = [
            jnp.where(laneid[...] + (k * LANES) <= mark, v1n[k], v1t[k]) for k in range(tiles)
        ] + [v1t[k] for k in range(tiles, W1 // LANES)]
        tops = jnp.concatenate([top] * (wide // LANES), axis=1)
        product = None
        for k in range(0, W1, 2 * LANES):
            weights = jnp.exp2(logits[k : k + 2 * LANES] * scale - tops).astype(bf16)
            two = jnp.concatenate(values[k // LANES : k // LANES + 2], axis=1)
            some = jnp.dot(two, weights, preferred_element_type=f32)
            product = some if product is None else product + some
        total = None
        for c in range(0, wide, LANES):
            k = (n + c) // LANES
            near = v2x[g + k]
            if k == 0:
                near = jnp.where(iota((VR, LANES), 1) // heads <= u, v2x[g + near_tiles], near)
            some = product[:, c : c + LANES] * near
            total = some if total is None else total + some
        return total

    def keep(g, u, total, top):
        part[g * group + u] = total
        top2[g * group + u] = jnp.broadcast_to(top, (8, LANES))
        bad[...] = jnp.where(total[DH : DH + 8] < LIMIT, bad[...], 1.0)

    def finish(g):
        lane = iota((VR, LANES), 1)
        sums = []
        for u in range(group):
            top = top2[g * group + u]
            best = top
            shift = LANES // 2
            while shift >= heads:
                best = jnp.maximum(best, pltpu.roll(best, shift, 1))
                shift //= 2
            sums.append(part[g * group + u] * jnp.exp2(top - best)[:1])
        shift = heads
        while shift < LANES:
            low = lane % (2 * shift) < shift
            sums = [
                jnp.where(low, a, b) + pltpu.roll(jnp.where(low, b, a), shift, 1)
                for a, b in zip(sums[::2], sums[1::2])
            ]
            shift *= 2
        value = sums[0][:DH] * (1.0 / sums[0][DH : DH + 1])
        spot = (plan_ref[order + g * group // QB] * QB + g * group % QB) * heads
        rows[pl.ds(pl.multiple_of(spot, LANES), LANES), :] = value.T

    def run(exact):
        prepare()

        def block(b, _):
            inv = plan_ref[masked + b]
            g0 = b * (QB // group)

            @pl.when((b == 0) | (inv == W1))
            def _():
                reset(b * QB, inv)

            def fast(s, _):
                if span == QB // group:
                    each = -(-senders // blocks)
                    for k in range(each):
                        device = jnp.minimum(b * each + k, senders - 1)
                        few_ref[0] = jnp.where(most_alike(device) > room, 0, few_ref[0])
                work = []
                for u in range(span * group):
                    work += [(u, n) for n in range(0, cols, wide)]
                at = [divmod(u, group) for u in range(span * group)]
                first = g0 + s * span
                source = [scores(first + k, u) for k, u in at]
                top = total = None
                ahead = [next(source[u]) for u, n in work[:AHEAD]]
                for i, (u, n) in enumerate(work):
                    if i + AHEAD < len(work):
                        ahead.append(next(source[work[i + AHEAD][0]]))
                    logits = ahead.pop(0)
                    g, v = first + at[u][0], at[u][1]
                    if n == 0:
                        top = highest(logits[:SAMPLE]) * scale
                        total = None
                    some = mix(g, v, n, logits, top)
                    total = some if total is None else total + some
                    if n + wide == cols:
                        keep(g, v, total, top)
                        if v == group // 2:
                            finish(jnp.maximum(g - 1, 0))
                return 0

            def slow(s, _):
                g, u = g0 + s // group, s % group
                best = None
                for logits in scores(g, u):
                    best = highest(logits, best)
                total = None
                for n, logits in zip(range(0, cols, wide), scores(g, u)):
                    some = mix(g, u, n, logits, best * scale)
                    total = some if total is None else total + some
                keep(g, u, total, best * scale)
                return 0

            if exact:
                return lax.fori_loop(0, QB, slow, 0)
            return lax.fori_loop(0, QB // group // span, fast, 0)

        lax.fori_loop(0, tokens // QB, block, 0)
        if exact:
            lax.fori_loop(0, tokens // group - 1, lambda g, _: finish(g) or 0, 0)
        finish(jnp.int32(tokens // group - 1))

    few_ref[0] = jnp.int32(span == QB // group)
    for r in range(GROUP - 1):
        line = iota((room * QB, tokens), 0) + plan_ref[sent + r] * QB
        chosen = (line == iota((room * QB, tokens), 1)).astype(f32).astype(bf16)
        pick_ref[r * room * QB : (r + 1) * room * QB, :] = chosen
    run(False)

    @pl.when(jnp.max(bad[...]) > 0)
    def _():
        run(True)

    attended = jnp.concatenate(
        [rows[pl.ds(h, tokens, stride=heads), :].astype(bf16) for h in range(heads)], axis=1
    )
    weight_copy.wait()
    width = out_refs[0].shape[1]
    step = 2 * LANES
    for k, out_ref in enumerate(out_refs):
        begin = 0 if outputs == 1 else jnp.where(here == k, width, 0)
        for n in range(0, width, step):
            some = wbuf[:, pl.ds(pl.multiple_of(begin + n, step), step)]
            out_ref[:, n : n + step] = jnp.dot(attended, some, preferred_element_type=f32)


VMEM = pl.BlockSpec(memory_space=pltpu.VMEM)
HBM = pl.BlockSpec(memory_space=pltpu.HBM)
SMEM = pl.BlockSpec(memory_space=pltpu.SMEM)


def own_layouts(table, queries, kv_rows):
    tokens, width = queries.shape
    heads = width // DH
    size = max(heads, PACK)
    f32, bf16 = jnp.float32, jnp.bfloat16
    return pl.pallas_call(
        own_kernel,
        out_shape=[
            jax.ShapeDtypeStruct((tokens * heads, DH), f32),
            jax.ShapeDtypeStruct((tokens, DH), bf16),
            jax.ShapeDtypeStruct((tokens // LANES, VR, LANES), bf16),
            jax.ShapeDtypeStruct((tokens * heads // size, size, DH), bf16),
            jax.ShapeDtypeStruct((tokens * heads // LANES, VR, LANES), f32),
            jax.ShapeDtypeStruct((plan_places(tokens // QB)[-1],), jnp.int32),
        ],
        in_specs=[SMEM] + [VMEM] * 2,
        out_specs=[VMEM] * 5 + [SMEM],
        compiler_params=pltpu.CompilerParams(vmem_limit_bytes=16 * 2**20),
        cost_estimate=pl.CostEstimate(flops=10**9, bytes_accessed=4 * 2**20, transcendentals=0),
    )(table, queries, kv_rows)


def attended_and_projected(own, shards, plan, table, weight, outputs):
    heads = own[0].shape[0] // own[1].shape[0]
    tokens = own[1].shape[0]
    sends = (GROUP - 1) * (tokens // QB // 2) * QB
    size = max(heads, PACK)
    f32, bf16 = jnp.float32, jnp.bfloat16
    return pl.pallas_call(
        functools.partial(attention_kernel, len(shards), outputs),
        out_shape=[jax.ShapeDtypeStruct((tokens, weight.shape[1] // outputs), f32)] * outputs
        + [
            jax.ShapeDtypeStruct((1,), jnp.int32),
            jax.ShapeDtypeStruct((sends, tokens), bf16),
        ],
        in_specs=[SMEM] * 2 + [VMEM] * 5 + [HBM] + [VMEM] * len(shards),
        out_specs=[VMEM] * outputs + [SMEM, VMEM],
        scratch_shapes=[
            pltpu.VMEM((W1, 4 * DH), bf16),
            pltpu.VMEM(weight.shape, bf16),
            pltpu.SemaphoreType.DMA,
            pltpu.VMEM((tokens, DH), bf16),
            pltpu.VMEM((W1, DH), bf16),
            pltpu.VMEM((W1 // LANES, VR, LANES), bf16),
            pltpu.VMEM((tokens // LANES, VR, LANES), bf16),
            pltpu.VMEM(((tokens + W2) * heads // size, size, DH), bf16),
            pltpu.VMEM(((tokens + W2) * heads // LANES, VR, LANES), f32),
            pltpu.VMEM((LANES, DH), bf16),
            pltpu.VMEM((VR, LANES), bf16),
            pltpu.VMEM((tokens, VR, LANES), f32),
            pltpu.VMEM((tokens, 8, LANES), f32),
            pltpu.VMEM((8, LANES), f32),
            pltpu.VMEM((tokens * heads, DH), f32),
        ],
        compiler_params=pltpu.CompilerParams(vmem_limit_bytes=43 * 2**20),
    )(plan, table, *own, weight, *shards)

def shifted(block, axis, distance):
    devices = range(lax.axis_size(axis))
    return lax.ppermute(block, axis, [(i - distance, i) for i in devices if i - distance in devices])


def swapped(block, axis, bits):
    return lax.ppermute(block, axis, [(i, i ^ bits) for i in range(lax.axis_size(axis))])


def collect_window(kv_rows, back, own):
    if lax.axis_size("head") != 2 or back != 4:
        return [shifted(kv_rows, "ctx", back - k) for k in range(back)], own

    def taken(distances):
        devices = range(lax.axis_size("ctx"))
        route = [
            ((i - d) % len(devices) * 2 + h, i * 2 + h) for i in devices for h, d in enumerate(distances)
        ]
        return lax.ppermute(kv_rows, ("ctx", "head"), route)

    parts, own = lax.optimization_barrier(([taken((2, 4)), taken((1, 3))], own))
    held = jnp.concatenate(parts, axis=0)
    return [held, swapped(held, "head", 1)], own


def exchanged(terms, plan, position, blocks):
    room = blocks // 2
    pick, some_slots, whole_slots, few = plan

    def added(terms):
        return sum(terms[1:], terms[0]).astype(jnp.bfloat16)

    def placed(pieces, slots):
        tokens = blocks * QB
        rows = (slots[:, None] * QB + np.arange(QB, dtype=np.int32)[None, :]).reshape(-1)
        stored = position * tokens + jnp.arange(tokens, dtype=jnp.int32)
        pick = (rows[:, None] == stored[None, :]).astype(jnp.bfloat16)
        return lax.dot_general(
            jnp.concatenate(pieces, axis=0),
            pick,
            (((0,), (0,)), ((), ())),
            preferred_element_type=jnp.float32,
        ).astype(jnp.bfloat16)

    def some(*terms):
        own = added(terms)
        rows = jnp.dot(pick, own, preferred_element_type=jnp.float32).astype(jnp.bfloat16)
        rows = rows.reshape(GROUP - 1, room * QB, -1)
        pieces = [own] + [swapped(rows[r - 1], "ctx", r) for r in range(1, GROUP)]
        return placed(pieces, some_slots)

    def whole(*terms):
        own = added(terms)
        pieces = [own] + [swapped(own, "ctx", r) for r in range(1, GROUP)]
        return placed(pieces, whole_slots)

    return lax.cond(few, some, whole, *terms)


def body(queries, kv_rows, doc_start, destination, out_weight):
    position = lax.axis_index("ctx").astype(jnp.int32)
    tokens = queries.shape[0]
    blocks = tokens // QB
    here = lax.axis_index("head").astype(jnp.int32)
    table = jnp.concatenate([jnp.stack([position, here]), doc_start, destination])
    own = own_layouts(table, queries, kv_rows)
    shards, (*own, plan) = collect_window(kv_rows, W1 // tokens, own)
    outputs = 2 if len(shards) == 2 else 1
    results = attended_and_projected(own, shards, plan, table, out_weight, outputs)
    partials, few, pick = results[:outputs], results[outputs], results[outputs + 1]
    some, whole, end = plan_places(blocks)[-3:]
    parts = (pick, plan[some:whole], plan[whole:end], few[0] > 0)
    if outputs == 2:
        terms = [partials[1], swapped(partials[0], "head", 1)]
    else:
        terms = [lax.psum_scatter(partials[0], "head", scatter_dimension=1, tiled=True)]
    return exchanged(terms, parts, position, blocks)


def solution(mesh):
    in_specs = (P("ctx", "head"), P("ctx", None), P(), P(), P("head", None))
    return jax.shard_map(
        body, mesh=mesh, in_specs=in_specs, out_specs=P("head", "ctx"), check_vma=False
    )
```

```python
import functools

import jax
import jax.numpy as jnp
import numpy as np
from jax import lax
from jax.experimental import pallas as pl
from jax.experimental.pallas import tpu as pltpu
from jax.sharding import PartitionSpec as P

DH = 128
W1 = 512
W2 = 32
QB = 32
LANES = 128
PACK = 16
VR = DH + PACK
SAMPLE = 32
AHEAD = 3
SPAN = 4
LIMIT = 1e30
LOG2E = 1.4426950408889634


def iota(shape, dim):
    return lax.broadcasted_iota(jnp.int32, shape, dim)


def spread(columns, first, heads):
    pick = iota((columns.shape[1], LANES), 0) == first + iota((columns.shape[1], LANES), 1) // heads
    pick = pick.astype(jnp.float32).astype(jnp.bfloat16)
    return jnp.dot(columns, pick, preferred_element_type=jnp.float32)


def with_ones(values):
    return jnp.concatenate(
        [values.astype(jnp.float32).T, jnp.ones((VR - DH, LANES), jnp.float32)], axis=0
    ).astype(jnp.bfloat16)


GROUP = 4


def plan_places(blocks):
    room = blocks // 2
    sizes = (blocks, 1, blocks, GROUP - 1, blocks + (GROUP - 1) * room, GROUP * blocks, 1)
    return [sum(sizes[:k]) for k in range(len(sizes) + 1)]


def make_plan(table_ref, plan_ref, blocks):
    room = blocks // 2
    position, here = table_ref[0], table_ref[1]
    total = (table_ref.shape[0] - 2) // 2
    target = 2 + total
    place = lax.rem(position, GROUP)
    masked, head, order, sent, some, whole, _, _ = plan_places(blocks)
    one, zero = jnp.int32(1), jnp.int32(0)
    for k in range(blocks):
        block = position * blocks + k
        outside = table_ref[2 + block] - (block * QB - W1)
        plan_ref[masked + k] = jnp.clip(outside, 0, W1)
    plan_ref[head] = here
    for r in range(GROUP):
        source = lax.bitwise_xor(place, jnp.int32(r))
        slots = [table_ref[target + (position - place + source) * blocks + k] for k in range(blocks)]
        far = [lax.bitwise_xor(lax.rem(lax.div(s, blocks), GROUP), source) for s in slots]
        for k in range(blocks):
            at = zero
            for j in range(blocks):
                if j != k:
                    ahead = far[j] <= far[k] if j < k else far[j] < far[k]
                    at = at + jnp.where(ahead, one, zero)
            plan_ref[whole + r * blocks + at] = slots[k]
            if r == 0:
                plan_ref[order + k] = at
        for distance in range(1, GROUP) if r == 0 else (r,):
            nearer = zero
            for k in range(blocks):
                nearer = nearer + jnp.where(far[k] < distance, one, zero)
            nearer = jnp.minimum(nearer, blocks - room)
            if r == 0:
                plan_ref[sent + distance - 1] = nearer
            else:
                for c in range(room):
                    into = some + blocks + (r - 1) * room + c
                    plan_ref[into] = plan_ref[whole + r * blocks + nearer + c]
    for k in range(blocks):
        plan_ref[some + k] = plan_ref[whole + k]


def own_kernel(q_ref, kv_ref, q3, k1o, v1o, k2o, v2o):
    f32, bf16 = jnp.float32, jnp.bfloat16
    tokens = q_ref.shape[0]
    heads = q_ref.shape[1] // DH
    group = LANES // heads
    k1o[...] = kv_ref[:, :DH]
    second = kv_ref[:, 2 * DH : 3 * DH].astype(f32)
    second = jnp.broadcast_to(second[:, None, :], (tokens, heads, DH))
    k2o[...] = second.reshape(k2o.shape).astype(bf16)
    for k in range(tokens // LANES):
        v1o[k] = with_ones(kv_ref[k * LANES : (k + 1) * LANES, DH : 2 * DH])
        columns = with_ones(kv_ref[k * LANES : (k + 1) * LANES, 3 * DH :])
        for c in range(heads):
            v2o[k * heads + c] = spread(columns, c * group, heads)
    for h in range(heads):
        q3[pl.ds(h, tokens, stride=heads), :] = q_ref[:, h * DH : (h + 1) * DH].astype(f32)


def attention_kernel(pairs, outputs, table_ref, q3, k1o, v1o, k2o, v2o, w_ref, *refs):
    shards, refs = refs[:pairs], refs[pairs:]
    out_refs, plan_ref, pick_ref, refs = refs[:outputs], refs[outputs], refs[outputs + 1], refs[outputs + 2 :]
    kv_ref, wbuf, wsem, k1n, k1s, v1t, v1n, k2x, v2x, rowid, laneid, part, top2, bad, rows = refs
    tokens = k1o.shape[0]
    heads = q3.shape[0] // tokens
    cols = W2 * heads
    group = LANES // heads
    tiles = tokens // LANES
    blocks = tokens // QB
    near_tiles = cols // LANES
    size = max(heads, PACK)
    pack = size // heads
    wide = min(2 * LANES, cols)
    span = min(SPAN, QB // group)
    scale = LOG2E / np.sqrt(DH)
    f32, bf16 = jnp.float32, jnp.bfloat16

    room = blocks // 2
    total = (table_ref.shape[0] - 2) // 2
    senders = total // blocks

    def most_alike(device):
        to = [lax.rem(lax.div(table_ref[2 + total + device * blocks + k], blocks), GROUP) for k in range(blocks)]
        most = jnp.int32(1)
        for k in range(blocks - room):
            alike = jnp.int32(1)
            for j in range(k + 1, blocks):
                alike = alike + jnp.where(to[j] == to[k], 1, 0).astype(jnp.int32)
            most = jnp.maximum(most, alike)
        return most

    def either(cond, a, b):
        if isinstance(cond, bool):
            return a if cond else b
        return jnp.where(cond, a, b)

    weight_copy = pltpu.make_async_copy(w_ref, wbuf, wsem)
    weight_copy.start()
    masked, head, order, sent, _, _, small, _ = plan_places(blocks)
    here = table_ref[1]
    make_plan(table_ref, plan_ref, blocks)

    def lay(order):
        at = 0
        for ref in order:
            kv_ref[at : at + ref.shape[0], :] = ref[...]
            at += ref.shape[0]

    if outputs == 2:

        @pl.when(here == 0)
        def _():
            lay(shards[::-1])

        @pl.when(here != 0)
        def _():
            lay(shards)

    else:
        lay(shards)

    def prepare():
        rowid[...] = iota(rowid.shape, 0).astype(f32).astype(bf16)
        laneid[...] = iota(laneid.shape, 1).astype(f32).astype(bf16)
        bad[...] = jnp.zeros_like(bad)
        k1n[...] = k1o[...]
        v1n[...] = v1o[...]
        second = kv_ref[W1 - W2 :, 2 * DH : 3 * DH].astype(f32)
        second = jnp.broadcast_to(second[:, None, :], (W2, heads, DH))
        k2x[: W2 // pack] = second.reshape(W2 // pack, size, DH).astype(bf16)
        k2x[W2 // pack :] = k2o[...]
        columns = with_ones(kv_ref[W1 - LANES :, 3 * DH :])
        for k in range(near_tiles):
            v2x[k] = spread(columns, LANES - W2 + k * group, heads)
        v2x[near_tiles:] = v2o[...]

    def reset(t, inv):
        kt = k1o[pl.ds(pl.multiple_of(t, PACK), PACK), :].astype(f32)[:1]
        window = kv_ref[:, : 2 * DH].astype(f32)
        ok = iota((W1, DH), 0) >= inv
        k1s[...] = jnp.where(ok, window[:, :DH], kt).astype(bf16)
        values = jnp.where(ok, window[:, DH:], 0.0)
        for k in range(W1 // LANES):
            v1t[k, :DH] = values[k * LANES : (k + 1) * LANES].T.astype(bf16)
            live = k * LANES + iota((VR - DH, LANES), 1) >= inv
            v1t[k, DH:] = live.astype(f32).astype(bf16)
        k1n[...] = jnp.where(iota((tokens, DH), 0) < t, kt, k1n[...].astype(f32)).astype(bf16)
        for k in range(tiles):
            gone = k * LANES + iota((VR, LANES), 1) < t
            v1n[k] = jnp.where(gone, 0.0, v1n[k].astype(f32)).astype(bf16)

        @pl.when(inv == W1)
        def _():
            fill = jnp.broadcast_to(k2x[(t + W2) // pack].astype(f32)[:1], (size, DH)).astype(bf16)
            for s in range(W2 // pack):
                k2x[t // pack + s] = fill
            for k in range(near_tiles):
                v2x[t // group + k] = jnp.zeros((VR, LANES), f32)

    def scores(g, u):
        t = g * group + u
        mark = t.astype(f32).astype(bf16)
        keys = [
            jnp.where(rowid[...] + (k * LANES) <= mark, k1n[k * LANES : (k + 1) * LANES], k1s[k * LANES : (k + 1) * LANES])
            for k in range(tiles)
        ]
        keys = jnp.concatenate(keys + [k1s[tokens:]], axis=0)
        query = q3[pl.ds(t * heads, heads), :]
        if heads < PACK:
            query = jnp.concatenate([query] * pack, axis=0)
        query = query.astype(bf16)
        base = g * (group // pack)
        for n in range(0, cols, wide):
            paired = []
            for s in range(n // size, (n + wide) // size):
                if s * pack >= group:
                    near_keys = k2x[base + s]
                elif pack == 1:
                    near_keys = k2x[base + either(s <= u, s + W2, s)]
                else:
                    token = s * pack + iota((size, DH), 0) // heads
                    after = k2x[base + s + W2 // pack].astype(f32)
                    near_keys = jnp.where(token <= u, after, k2x[base + s].astype(f32)).astype(bf16)
                paired.append(near_keys * query)
            yield lax.dot_general(
                keys,
                jnp.concatenate(paired, axis=0),
                (((1,), (1,)), ((), ())),
                preferred_element_type=f32,
            )

    def highest(logits, best=None):
        top = jnp.max(logits, axis=0, keepdims=True)
        for k in range(0, wide, LANES):
            some = top[:, k : k + LANES]
            best = some if best is None else jnp.maximum(best, some)
        return best

    def mix(g, u, n, logits, top):
        mark = (g * group + u).astype(f32).astype(bf16)
        values = [
            jnp.where(laneid[...] + (k * LANES) <= mark, v1n[k], v1t[k]) for k in range(tiles)
        ] + [v1t[k] for k in range(tiles, W1 // LANES)]
        tops = jnp.concatenate([top] * (wide // LANES), axis=1)
        product = None
        for k in range(0, W1, 2 * LANES):
            weights = jnp.exp2(logits[k : k + 2 * LANES] * scale - tops).astype(bf16)
            two = jnp.concatenate(values[k // LANES : k // LANES + 2], axis=1)
            some = jnp.dot(two, weights, preferred_element_type=f32)
            product = some if product is None else product + some
        total = None
        for c in range(0, wide, LANES):
            k = (n + c) // LANES
            near = v2x[g + k]
            if k == 0:
                near = jnp.where(iota((VR, LANES), 1) // heads <= u, v2x[g + near_tiles], near)
            some = product[:, c : c + LANES] * near
            total = some if total is None else total + some
        return total

    def keep(g, u, total, top):
        part[g * group + u] = total
        top2[g * group + u] = jnp.broadcast_to(top, (8, LANES))
        bad[...] = jnp.where(total[DH : DH + 8] < LIMIT, bad[...], 1.0)

    def finish(g):
        lane = iota((VR, LANES), 1)
        sums = []
        for u in range(group):
            top = top2[g * group + u]
            best = top
            shift = LANES // 2
            while shift >= heads:
                best = jnp.maximum(best, pltpu.roll(best, shift, 1))
                shift //= 2
            sums.append(part[g * group + u] * jnp.exp2(top - best)[:1])
        shift = heads
        while shift < LANES:
            low = lane % (2 * shift) < shift
            sums = [
                jnp.where(low, a, b) + pltpu.roll(jnp.where(low, b, a), shift, 1)
                for a, b in zip(sums[::2], sums[1::2])
            ]
            shift *= 2
        value = sums[0][:DH] * (1.0 / sums[0][DH : DH + 1])
        spot = (plan_ref[order + g * group // QB] * QB + g * group % QB) * heads
        rows[pl.ds(pl.multiple_of(spot, LANES), LANES), :] = value.T

    def run(exact):
        prepare()

        def block(b, _):
            inv = plan_ref[masked + b]
            g0 = b * (QB // group)

            @pl.when((b == 0) | (inv == W1))
            def _():
                reset(b * QB, inv)

            def fast(s, _):
                if span == QB // group:
                    each = -(-senders // blocks)
                    for k in range(each):
                        device = jnp.minimum(b * each + k, senders - 1)
                        plan_ref[small] = jnp.where(most_alike(device) > room, 0, plan_ref[small])
                work = []
                for u in range(span * group):
                    work += [(u, n) for n in range(0, cols, wide)]
                at = [divmod(u, group) for u in range(span * group)]
                first = g0 + s * span
                source = [scores(first + k, u) for k, u in at]
                top = total = None
                ahead = [next(source[u]) for u, n in work[:AHEAD]]
                for i, (u, n) in enumerate(work):
                    if i + AHEAD < len(work):
                        ahead.append(next(source[work[i + AHEAD][0]]))
                    logits = ahead.pop(0)
                    g, v = first + at[u][0], at[u][1]
                    if n == 0:
                        top = highest(logits[:SAMPLE]) * scale
                        total = None
                    some = mix(g, v, n, logits, top)
                    total = some if total is None else total + some
                    if n + wide == cols:
                        keep(g, v, total, top)
                        if v == group // 2:
                            finish(jnp.maximum(g - 1, 0))
                return 0

            def slow(s, _):
                g, u = g0 + s // group, s % group
                best = None
                for logits in scores(g, u):
                    best = highest(logits, best)
                total = None
                for n, logits in zip(range(0, cols, wide), scores(g, u)):
                    some = mix(g, u, n, logits, best * scale)
                    total = some if total is None else total + some
                keep(g, u, total, best * scale)
                return 0

            if exact:
                return lax.fori_loop(0, QB, slow, 0)
            return lax.fori_loop(0, QB // group // span, fast, 0)

        lax.fori_loop(0, tokens // QB, block, 0)
        if exact:
            lax.fori_loop(0, tokens // group - 1, lambda g, _: finish(g) or 0, 0)
        finish(jnp.int32(tokens // group - 1))

    plan_ref[small] = jnp.int32(span == QB // group)
    for r in range(GROUP - 1):
        line = iota((room * QB, tokens), 0) + plan_ref[sent + r] * QB
        chosen = (line == iota((room * QB, tokens), 1)).astype(f32).astype(bf16)
        pick_ref[r * room * QB : (r + 1) * room * QB, :] = chosen
    run(False)

    @pl.when(jnp.max(bad[...]) > 0)
    def _():
        run(True)

    attended = jnp.concatenate(
        [rows[pl.ds(h, tokens, stride=heads), :].astype(bf16) for h in range(heads)], axis=1
    )
    weight_copy.wait()
    width = out_refs[0].shape[1]
    step = 2 * LANES
    for k, out_ref in enumerate(out_refs):
        begin = 0 if outputs == 1 else jnp.where(here == k, width, 0)
        for n in range(0, width, step):
            some = wbuf[:, pl.ds(pl.multiple_of(begin + n, step), step)]
            out_ref[:, n : n + step] = jnp.dot(attended, some, preferred_element_type=f32)


VMEM = pl.BlockSpec(memory_space=pltpu.VMEM)
HBM = pl.BlockSpec(memory_space=pltpu.HBM)
SMEM = pl.BlockSpec(memory_space=pltpu.SMEM)


def own_layouts(queries, kv_rows):
    tokens, width = queries.shape
    heads = width // DH
    size = max(heads, PACK)
    f32, bf16 = jnp.float32, jnp.bfloat16
    return pl.pallas_call(
        own_kernel,
        out_shape=[
            jax.ShapeDtypeStruct((tokens * heads, DH), f32),
            jax.ShapeDtypeStruct((tokens, DH), bf16),
            jax.ShapeDtypeStruct((tokens // LANES, VR, LANES), bf16),
            jax.ShapeDtypeStruct((tokens * heads // size, size, DH), bf16),
            jax.ShapeDtypeStruct((tokens * heads // LANES, VR, LANES), f32),
        ],
        in_specs=[VMEM] * 2,
        out_specs=[VMEM] * 5,
        compiler_params=pltpu.CompilerParams(vmem_limit_bytes=16 * 2**20),
        cost_estimate=pl.CostEstimate(flops=10**9, bytes_accessed=4 * 2**20, transcendentals=0),
    )(queries, kv_rows)


def attended_and_projected(own, shards, table, weight, outputs):
    heads = own[0].shape[0] // own[1].shape[0]
    tokens = own[1].shape[0]
    sends = (GROUP - 1) * (tokens // QB // 2) * QB
    size = max(heads, PACK)
    f32, bf16 = jnp.float32, jnp.bfloat16
    return pl.pallas_call(
        functools.partial(attention_kernel, len(shards), outputs),
        out_shape=[jax.ShapeDtypeStruct((tokens, weight.shape[1] // outputs), f32)] * outputs
        + [
            jax.ShapeDtypeStruct((plan_places(tokens // QB)[-1],), jnp.int32),
            jax.ShapeDtypeStruct((sends, tokens), bf16),
        ],
        in_specs=[SMEM] + [VMEM] * 5 + [HBM] + [VMEM] * len(shards),
        out_specs=[VMEM] * outputs + [SMEM, VMEM],
        scratch_shapes=[
            pltpu.VMEM((W1, 4 * DH), bf16),
            pltpu.VMEM(weight.shape, bf16),
            pltpu.SemaphoreType.DMA,
            pltpu.VMEM((tokens, DH), bf16),
            pltpu.VMEM((W1, DH), bf16),
            pltpu.VMEM((W1 // LANES, VR, LANES), bf16),
            pltpu.VMEM((tokens // LANES, VR, LANES), bf16),
            pltpu.VMEM(((tokens + W2) * heads // size, size, DH), bf16),
            pltpu.VMEM(((tokens + W2) * heads // LANES, VR, LANES), f32),
            pltpu.VMEM((LANES, DH), bf16),
            pltpu.VMEM((VR, LANES), bf16),
            pltpu.VMEM((tokens, VR, LANES), f32),
            pltpu.VMEM((tokens, 8, LANES), f32),
            pltpu.VMEM((8, LANES), f32),
            pltpu.VMEM((tokens * heads, DH), f32),
        ],
        compiler_params=pltpu.CompilerParams(vmem_limit_bytes=43 * 2**20),
    )(table, *own, weight, *shards)

def shifted(block, axis, distance):
    devices = range(lax.axis_size(axis))
    return lax.ppermute(block, axis, [(i - distance, i) for i in devices if i - distance in devices])


def swapped(block, axis, bits):
    return lax.ppermute(block, axis, [(i, i ^ bits) for i in range(lax.axis_size(axis))])


def collect_window(kv_rows, back, own):
    if lax.axis_size("head") != 2 or back != 4:
        return [shifted(kv_rows, "ctx", back - k) for k in range(back)], own

    def taken(distances):
        devices = range(lax.axis_size("ctx"))
        route = [
            ((i - d) % len(devices) * 2 + h, i * 2 + h) for i in devices for h, d in enumerate(distances)
        ]
        return lax.ppermute(kv_rows, ("ctx", "head"), route)

    parts, own = lax.optimization_barrier(([taken((2, 4)), taken((1, 3))], own))
    held = jnp.concatenate(parts, axis=0)
    return [held, swapped(held, "head", 1)], own


def exchanged(terms, plan, position, blocks):
    room = blocks // 2
    pick, some_slots, whole_slots, few = plan

    def added(terms):
        return sum(terms[1:], terms[0]).astype(jnp.bfloat16)

    def placed(pieces, slots):
        tokens = blocks * QB
        rows = (slots[:, None] * QB + np.arange(QB, dtype=np.int32)[None, :]).reshape(-1)
        stored = position * tokens + jnp.arange(tokens, dtype=jnp.int32)
        pick = (rows[:, None] == stored[None, :]).astype(jnp.bfloat16)
        return lax.dot_general(
            jnp.concatenate(pieces, axis=0),
            pick,
            (((0,), (0,)), ((), ())),
            preferred_element_type=jnp.float32,
        ).astype(jnp.bfloat16)

    def some(*terms):
        own = added(terms)
        rows = jnp.dot(pick, own, preferred_element_type=jnp.float32).astype(jnp.bfloat16)
        rows = rows.reshape(GROUP - 1, room * QB, -1)
        pieces = [own] + [swapped(rows[r - 1], "ctx", r) for r in range(1, GROUP)]
        return placed(pieces, some_slots)

    def whole(*terms):
        own = added(terms)
        pieces = [own] + [swapped(own, "ctx", r) for r in range(1, GROUP)]
        return placed(pieces, whole_slots)

    return lax.cond(few, some, whole, *terms)


def body(queries, kv_rows, doc_start, destination, out_weight):
    position = lax.axis_index("ctx").astype(jnp.int32)
    tokens = queries.shape[0]
    blocks = tokens // QB
    here = lax.axis_index("head").astype(jnp.int32)
    table = jnp.concatenate([jnp.stack([position, here]), doc_start, destination])
    own = own_layouts(queries, kv_rows)
    shards, own = collect_window(kv_rows, W1 // tokens, own)
    outputs = 2 if len(shards) == 2 else 1
    results = attended_and_projected(own, shards, table, out_weight, outputs)
    partials, plan, pick = results[:outputs], results[outputs], results[outputs + 1]
    some, whole, small = plan_places(blocks)[-4:-1]
    parts = (pick, plan[some:whole], plan[whole:small], plan[small] > 0)
    if outputs == 2:
        terms = [partials[1], swapped(partials[0], "head", 1)]
    else:
        terms = [lax.psum_scatter(partials[0], "head", scatter_dimension=1, tiled=True)]
    return exchanged(terms, parts, position, blocks)


def solution(mesh):
    in_specs = (P("ctx", "head"), P("ctx", None), P(), P(), P("head", None))
    return jax.shard_map(
        body, mesh=mesh, in_specs=in_specs, out_specs=P("head", "ctx"), check_vma=False
    )
```

```python
import functools

import jax
import jax.numpy as jnp
import numpy as np
from jax import lax
from jax.experimental import pallas as pl
from jax.experimental.pallas import tpu as pltpu
from jax.sharding import PartitionSpec as P

DH = 128
W1 = 512
W2 = 32
QB = 32
LANES = 128
PACK = 16
VR = DH + PACK
SAMPLE = 32
AHEAD = 3
SPAN = 4
LIMIT = 1e30
LOG2E = 1.4426950408889634


def iota(shape, dim):
    return lax.broadcasted_iota(jnp.int32, shape, dim)


def spread(columns, first, heads):
    pick = iota((columns.shape[1], LANES), 0) == first + iota((columns.shape[1], LANES), 1) // heads
    pick = pick.astype(jnp.float32).astype(jnp.bfloat16)
    return jnp.dot(columns, pick, preferred_element_type=jnp.float32)


def with_ones(values):
    return jnp.concatenate(
        [values.astype(jnp.float32).T, jnp.ones((VR - DH, LANES), jnp.float32)], axis=0
    ).astype(jnp.bfloat16)


GROUP = 4


def plan_places(blocks):
    room = blocks // 2
    sizes = (blocks, 1, blocks, GROUP - 1, blocks + (GROUP - 1) * room, GROUP * blocks, 1)
    return [sum(sizes[:k]) for k in range(len(sizes) + 1)]


def make_plan(table_ref, plan_ref, blocks):
    room = blocks // 2
    position, here = table_ref[0], table_ref[1]
    total = (table_ref.shape[0] - 2) // 2
    target = 2 + total
    place = lax.rem(position, GROUP)
    masked, head, order, sent, some, whole, _, _ = plan_places(blocks)
    one, zero = jnp.int32(1), jnp.int32(0)
    for k in range(blocks):
        block = position * blocks + k
        outside = table_ref[2 + block] - (block * QB - W1)
        plan_ref[masked + k] = jnp.clip(outside, 0, W1)
    plan_ref[head] = here
    for r in range(GROUP):
        source = lax.bitwise_xor(place, jnp.int32(r))
        slots = [table_ref[target + (position - place + source) * blocks + k] for k in range(blocks)]
        far = [lax.bitwise_xor(lax.rem(lax.div(s, blocks), GROUP), source) for s in slots]
        for k in range(blocks):
            at = zero
            for j in range(blocks):
                if j != k:
                    ahead = far[j] <= far[k] if j < k else far[j] < far[k]
                    at = at + jnp.where(ahead, one, zero)
            plan_ref[whole + r * blocks + at] = slots[k]
            if r == 0:
                plan_ref[order + k] = at
        for distance in range(1, GROUP) if r == 0 else (r,):
            nearer = zero
            for k in range(blocks):
                nearer = nearer + jnp.where(far[k] < distance, one, zero)
            nearer = jnp.minimum(nearer, blocks - room)
            if r == 0:
                plan_ref[sent + distance - 1] = nearer
            else:
                for c in range(room):
                    into = some + blocks + (r - 1) * room + c
                    plan_ref[into] = plan_ref[whole + r * blocks + nearer + c]
    for k in range(blocks):
        plan_ref[some + k] = plan_ref[whole + k]


def own_kernel(q_ref, kv_ref, q3, k1o, v1o, k2o, v2o):
    f32, bf16 = jnp.float32, jnp.bfloat16
    tokens = q_ref.shape[0]
    heads = q_ref.shape[1] // DH
    group = LANES // heads
    k1o[...] = kv_ref[:, :DH]
    second = kv_ref[:, 2 * DH : 3 * DH].astype(f32)
    second = jnp.broadcast_to(second[:, None, :], (tokens, heads, DH))
    k2o[...] = second.reshape(k2o.shape).astype(bf16)
    for k in range(tokens // LANES):
        v1o[k] = with_ones(kv_ref[k * LANES : (k + 1) * LANES, DH : 2 * DH])
        columns = with_ones(kv_ref[k * LANES : (k + 1) * LANES, 3 * DH :])
        for c in range(heads):
            v2o[k * heads + c] = spread(columns, c * group, heads)
    for h in range(heads):
        q3[pl.ds(h, tokens, stride=heads), :] = q_ref[:, h * DH : (h + 1) * DH].astype(f32)


def attention_kernel(pairs, outputs, table_ref, q3, k1o, v1o, k2o, v2o, w_ref, *refs):
    shards, refs = refs[:pairs], refs[pairs:]
    out_refs, plan_ref, pick_ref, refs = refs[:outputs], refs[outputs], refs[outputs + 1], refs[outputs + 2 :]
    kv_ref, wbuf, wsem, k1n, k1s, v1t, v1n, k2x, v2x, rowid, laneid, part, top2, bad, rows = refs
    tokens = k1o.shape[0]
    heads = q3.shape[0] // tokens
    cols = W2 * heads
    group = LANES // heads
    tiles = tokens // LANES
    blocks = tokens // QB
    near_tiles = cols // LANES
    size = max(heads, PACK)
    pack = size // heads
    wide = min(2 * LANES, cols)
    span = min(SPAN, QB // group)
    scale = LOG2E / np.sqrt(DH)
    f32, bf16 = jnp.float32, jnp.bfloat16

    room = blocks // 2
    total = (table_ref.shape[0] - 2) // 2
    senders = total // blocks

    def most_alike(device):
        to = [lax.rem(lax.div(table_ref[2 + total + device * blocks + k], blocks), GROUP) for k in range(blocks)]
        most = jnp.int32(1)
        for k in range(blocks - room):
            alike = jnp.int32(1)
            for j in range(k + 1, blocks):
                alike = alike + jnp.where(to[j] == to[k], 1, 0).astype(jnp.int32)
            most = jnp.maximum(most, alike)
        return most

    def either(cond, a, b):
        if isinstance(cond, bool):
            return a if cond else b
        return jnp.where(cond, a, b)

    weight_copy = pltpu.make_async_copy(w_ref, wbuf, wsem)
    weight_copy.start()
    masked, head, order, sent, _, _, small, _ = plan_places(blocks)
    here = table_ref[1]
    make_plan(table_ref, plan_ref, blocks)

    def lay(order):
        at = 0
        for ref in order:
            kv_ref[at : at + ref.shape[0], :] = ref[...]
            at += ref.shape[0]

    if outputs == 2:

        @pl.when(here == 0)
        def _():
            lay(shards[::-1])

        @pl.when(here != 0)
        def _():
            lay(shards)

    else:
        lay(shards)

    def prepare():
        rowid[...] = iota(rowid.shape, 0).astype(f32).astype(bf16)
        laneid[...] = iota(laneid.shape, 1).astype(f32).astype(bf16)
        bad[...] = jnp.zeros_like(bad)
        k1n[...] = k1o[...]
        v1n[...] = v1o[...]
        second = kv_ref[W1 - W2 :, 2 * DH : 3 * DH].astype(f32)
        second = jnp.broadcast_to(second[:, None, :], (W2, heads, DH))
        k2x[: W2 // pack] = second.reshape(W2 // pack, size, DH).astype(bf16)
        k2x[W2 // pack :] = k2o[...]
        columns = with_ones(kv_ref[W1 - LANES :, 3 * DH :])
        for k in range(near_tiles):
            v2x[k] = spread(columns, LANES - W2 + k * group, heads)
        v2x[near_tiles:] = v2o[...]

    def reset(t, inv):
        kt = k1o[pl.ds(pl.multiple_of(t, PACK), PACK), :].astype(f32)[:1]
        window = kv_ref[:, : 2 * DH].astype(f32)
        ok = iota((W1, DH), 0) >= inv
        k1s[...] = jnp.where(ok, window[:, :DH], kt).astype(bf16)
        values = jnp.where(ok, window[:, DH:], 0.0)
        for k in range(W1 // LANES):
            v1t[k, :DH] = values[k * LANES : (k + 1) * LANES].T.astype(bf16)
            live = k * LANES + iota((VR - DH, LANES), 1) >= inv
            v1t[k, DH:] = live.astype(f32).astype(bf16)
        k1n[...] = jnp.where(iota((tokens, DH), 0) < t, kt, k1n[...].astype(f32)).astype(bf16)
        for k in range(tiles):
            gone = k * LANES + iota((VR, LANES), 1) < t
            v1n[k] = jnp.where(gone, 0.0, v1n[k].astype(f32)).astype(bf16)

        @pl.when(inv == W1)
        def _():
            fill = jnp.broadcast_to(k2x[(t + W2) // pack].astype(f32)[:1], (size, DH)).astype(bf16)
            for s in range(W2 // pack):
                k2x[t // pack + s] = fill
            for k in range(near_tiles):
                v2x[t // group + k] = jnp.zeros((VR, LANES), f32)

    def scores(g, u):
        t = g * group + u
        mark = t.astype(f32).astype(bf16)
        keys = [
            jnp.where(rowid[...] + (k * LANES) <= mark, k1n[k * LANES : (k + 1) * LANES], k1s[k * LANES : (k + 1) * LANES])
            for k in range(tiles)
        ]
        keys = jnp.concatenate(keys + [k1s[tokens:]], axis=0)
        query = q3[pl.ds(t * heads, heads), :]
        if heads < PACK:
            query = jnp.concatenate([query] * pack, axis=0)
        query = query.astype(bf16)
        base = g * (group // pack)
        for n in range(0, cols, wide):
            paired = []
            for s in range(n // size, (n + wide) // size):
                if s * pack >= group:
                    near_keys = k2x[base + s]
                elif pack == 1:
                    near_keys = k2x[base + either(s <= u, s + W2, s)]
                else:
                    token = s * pack + iota((size, DH), 0) // heads
                    after = k2x[base + s + W2 // pack].astype(f32)
                    near_keys = jnp.where(token <= u, after, k2x[base + s].astype(f32)).astype(bf16)
                paired.append(near_keys * query)
            yield lax.dot_general(
                keys,
                jnp.concatenate(paired, axis=0),
                (((1,), (1,)), ((), ())),
                preferred_element_type=f32,
            )

    def highest(logits, best=None):
        top = jnp.max(logits, axis=0, keepdims=True)
        for k in range(0, wide, LANES):
            some = top[:, k : k + LANES]
            best = some if best is None else jnp.maximum(best, some)
        return best

    def mix(g, u, n, logits, top):
        mark = (g * group + u).astype(f32).astype(bf16)
        values = [
            jnp.where(laneid[...] + (k * LANES) <= mark, v1n[k], v1t[k]) for k in range(tiles)
        ] + [v1t[k] for k in range(tiles, W1 // LANES)]
        tops = jnp.concatenate([top] * (wide // LANES), axis=1)
        product = None
        for k in range(0, W1, 2 * LANES):
            weights = jnp.exp2(logits[k : k + 2 * LANES] * scale - tops).astype(bf16)
            two = jnp.concatenate(values[k // LANES : k // LANES + 2], axis=1)
            some = jnp.dot(two, weights, preferred_element_type=f32)
            product = some if product is None else product + some
        total = None
        for c in range(0, wide, LANES):
            k = (n + c) // LANES
            near = v2x[g + k]
            if k == 0:
                near = jnp.where(iota((VR, LANES), 1) // heads <= u, v2x[g + near_tiles], near)
            some = product[:, c : c + LANES] * near
            total = some if total is None else total + some
        return total

    def keep(g, u, total, top):
        part[g * group + u] = total
        top2[g * group + u] = jnp.broadcast_to(top, (8, LANES))
        bad[...] = jnp.where(total[DH : DH + 8] < LIMIT, bad[...], 1.0)

    def finish(g):
        lane = iota((VR, LANES), 1)
        sums = []
        for u in range(group):
            top = top2[g * group + u]
            best = top
            shift = LANES // 2
            while shift >= heads:
                best = jnp.maximum(best, pltpu.roll(best, shift, 1))
                shift //= 2
            sums.append(part[g * group + u] * jnp.exp2(top - best)[:1])
        shift = heads
        while shift < LANES:
            low = lane % (2 * shift) < shift
            sums = [
                jnp.where(low, a, b) + pltpu.roll(jnp.where(low, b, a), shift, 1)
                for a, b in zip(sums[::2], sums[1::2])
            ]
            shift *= 2
        value = sums[0][:DH] * (1.0 / sums[0][DH : DH + 1])
        spot = (plan_ref[order + g * group // QB] * QB + g * group % QB) * heads
        rows[pl.ds(pl.multiple_of(spot, LANES), LANES), :] = value.T

    def run(exact):
        prepare()

        def block(b, _):
            inv = plan_ref[masked + b]
            g0 = b * (QB // group)

            @pl.when((b == 0) | (inv == W1))
            def _():
                reset(b * QB, inv)

            def fast(s, _):
                if span == QB // group:
                    each = -(-senders // blocks)
                    for k in range(each):
                        device = jnp.minimum(b * each + k, senders - 1)
                        plan_ref[small] = jnp.where(most_alike(device) > room, 0, plan_ref[small])
                work = []
                for u in range(span * group):
                    work += [(u, n) for n in range(0, cols, wide)]
                at = [divmod(u, group) for u in range(span * group)]
                first = g0 + s * span
                source = [scores(first + k, u) for k, u in at]
                top = total = None
                ahead = [next(source[u]) for u, n in work[:AHEAD]]
                for i, (u, n) in enumerate(work):
                    if i + AHEAD < len(work):
                        ahead.append(next(source[work[i + AHEAD][0]]))
                    logits = ahead.pop(0)
                    g, v = first + at[u][0], at[u][1]
                    if n == 0:
                        top = highest(logits[:SAMPLE]) * scale
                        total = None
                    some = mix(g, v, n, logits, top)
                    total = some if total is None else total + some
                    if n + wide == cols:
                        keep(g, v, total, top)
                        if v == group // 2:
                            finish(jnp.maximum(g - 1, 0))
                return 0

            def slow(s, _):
                g, u = g0 + s // group, s % group
                best = None
                for logits in scores(g, u):
                    best = highest(logits, best)
                total = None
                for n, logits in zip(range(0, cols, wide), scores(g, u)):
                    some = mix(g, u, n, logits, best * scale)
                    total = some if total is None else total + some
                keep(g, u, total, best * scale)
                return 0

            if exact:
                return lax.fori_loop(0, QB, slow, 0)
            return lax.fori_loop(0, QB // group // span, fast, 0)

        lax.fori_loop(0, tokens // QB, block, 0)
        if exact:
            lax.fori_loop(0, tokens // group - 1, lambda g, _: finish(g) or 0, 0)
        finish(jnp.int32(tokens // group - 1))

    plan_ref[small] = jnp.int32(span == QB // group)
    for r in range(GROUP - 1):
        line = iota((room * QB, tokens), 0) + plan_ref[sent + r] * QB
        chosen = (line == iota((room * QB, tokens), 1)).astype(f32).astype(bf16)
        pick_ref[r * room * QB : (r + 1) * room * QB, :] = chosen
    run(False)

    @pl.when(jnp.max(bad[...]) > 0)
    def _():
        run(True)

    attended = jnp.concatenate(
        [rows[pl.ds(h, tokens, stride=heads), :].astype(bf16) for h in range(heads)], axis=1
    )
    weight_copy.wait()
    width = out_refs[0].shape[1]
    step = 4 * LANES
    for k, out_ref in enumerate(out_refs):
        begin = 0 if outputs == 1 else jnp.where(here == k, width, 0)
        for n in range(0, width, step):
            some = wbuf[:, pl.ds(pl.multiple_of(begin + n, step), step)]
            out_ref[:, n : n + step] = jnp.dot(attended, some, preferred_element_type=f32)


VMEM = pl.BlockSpec(memory_space=pltpu.VMEM)
HBM = pl.BlockSpec(memory_space=pltpu.HBM)
SMEM = pl.BlockSpec(memory_space=pltpu.SMEM)


def own_layouts(queries, kv_rows):
    tokens, width = queries.shape
    heads = width // DH
    size = max(heads, PACK)
    f32, bf16 = jnp.float32, jnp.bfloat16
    return pl.pallas_call(
        own_kernel,
        out_shape=[
            jax.ShapeDtypeStruct((tokens * heads, DH), f32),
            jax.ShapeDtypeStruct((tokens, DH), bf16),
            jax.ShapeDtypeStruct((tokens // LANES, VR, LANES), bf16),
            jax.ShapeDtypeStruct((tokens * heads // size, size, DH), bf16),
            jax.ShapeDtypeStruct((tokens * heads // LANES, VR, LANES), f32),
        ],
        in_specs=[VMEM] * 2,
        out_specs=[VMEM] * 5,
        compiler_params=pltpu.CompilerParams(vmem_limit_bytes=16 * 2**20),
        cost_estimate=pl.CostEstimate(flops=10**9, bytes_accessed=4 * 2**20, transcendentals=0),
    )(queries, kv_rows)


def attended_and_projected(own, shards, table, weight, outputs):
    heads = own[0].shape[0] // own[1].shape[0]
    tokens = own[1].shape[0]
    sends = (GROUP - 1) * (tokens // QB // 2) * QB
    size = max(heads, PACK)
    f32, bf16 = jnp.float32, jnp.bfloat16
    return pl.pallas_call(
        functools.partial(attention_kernel, len(shards), outputs),
        out_shape=[jax.ShapeDtypeStruct((tokens, weight.shape[1] // outputs), f32)] * outputs
        + [
            jax.ShapeDtypeStruct((plan_places(tokens // QB)[-1],), jnp.int32),
            jax.ShapeDtypeStruct((sends, tokens), bf16),
        ],
        in_specs=[SMEM] + [VMEM] * 5 + [HBM] + [VMEM] * len(shards),
        out_specs=[VMEM] * outputs + [SMEM, VMEM],
        scratch_shapes=[
            pltpu.VMEM((W1, 4 * DH), bf16),
            pltpu.VMEM(weight.shape, bf16),
            pltpu.SemaphoreType.DMA,
            pltpu.VMEM((tokens, DH), bf16),
            pltpu.VMEM((W1, DH), bf16),
            pltpu.VMEM((W1 // LANES, VR, LANES), bf16),
            pltpu.VMEM((tokens // LANES, VR, LANES), bf16),
            pltpu.VMEM(((tokens + W2) * heads // size, size, DH), bf16),
            pltpu.VMEM(((tokens + W2) * heads // LANES, VR, LANES), f32),
            pltpu.VMEM((LANES, DH), bf16),
            pltpu.VMEM((VR, LANES), bf16),
            pltpu.VMEM((tokens, VR, LANES), f32),
            pltpu.VMEM((tokens, 8, LANES), f32),
            pltpu.VMEM((8, LANES), f32),
            pltpu.VMEM((tokens * heads, DH), f32),
        ],
        compiler_params=pltpu.CompilerParams(vmem_limit_bytes=43 * 2**20),
    )(table, *own, weight, *shards)

def shifted(block, axis, distance):
    devices = range(lax.axis_size(axis))
    return lax.ppermute(block, axis, [(i - distance, i) for i in devices if i - distance in devices])


def swapped(block, axis, bits):
    return lax.ppermute(block, axis, [(i, i ^ bits) for i in range(lax.axis_size(axis))])


def collect_window(kv_rows, back, own):
    if lax.axis_size("head") != 2 or back != 4:
        return [shifted(kv_rows, "ctx", back - k) for k in range(back)], own

    def taken(distances):
        devices = range(lax.axis_size("ctx"))
        route = [
            ((i - d) % len(devices) * 2 + h, i * 2 + h) for i in devices for h, d in enumerate(distances)
        ]
        return lax.ppermute(kv_rows, ("ctx", "head"), route)

    parts, own = lax.optimization_barrier(([taken((2, 4)), taken((1, 3))], own))
    held = jnp.concatenate(parts, axis=0)
    return [held, swapped(held, "head", 1)], own


def exchanged(terms, plan, position, blocks):
    room = blocks // 2
    pick, some_slots, whole_slots, few = plan

    def added(terms):
        return sum(terms[1:], terms[0]).astype(jnp.bfloat16)

    def placed(pieces, slots):
        tokens = blocks * QB
        rows = (slots[:, None] * QB + np.arange(QB, dtype=np.int32)[None, :]).reshape(-1)
        stored = position * tokens + jnp.arange(tokens, dtype=jnp.int32)
        pick = (rows[:, None] == stored[None, :]).astype(jnp.bfloat16)
        return lax.dot_general(
            jnp.concatenate(pieces, axis=0),
            pick,
            (((0,), (0,)), ((), ())),
            preferred_element_type=jnp.float32,
        ).astype(jnp.bfloat16)

    def some(*terms):
        own = added(terms)
        rows = jnp.dot(pick, own, preferred_element_type=jnp.float32).astype(jnp.bfloat16)
        rows = rows.reshape(GROUP - 1, room * QB, -1)
        pieces = [own] + [swapped(rows[r - 1], "ctx", r) for r in range(1, GROUP)]
        return placed(pieces, some_slots)

    def whole(*terms):
        own = added(terms)
        pieces = [own] + [swapped(own, "ctx", r) for r in range(1, GROUP)]
        return placed(pieces, whole_slots)

    return lax.cond(few, some, whole, *terms)


def body(queries, kv_rows, doc_start, destination, out_weight):
    position = lax.axis_index("ctx").astype(jnp.int32)
    tokens = queries.shape[0]
    blocks = tokens // QB
    here = lax.axis_index("head").astype(jnp.int32)
    table = jnp.concatenate([jnp.stack([position, here]), doc_start, destination])
    own = own_layouts(queries, kv_rows)
    shards, own = collect_window(kv_rows, W1 // tokens, own)
    outputs = 2 if len(shards) == 2 else 1
    results = attended_and_projected(own, shards, table, out_weight, outputs)
    partials, plan, pick = results[:outputs], results[outputs], results[outputs + 1]
    some, whole, small = plan_places(blocks)[-4:-1]
    parts = (pick, plan[some:whole], plan[whole:small], plan[small] > 0)
    if outputs == 2:
        terms = [partials[1], swapped(partials[0], "head", 1)]
    else:
        terms = [lax.psum_scatter(partials[0], "head", scatter_dimension=1, tiled=True)]
    return exchanged(terms, parts, position, blocks)


def solution(mesh):
    in_specs = (P("ctx", "head"), P("ctx", None), P(), P(), P("head", None))
    return jax.shard_map(
        body, mesh=mesh, in_specs=in_specs, out_specs=P("head", "ctx"), check_vma=False
    )
```
